256 devices in a mesh: dp: 32 (over y, x, core), tensor: 8 (over z).
Axes of the slice: x: 4, y: 4, z: 8, core: 2. Of those that a mesh axis runs over, the one named last changes fastest.
Arguments:
- x_in: bfloat16 [32768, 8192], P(('dp', 'tensor')), may hold values from -6 to 6
- z_in: bfloat16 [32768, 8192], P(('dp', 'tensor')), may hold values from -6 to 6
- bc_in: bfloat16 [32768, 2048], P(('dp', 'tensor')), may hold values from -6 to 6
- dt_in: bfloat16 [32768, 128], P(('dp', 'tensor')), may hold values from -4 to 4
- conv_x_param: float32 [5, 8192], P(None, 'tensor'), may hold values from -3 to 3
- conv_bc_param: float32 [5, 2048], P(None, 'tensor'), may hold values from -3 to 3
- decay_rate: float32 [128], P('tensor'), may hold values from 0.01 to 2
- dt_bias: float32 [128], P('tensor'), may hold values from -3 to 0
- skip_gain: float32 [128], P('tensor'), may hold values from -3 to 3
- norm_gain: float32 [8192], P('tensor'), may hold values from 0.5 to 1.5
- ssm_state: float32 [128, 128, 64, 128], P('dp', 'tensor'), may hold values from -0.6 to 0.6
- conv_x_state: float32 [128, 3, 8192], P('dp', None, 'tensor'), may hold values from -6 to 6
- conv_bc_state: float32 [128, 3, 2048], P('dp', None, 'tensor'), may hold values from -6 to 6
- lengths: int32 [128], replicated, may hold values from 3 to 640, as said below
- prefill_owner: int32 [128], replicated, may hold values from 0 to 31, as said below
- row_start: int32 [128], replicated, may hold values from 0 to 1021, as said below
Outputs:
- y_out: bfloat16 [32768, 8192], P('dp', 'tensor')
- new_ssm_state: float32 [128, 128, 64, 128], P('dp', 'tensor')
- new_conv_x_state: float32 [128, 3, 8192], P('dp', None, 'tensor')
- new_conv_bc_state: float32 [128, 3, 2048], P('dp', None, 'tensor')
The draws below stay inside these ranges and needn't reach their ends.
Inputs may be any that keep to these rules, and one draw needn't show every extreme that they name: `prefill_owner`: conversation c is held by index c // 4 along dp. Of the 4 conversations of one index, two are prefilled there, one on the next index and one on the previous index, cyclically; so every index prefills 4 conversations. The lengths of the conversations of one prefill owner add up to 1024. `row_start`: the conversations of one prefill owner cover its 1024 rows in consecutive runs, each row in exactly one.
All inputs are finite; a program needn't handle non-finite values.
Results may differ from the reference program's by a relative error of at most 0.005.
Values may be sent and summed in bfloat16 or wider, within the bound.
No kernel may reach another device: no remote copies, remote signals or barrier semaphores. Data moves between devices by JAX's collectives and lax.ppermute only.
A program may use at most 128 MiB of HBM per device.

```python
import math
import jax
import jax.numpy as jnp
from jax import lax

HEADS = 128
HEADDIM = 64
STATE = 128
GROUPS = 8
SLOTS = 4
ROWS = 1024
MAXLEN = 640
HD = 8192
BCW = 2048
CONVS = 128
TOKENS = 32768
N_DP = 32


def plan_tables(key):
    rank_scores = jax.random.randint(jax.random.fold_in(key, 11), (N_DP, SLOTS), 0, 1 << 20) * SLOTS + jnp.arange(SLOTS, dtype=jnp.int32)[None, :]
    order_idx = jnp.argsort(rank_scores, axis=1)
    role_table = jnp.array([0, 0, 1, 2], dtype=jnp.int32)
    roles = role_table[order_idx]
    weights = jax.random.randint(jax.random.fold_in(key, 12), (N_DP, SLOTS), 16, 64)
    shares = weights * (ROWS - SLOTS) // jnp.sum(weights, axis=1, keepdims=True) + 1
    leading = ROWS - jnp.sum(shares[:, 1:], axis=1)
    shares = jnp.concatenate([leading[:, None], shares[:, 1:]], axis=1)
    longest_owner = jax.random.randint(jax.random.fold_in(key, 13), (), 0, N_DP)
    rest_piece = (ROWS - MAXLEN - 3) // 2
    special = jnp.array([MAXLEN, rest_piece, ROWS - MAXLEN - 3 - rest_piece, 3], dtype=jnp.int32)
    owner_rows = jnp.arange(N_DP, dtype=jnp.int32)[:, None]
    shares = jnp.where(owner_rows == longest_owner, special[None, :], shares)
    firsts = jnp.cumsum(shares, axis=1) - shares
    stay_rank = jnp.cumsum((roles == 0).astype(jnp.int32), axis=1) - 1
    owner_idx = jnp.where(roles == 0, owner_rows, jnp.where(roles == 1, (owner_rows + 1) % N_DP, (owner_rows + N_DP - 1) % N_DP))
    slot_idx = jnp.where(roles == 0, stay_rank, jnp.where(roles == 1, 2, 3))
    return (shares[owner_idx, slot_idx].reshape(-1), owner_idx.reshape(-1), firsts[owner_idx, slot_idx].reshape(-1))


def draw_lengths(key, part):
    tables = plan_tables(key)
    return tables[0].astype(jnp.int32)


def draw_prefill_owner(key, part):
    tables = plan_tables(key)
    return tables[1].astype(jnp.int32)


def draw_row_start(key, part):
    tables = plan_tables(key)
    return tables[2].astype(jnp.int32)


def steps_of(rng, shape, split, smallest, high):
    level = 1.0
    for dim, blocks in split:
        heights = jax.random.uniform(jax.random.fold_in(jax.random.fold_in(rng, 6), dim), (blocks,), jnp.float32, smallest / len(split), high / len(split))
        level = level * jnp.repeat(jnp.exp(heights), shape[dim] // blocks).reshape((-1,) + (1,) * (len(shape) - 1 - dim))
    return level


def bell_draw(rng, extent, deviation, bound, split=(), kind=jnp.bfloat16):
    factor_of = steps_of(rng, extent, split, -0.22, 0.18) if split else 1.0
    drawn = jax.random.normal(rng, extent, jnp.float32) * deviation * factor_of
    return jnp.minimum(jnp.maximum(drawn, -bound), bound).astype(kind)


def setup_inputs(seed: int = 0) -> dict:
    key_of = jax.random.split(jax.random.key(seed), 17)
    return {
        "x_in": bell_draw(key_of[0], (TOKENS, HD), 1.0, 6.0, ((0, 256),)),
        "z_in": bell_draw(key_of[1], (TOKENS, HD), 1.0, 6.0, ((0, 256),)),
        "bc_in": bell_draw(key_of[2], (TOKENS, BCW), 1.0, 6.0, ((0, 256),)),
        "dt_in": bell_draw(key_of[3], (TOKENS, HEADS), 1.0, 4.0, ((0, 256),)),
        "conv_x_param": bell_draw(key_of[4], (5, HD), 0.5, 3.0, ((1, 8),), jnp.float32),
        "conv_bc_param": bell_draw(key_of[5], (5, BCW), 0.5, 3.0, ((1, 8),), jnp.float32),
        "decay_rate": jnp.clip(jnp.exp(math.log(2.0) - 5.2983174 * jax.random.uniform(key_of[6], (HEADS,), jnp.float32) ** steps_of(key_of[6], (HEADS,), ((0, 8),), -0.2, 0.2)), 0.01, 2.0),
        "dt_bias": jnp.clip(-3.0 + 3.0 * jax.random.uniform(key_of[7], (HEADS,), jnp.float32) ** steps_of(key_of[7], (HEADS,), ((0, 8),), -0.2, 0.2), -3.0, 0.0),
        "skip_gain": bell_draw(key_of[8], (HEADS,), 1.0, 3.0, ((0, 8),), jnp.float32),
        "norm_gain": jnp.clip(1.0 + 0.1 * jax.random.normal(key_of[9], (HD,), jnp.float32), 0.5, 1.5),
        "ssm_state": bell_draw(key_of[10], (CONVS, HEADS, HEADDIM, STATE), 0.1, 0.6, ((0, 32), (1, 8)), jnp.float32),
        "conv_x_state": bell_draw(key_of[11], (CONVS, 3, HD), 1.0, 6.0, ((0, 32), (2, 8)), jnp.float32),
        "conv_bc_state": bell_draw(key_of[12], (CONVS, 3, BCW), 1.0, 6.0, ((0, 32), (2, 8)), jnp.float32),
        "lengths": draw_lengths(jax.random.fold_in(key_of[16], 71), 0),
        "prefill_owner": draw_prefill_owner(jax.random.fold_in(key_of[16], 71), 0),
        "row_start": draw_row_start(jax.random.fold_in(key_of[16], 71), 0),
    }


EPSILON = 1e-05
best_precision = lax.Precision.HIGHEST

def plan_rows(owner_idx, lengths, prefill_owner, row_start, row_count):
    conv_ids = jnp.nonzero(prefill_owner == owner_idx, size=SLOTS)[0].astype(jnp.int32)
    order_idx = jnp.argsort(row_start[conv_ids]).astype(jnp.int32)
    conv_ids = conv_ids[order_idx]
    starts = row_start[conv_ids]
    seg_lengths = lengths[conv_ids]
    row_idx = jnp.arange(row_count, dtype=jnp.int32)
    inside = (row_idx[:, None] >= starts[None, :]) & (row_idx[:, None] < (starts + seg_lengths)[None, :])
    segment = lax.optimization_barrier(jnp.sum(jnp.where(inside, jnp.arange(SLOTS, dtype=jnp.int32)[None, :], 0), axis=1))
    position = row_idx - lax.optimization_barrier(jnp.sum(jnp.where(inside, starts[None, :], 0), axis=1))
    same_tri = (segment[:, None] == segment[None, :]) & (row_idx[None, :] <= row_idx[:, None])
    return (conv_ids, starts, seg_lengths, inside, position, same_tri)

def causal_conv(values, param, state, inside, position):
    row_count, channels = values.shape
    result = param[4][None, :] + param[3][None, :] * values
    for lag_rows in (1, 2, 3):
        shifted = jnp.concatenate([jnp.zeros((lag_rows, channels), jnp.float32), values[:-lag_rows]], axis=0)
        picker = inside[:, :, None] & ((3 - lag_rows + position)[:, None, None] == jnp.arange(3, dtype=jnp.int32)[None, None, :])
        from_state = jnp.dot(picker.astype(jnp.float32).reshape(row_count, SLOTS * 3), state.reshape(SLOTS * 3, channels), precision=best_precision, preferred_element_type=jnp.float32)
        previous = jnp.where((position >= lag_rows)[:, None], shifted, from_state)
        result = result + param[3 - lag_rows][None, :] * previous
    return result

def last_inputs(values, starts, seg_lengths):
    row_idx = jnp.arange(values.shape[0], dtype=jnp.int32)
    target = (starts + seg_lengths)[:, None] - 3 + jnp.arange(3, dtype=jnp.int32)[None, :]
    picker = (target[:, :, None] == row_idx[None, None, :]).astype(jnp.float32).reshape(SLOTS * 3, values.shape[0])
    taken = jnp.dot(picker, values, precision=best_precision, preferred_element_type=jnp.float32)
    return taken.reshape(SLOTS, 3, values.shape[1])

def head_scan(x_head, dt_head, decay_speed, skip_value, mix_matrix, c_half, b_half, initial_head, inside, starts, seg_lengths, same_tri):
    log_decay = -dt_head * decay_speed
    running = jnp.cumsum(log_decay)
    before = running[starts] - log_decay[starts]
    cumulated = running - lax.optimization_barrier(jnp.sum(jnp.where(inside, before[None, :], 0.0), axis=1))
    end_decay = running[starts + seg_lengths - 1] - before
    spread = jnp.where(same_tri, cumulated[:, None] - cumulated[None, :], 0.0)
    decay_matrix = jnp.where(same_tri, jnp.exp(spread), 0.0)
    scores = (mix_matrix * decay_matrix * dt_head[None, :]).astype(jnp.bfloat16)
    output = jnp.dot(scores, x_head, preferred_element_type=jnp.float32)
    state_rows = jnp.transpose(initial_head, (2, 0, 1)).reshape(initial_head.shape[2], SLOTS * HEADDIM)
    state_hi = state_rows.astype(jnp.bfloat16)
    state_lo = (state_rows - lax.optimization_barrier(state_hi).astype(jnp.float32)).astype(jnp.bfloat16)
    initial_term = jnp.dot(c_half, state_hi, preferred_element_type=jnp.float32) + jnp.dot(c_half, state_lo, preferred_element_type=jnp.float32)
    initial_term = lax.optimization_barrier(jnp.sum(jnp.where(inside[:, :, None], initial_term.reshape(-1, SLOTS, HEADDIM), 0.0), axis=1))
    x_wide = x_head.astype(jnp.float32)
    output = output + jnp.exp(cumulated)[:, None] * initial_term + skip_value * x_wide
    row_end = lax.optimization_barrier(jnp.sum(jnp.where(inside, end_decay[None, :], 0.0), axis=1))
    carried = (x_wide * (jnp.exp(row_end - cumulated) * dt_head)[:, None]).astype(jnp.bfloat16)
    b_slots = jnp.where(inside[:, :, None], b_half[:, None, :], jnp.zeros((), jnp.bfloat16)).reshape(b_half.shape[0], -1)
    final_state = jnp.dot(carried.T, b_slots, preferred_element_type=jnp.float32).reshape(HEADDIM, SLOTS, -1)
    final_state = jnp.transpose(final_state, (1, 0, 2)) + jnp.exp(end_decay)[:, None, None] * initial_head
    return (output, final_state)

def group_block(x_group, z_group, bc_group, dt_group, rate_group, skip_group, gain_group, initial_group, inside, starts, seg_lengths, same_tri):
    b_half = bc_group[:, :STATE]
    c_half = bc_group[:, STATE:]
    mix_matrix = jnp.dot(c_half, b_half.T, preferred_element_type=jnp.float32)

    def one_head(head_idx):
        x_head = lax.dynamic_slice_in_dim(x_group, head_idx * HEADDIM, HEADDIM, 1)
        dt_head = lax.dynamic_index_in_dim(dt_group, head_idx, 1, keepdims=False)
        decay_speed = lax.dynamic_index_in_dim(rate_group, head_idx, 0, keepdims=False)
        skip_value = lax.dynamic_index_in_dim(skip_group, head_idx, 0, keepdims=False)
        initial_head = lax.dynamic_index_in_dim(initial_group, head_idx, 1, keepdims=False)
        return head_scan(x_head, dt_head, decay_speed, skip_value, mix_matrix, c_half, b_half, initial_head, inside, starts, seg_lengths, same_tri)
    head_outputs, head_states = lax.map(one_head, jnp.arange(HEADS // GROUPS, dtype=jnp.int32))
    joined = jnp.transpose(head_outputs, (1, 0, 2)).reshape(head_outputs.shape[1], -1)
    gated = joined * jax.nn.silu(z_group.astype(jnp.float32))
    mean_square = lax.optimization_barrier(jnp.mean(gated * gated, axis=1, keepdims=True))
    normed = (gated * lax.rsqrt(mean_square + EPSILON) * gain_group[None, :]).astype(jnp.bfloat16)
    return (normed, jnp.transpose(head_states, (1, 0, 2, 3)))

def mixer(x_rows, z_rows, bc_rows, dt_rows, conv_x_param, conv_bc_param, decay_rate, dt_bias, skip_gain, norm_gain, initial_ssm, initial_cx, initial_cbc, inside, position, starts, seg_lengths, same_tri):
    x_values = x_rows.astype(jnp.float32)
    bc_values = bc_rows.astype(jnp.float32)
    x_conv = jax.nn.silu(causal_conv(x_values, conv_x_param, initial_cx, inside, position)).astype(jnp.bfloat16)
    bc_conv = jax.nn.silu(causal_conv(bc_values, conv_bc_param, initial_cbc, inside, position)).astype(jnp.bfloat16)
    dt_all = jax.nn.softplus(dt_rows.astype(jnp.float32) + dt_bias[None, :])
    per_group = HEADS // GROUPS
    group_count = dt_rows.shape[1] // per_group
    outputs = []
    finals = []
    for group_idx in range(group_count):
        col_lo = group_idx * per_group * HEADDIM
        col_hi = col_lo + per_group * HEADDIM
        head_lo = group_idx * per_group
        head_hi = head_lo + per_group
        bc_lo = group_idx * 2 * STATE
        normed, final_group = group_block(x_conv[:, col_lo:col_hi], z_rows[:, col_lo:col_hi], bc_conv[:, bc_lo:bc_lo + 2 * STATE], dt_all[:, head_lo:head_hi], decay_rate[head_lo:head_hi], skip_gain[head_lo:head_hi], norm_gain[col_lo:col_hi], initial_ssm[:, head_lo:head_hi], inside, starts, seg_lengths, same_tri)
        outputs.append(normed)
        finals.append(final_group)
    y_block = jnp.concatenate(outputs, axis=1)
    final_ssm = jnp.concatenate(finals, axis=1)
    return (y_block, final_ssm, last_inputs(x_values, starts, seg_lengths), last_inputs(bc_values, starts, seg_lengths))

def reference(x_in, z_in, bc_in, dt_in, conv_x_param, conv_bc_param, decay_rate, dt_bias, skip_gain, norm_gain, ssm_state, conv_x_state, conv_bc_state, lengths, prefill_owner, row_start):

    def one_owner(owner_idx):
        conv_ids, starts, seg_lengths, inside, position, same_tri = plan_rows(owner_idx, lengths, prefill_owner, row_start, ROWS)
        first_row = (owner_idx * ROWS).astype(jnp.int32)

        def take_rows(source):
            return lax.dynamic_slice_in_dim(source, first_row, ROWS, 0)
        y_block, final_ssm, final_cx, final_cbc = mixer(take_rows(x_in), take_rows(z_in), take_rows(bc_in), take_rows(dt_in), conv_x_param, conv_bc_param, decay_rate, dt_bias, skip_gain, norm_gain, ssm_state[conv_ids], conv_x_state[conv_ids], conv_bc_state[conv_ids], inside, position, starts, seg_lengths, same_tri)
        return (y_block, final_ssm, final_cx, final_cbc, conv_ids)
    y_all, ssm_all, cx_all, cbc_all, ids_all = lax.map(one_owner, jnp.arange(N_DP, dtype=jnp.int32))
    flat_ids = ids_all.reshape(-1)
    new_ssm = jnp.zeros_like(ssm_state).at[flat_ids].set(ssm_all.reshape((-1,) + ssm_state.shape[1:]))
    new_cx = jnp.zeros_like(conv_x_state).at[flat_ids].set(cx_all.reshape((-1,) + conv_x_state.shape[1:]))
    new_cbc = jnp.zeros_like(conv_bc_state).at[flat_ids].set(cbc_all.reshape((-1,) + conv_bc_state.shape[1:]))
    return (y_all.reshape(TOKENS, HD), new_ssm, new_cx, new_cbc)
```

```python
import functools
import math

import jax
import jax.numpy as jnp
from jax import lax
from jax.experimental import pallas as pl
from jax.experimental.pallas import tpu as pltpu
from jax.sharding import PartitionSpec as P

HEADS = 128
HEADDIM = 64
STATE = 128
GROUPS = 8
SLOTS = 4
ROWS = 1024
GH = HEADS // GROUPS
GC = GH * HEADDIM
Q = 256
CHUNKS = ROWS // Q
TENSOR = 8
SRC_ROWS = ROWS // TENSOR
EPSILON = 1e-05
LOG2E = math.log2(math.e)
MIB = 1 << 20

F32 = jnp.float32
BF16 = jnp.bfloat16


def mm(a, b):
    return jnp.dot(a, b, preferred_element_type=F32)


def iota(shape, dim):
    return lax.broadcasted_iota(jnp.int32, shape, dim)


def silu(v):
    half = v * 0.5
    return half + half * jnp.tanh(half)


def split2(v):
    hi = v.astype(BF16)
    return hi, (v - hi.astype(F32)).astype(BF16)


def split3(v):
    hi = v.astype(BF16)
    rest = v - hi.astype(F32)
    mid = rest.astype(BF16)
    return hi, mid, (rest - mid.astype(F32)).astype(BF16)


def segment_of(row_ids, seg):
    total = jnp.zeros(row_ids.shape, jnp.int32)
    for k in range(1, SLOTS):
        total = total + (row_ids >= seg[k]).astype(jnp.int32)
    return total


def boundary_targets(shape, dim, seg):
    idx = iota(shape, dim) % 16
    target = jnp.full(shape, -1, jnp.int32)
    for s in range(SLOTS):
        for q in range(3):
            target = jnp.where(idx == 3 * s + q, seg[s] + q, target)
    return jnp.where(iota(shape, dim) < 48, target, -1)


def last_rows(x_ref, lanes, seg):
    idx = iota((16, 1), 0)
    target = jnp.full((16, 1), -1, jnp.int32)
    for s in range(SLOTS):
        for q in range(3):
            target = jnp.where(idx == 3 * s + q, seg[4 + s] - 3 + q, target)
    picker = (iota((16, ROWS), 1) == target).astype(F32).astype(BF16)
    return mm(picker, x_ref[0:ROWS, lanes])


def boundary_terms(last, state, param, lanes):
    diff = state - pltpu.roll(last, 3, 0)
    q = iota((16, 1), 0) % 3
    term = param[0:1, lanes] * diff
    term = term + jnp.where(q <= 1, param[1:2, lanes] * pltpu.roll(diff, 15, 0), 0.0)
    term = term + jnp.where(q == 0, param[2:3, lanes] * pltpu.roll(diff, 14, 0), 0.0)
    return split3(term)


def conv_rows(x_ref, r0, count, lanes, param, terms_ref, targets):
    prev = pl.multiple_of(jnp.maximum(r0 - 16, 0), 16)
    halo = x_ref[pl.ds(prev, 16), lanes].astype(F32) * jnp.where(r0 > 0, 1.0, 0.0)
    value = jnp.concatenate([halo, x_ref[pl.ds(r0, count), lanes].astype(F32)], axis=0)
    onehot = (iota((count, 128), 0) + r0 == targets).astype(F32).astype(BF16)
    total = mm(onehot, terms_ref[:, lanes]) + param[4:5, lanes]
    total = total + param[3:4, lanes] * value[16:]
    for lag in (1, 2, 3):
        total = total + param[3 - lag : 4 - lag, lanes] * pltpu.roll(value, lag, 0)[16:]
    return silu(total)


def store_terms(terms_ref, lanes, parts):
    for i, part in enumerate(parts):
        terms_ref[16 * i : 16 * i + 16, lanes] = part


def pack_kernel(bc, dt, out):
    dt_t = dt[...].astype(F32).T.astype(BF16)
    for t in range(TENSOR):
        out[t, 0:SRC_ROWS, :] = bc[:, 2 * STATE * t : 2 * STATE * (t + 1)]
        out[t, SRC_ROWS : SRC_ROWS + GH, 0:SRC_ROWS] = dt_t[GH * t : GH * (t + 1), :]
        out[t, SRC_ROWS : SRC_ROWS + GH, SRC_ROWS:] = jnp.zeros((GH, SRC_ROWS), BF16)


def prep_kernel(
    seg,
    bcdt,
    conv_state,
    own,
    lft,
    rgt,
    param,
    rate,
    bias,
    b_t_out,
    c_out,
    mix_out,
    col_out,
    row_out,
    dec_out,
    last_out,
    init_out,
    bc_rows,
    b_rows,
    terms,
):
    for s in range(TENSOR):
        bc_rows[SRC_ROWS * s : SRC_ROWS * (s + 1), :] = bcdt[s, 0:SRC_ROWS, :]
    every = slice(0, 2 * STATE)
    last = last_rows(bc_rows, every, seg)
    last_out[...] = last
    terms[...] = jnp.zeros_like(terms)
    store_terms(terms, every, boundary_terms(last, conv_state[...], param, every))
    targets = boundary_targets((1, 128), 1, seg)

    @pl.loop(0, ROWS // 64)
    def _(i):
        r0 = pl.multiple_of(i * 64, 64)
        value = conv_rows(bc_rows, r0, 64, every, param, terms, targets).astype(BF16)
        b_rows[pl.ds(r0, 64), :] = value[:, 0:STATE]
        c_out[pl.ds(r0, 64), :] = value[:, STATE:]

    dec_sum = jnp.zeros((GH, 128), F32)
    for c in range(CHUNKS):
        b_t = b_rows[Q * c : Q * (c + 1), :].astype(F32).T.astype(BF16)
        b_t_out[c] = b_t
        seg_col = segment_of(iota((Q, 1), 0) + Q * c, seg)
        seg_row = segment_of(iota((1, Q), 1) + Q * c, seg)
        same = seg_col == seg_row
        row_id, col_id = iota((Q, Q), 0), iota((Q, Q), 1)
        mix = mm(c_out[Q * c : Q * (c + 1), :], b_t)
        mix_out[c] = jnp.where(same & (col_id <= row_id), mix, 0.0)
        up_to = jnp.where(same & (row_id <= col_id), 1.0, 0.0).astype(BF16)
        after = jnp.where(same & (row_id > col_id), 1.0, 0.0).astype(BF16)
        raw = jnp.concatenate(
            [bcdt[s, SRC_ROWS : SRC_ROWS + GH, 0:SRC_ROWS] for s in (2 * c, 2 * c + 1)], axis=1
        ).astype(F32) + bias[...]
        step = jnp.maximum(raw, 0.0) + jnp.log1p(jnp.exp(-jnp.abs(raw)))
        log_decay = step * rate[...] * (-LOG2E)
        parts = jnp.concatenate(split3(log_decay), axis=0)

        def summed(mask):
            three = mm(parts, mask)
            return three[0:GH] + three[GH : 2 * GH] + three[2 * GH : 3 * GH]

        running = summed(up_to)
        rest = summed(after)
        row_out[c] = running - jnp.log2(step)
        stack = jnp.concatenate(
            [running, jnp.exp2(running), jnp.exp2(rest) * step, jnp.zeros((80, Q), F32)], axis=0
        )
        col_out[c] = stack.T
        pair = jnp.where(seg_col + SLOTS * c == iota((Q, 128), 1), 1.0, 0.0).astype(BF16)
        dec_sum = dec_sum + summed(pair)
    decay = jnp.concatenate([jnp.exp2(dec_sum), jnp.zeros((128 - GH, 128), F32)], axis=0).T[0:16]
    spread = jnp.where(iota((128, GC), 0) == iota((128, GC), 1) // HEADDIM, 1.0, 0.0).astype(BF16)
    dec_hi, dec_lo = split2(decay)
    dec_out[...] = mm(dec_hi, spread) + mm(dec_lo, spread)

    def load_state(k, ref_of):
        for b in range(GC // 128):
            init_out[k, :, 128 * b : 128 * (b + 1)] = ref_of(b).T

    @pl.loop(0, SLOTS)
    def _(k):
        source = seg[8 + k]

        @pl.when(source < SLOTS)
        def _():
            load_state(k, lambda b: own[jnp.minimum(source, SLOTS - 1), 128 * b : 128 * (b + 1), :])

        @pl.when(source == SLOTS)
        def _():
            load_state(k, lambda b: lft[128 * b : 128 * (b + 1), :])

        @pl.when(source == SLOTS + 1)
        def _():
            load_state(k, lambda b: rgt[128 * b : 128 * (b + 1), :])


def main_kernel(
    seg,
    x_in,
    conv_state,
    param,
    skip,
    b_t_in,
    c_in,
    mix_in,
    col_in,
    row_in,
    dec_in,
    init_in,
    y_out,
    own_out,
    lft_out,
    rgt_out,
    last_out,
    terms,
    x_conv,
    x_weighted,
    state,
    inter,
    spread_e,
    spread_w,
):
    terms[...] = jnp.zeros_like(terms)
    targets = boundary_targets((1, 128), 1, seg)
    for lt in range(GC // 256):
        lanes = slice(256 * lt, 256 * (lt + 1))
        last = last_rows(x_in, lanes, seg)
        last_out[:, lanes] = last
        store_terms(terms, lanes, boundary_terms(last, conv_state[:, lanes], param, lanes))
        row_id = iota((256, 256), 0) % 128
        head_id = (iota((256, 256), 1) + 256 * lt) // HEADDIM
        spread_e[:, lanes] = jnp.where(row_id - GH == head_id, 1.0, 0.0).astype(BF16)
        spread_w[:, lanes] = jnp.where(row_id - 2 * GH == head_id, 1.0, 0.0).astype(BF16)

    @pl.loop(0, ROWS // 64)
    def _(i):
        r0 = pl.multiple_of(i * 64, 64)
        for lt in range(GC // 256):
            lanes = slice(256 * lt, 256 * (lt + 1))
            value = conv_rows(x_in, r0, 64, lanes, param, terms, targets)
            x_conv[pl.ds(r0, 64), lanes] = value.astype(BF16)

    @pl.loop(0, SLOTS)
    def _(k):
        state[k] = init_in[k]

    @pl.loop(0, CHUNKS)
    def _(c):
        r0 = pl.multiple_of(c * Q, Q)
        rows = pl.ds(r0, Q)
        col = col_in[c]
        col_hi, col_lo = split2(col)
        col_two = jnp.concatenate([col_hi, col_lo], axis=1)
        for lt in range(GC // 256):
            lanes = slice(256 * lt, 256 * (lt + 1))
            weight = mm(col_two, spread_w[:, lanes])
            x_weighted[:, lanes] = (x_conv[rows, lanes].astype(F32) * weight).astype(BF16)
            inter[:, lanes] = jnp.zeros((Q, 256), F32)

        @pl.loop(0, SLOTS)
        def _(k):
            first, end = seg[k], seg[4 + k]

            @pl.when((first < r0 + Q) & (end > r0))
            def _():
                row_id = iota((Q, STATE), 0) + r0
                c_part = jnp.where(
                    (row_id >= first) & (row_id < end), c_in[rows, :].astype(F32), 0.0
                ).astype(BF16)
                c_two = jnp.concatenate([c_part, c_part], axis=1)
                col_id = iota((STATE, Q), 1) + r0
                b_part = jnp.where(
                    (col_id >= first) & (col_id < end), b_t_in[c].astype(F32), 0.0
                ).astype(BF16)
                decay = dec_in[pl.ds(c * SLOTS + k, 1), :]
                for lt in range(GC // 256):
                    lanes = slice(256 * lt, 256 * (lt + 1))
                    old = state[k, :, lanes]
                    both = jnp.concatenate(split2(old), axis=0)
                    inter[:, lanes] += mm(c_two, both)
                    state[k, :, lanes] = old * decay[:, lanes] + mm(b_part, x_weighted[:, lanes])

        low_half = iota((Q, 128), 1) < HEADDIM
        for lt in range(GC // 256):
            lanes = slice(256 * lt, 256 * (lt + 1))
            scale = mm(col_two, spread_e[:, lanes])
            inter[:, lanes] = inter[:, lanes] * scale + x_conv[rows, lanes].astype(F32) * skip[
                0:1, lanes
            ]
        for hp in range(GH // 2):
            lanes = slice(128 * hp, 128 * (hp + 1))
            x_pair = x_conv[rows, lanes].astype(F32)
            x_low = jnp.where(low_half, x_pair, 0.0).astype(BF16)
            x_high = jnp.where(low_half, 0.0, x_pair).astype(BF16)
            for half in range(2):
                depth = 128 * (half + 1)
                part = slice(128 * half, 128 * (half + 1))
                mix = mix_in[c, part, 0:depth]
                total = inter[part, lanes]
                for h, x_one in ((2 * hp, x_low), (2 * hp + 1, x_high)):
                    spread = col[part, h : h + 1] - row_in[c, h : h + 1, 0:depth]
                    scores = (jnp.exp2(jnp.minimum(spread, 126.0)) * mix).astype(BF16)
                    total = total + mm(scores, x_one[0:depth])
                y_out[pl.ds(r0 + 128 * half, 128), lanes] = total

    @pl.loop(0, SLOTS)
    def _(k):
        source = seg[8 + k]
        for b in range(GC // 128):
            part = slice(128 * b, 128 * (b + 1))
            block = state[k, :, part].T

            @pl.when(source < SLOTS)
            def _():
                own_out[jnp.minimum(source, SLOTS - 1), part, :] = block

            @pl.when(source == SLOTS)
            def _():
                lft_out[part, :] = block.astype(BF16)

            @pl.when(source == SLOTS + 1)
            def _():
                rgt_out[part, :] = block.astype(BF16)


def gate_kernel(y_in, z_in, gain, out):
    gated = y_in[...] * silu(z_in[...].astype(F32))
    mean = jnp.sum(gated * gated, axis=1, keepdims=True) * (1.0 / GC)
    out[...] = (gated * lax.rsqrt(mean + EPSILON) * gain[...]).astype(BF16)


VMEM = pl.BlockSpec(memory_space=pltpu.VMEM)
SMEM = pl.BlockSpec(memory_space=pltpu.SMEM)


def params(mib):
    return pltpu.CompilerParams(vmem_limit_bytes=mib * MIB)


def pack(bc_in, dt_in):
    return pl.pallas_call(
        pack_kernel,
        out_shape=jax.ShapeDtypeStruct((TENSOR, SRC_ROWS + GH, 2 * STATE), BF16),
        in_specs=[VMEM, VMEM],
        out_specs=VMEM,
        compiler_params=params(8),
        name="pack",
    )(bc_in, dt_in)


def prep(seg, bcdt, conv_state, own, lft, rgt, param, rate, bias):
    return pl.pallas_call(
        prep_kernel,
        out_shape=(
            jax.ShapeDtypeStruct((CHUNKS, STATE, Q), BF16),
            jax.ShapeDtypeStruct((ROWS, STATE), BF16),
            jax.ShapeDtypeStruct((CHUNKS, Q, Q), F32),
            jax.ShapeDtypeStruct((CHUNKS, Q, 128), F32),
            jax.ShapeDtypeStruct((CHUNKS, GH, Q), F32),
            jax.ShapeDtypeStruct((16, GC), F32),
            jax.ShapeDtypeStruct((16, 2 * STATE), F32),
            jax.ShapeDtypeStruct((SLOTS, STATE, GC), F32),
        ),
        in_specs=[SMEM] + [VMEM] * 8,
        out_specs=(VMEM,) * 8,
        scratch_shapes=[
            pltpu.VMEM((ROWS, 2 * STATE), BF16),
            pltpu.VMEM((ROWS, STATE), BF16),
            pltpu.VMEM((128, 2 * STATE), BF16),
        ],
        compiler_params=params(24),
        cost_estimate=pl.CostEstimate(
            flops=6_000_000_000, bytes_accessed=8 * MIB, transcendentals=500_000
        ),
        name="prep",
    )(seg, bcdt, conv_state, own, lft, rgt, param, rate, bias)


def scan(seg, x_rows, conv_state, param, skip, prepared):
    b_t, c_rows, mix, col, row, dec, init = prepared
    return pl.pallas_call(
        main_kernel,
        out_shape=(
            jax.ShapeDtypeStruct((ROWS, GC), F32),
            jax.ShapeDtypeStruct((SLOTS, GC, STATE), F32),
            jax.ShapeDtypeStruct((GC, STATE), BF16),
            jax.ShapeDtypeStruct((GC, STATE), BF16),
            jax.ShapeDtypeStruct((16, GC), F32),
        ),
        in_specs=[SMEM] + [VMEM] * 11,
        out_specs=(VMEM,) * 5,
        scratch_shapes=[
            pltpu.VMEM((128, GC), BF16),
            pltpu.VMEM((ROWS, GC), BF16),
            pltpu.VMEM((Q, GC), BF16),
            pltpu.VMEM((SLOTS, STATE, GC), F32),
            pltpu.VMEM((Q, GC), F32),
            pltpu.VMEM((256, GC), BF16),
            pltpu.VMEM((256, GC), BF16),
        ],
        compiler_params=params(40),
        cost_estimate=pl.CostEstimate(
            flops=20_000_000_000, bytes_accessed=16 * MIB, transcendentals=5_000_000
        ),
        name="scan",
    )(seg, x_rows, conv_state, param, skip, b_t, c_rows, mix, col, row, dec, init)


def gate(y, z_rows, gain):
    block = 128
    return pl.pallas_call(
        gate_kernel,
        out_shape=jax.ShapeDtypeStruct((ROWS, GC), BF16),
        grid=(ROWS // block,),
        in_specs=[
            pl.BlockSpec((block, GC), lambda i: (i, 0)),
            pl.BlockSpec((block, GC), lambda i: (i, 0)),
            pl.BlockSpec((1, GC), lambda i: (0, 0)),
        ],
        out_specs=pl.BlockSpec((block, GC), lambda i: (i, 0)),
        compiler_params=params(16),
        cost_estimate=pl.CostEstimate(
            flops=20_000_000, bytes_accessed=8 * MIB, transcendentals=1_000_000
        ),
        name="gate",
    )(y, z_rows, gain)


def shifted(value, steps):
    count = lax.axis_size("dp")
    pairs = [(source, (source + steps) % count) for source in range(count)]
    return lax.ppermute(value, "dp", pairs)


def plan(lengths, prefill_owner, row_start, me, left, right):
    ids = jnp.arange(prefill_owner.shape[0], dtype=jnp.int32)
    mine = prefill_owner == me
    home = ids // SLOTS
    code = jnp.where(home == me, ids % SLOTS, jnp.where(home == left, SLOTS, SLOTS + 1))
    before = mine[None, :] & (row_start[None, :] < row_start[:, None])
    rank = jnp.sum(before.astype(jnp.int32), axis=1)
    chosen = mine[None, :] & (rank[None, :] == jnp.arange(SLOTS, dtype=jnp.int32)[:, None])

    def pick(values):
        return jnp.sum(jnp.where(chosen, values[None, :], 0), axis=1)

    starts = pick(row_start)
    codes = pick(code)
    seg = jnp.concatenate([starts, starts + pick(lengths), codes, jnp.zeros((4,), jnp.int32)])
    slot_right = jnp.sum(jnp.where((home == me) & (prefill_owner == right), ids % SLOTS, 0))
    slot_left = jnp.sum(jnp.where((home == me) & (prefill_owner == left), ids % SLOTS, 0))
    return seg, codes, slot_right, slot_left


def shards(
    x_in,
    z_in,
    bc_in,
    dt_in,
    conv_x_param,
    conv_bc_param,
    decay_rate,
    dt_bias,
    skip_gain,
    norm_gain,
    ssm_state,
    conv_x_state,
    conv_bc_state,
    lengths,
    prefill_owner,
    row_start,
):
    dp_count = lax.axis_size("dp")
    me = lax.axis_index("dp")
    left = (me + dp_count - 1) % dp_count
    right = (me + 1) % dp_count
    bcdt = lax.all_to_all(pack(bc_in, dt_in), "tensor", split_axis=0, concat_axis=0, tiled=True)
    x_rows = lax.all_to_all(x_in, "tensor", split_axis=1, concat_axis=0, tiled=True)
    z_rows = lax.all_to_all(z_in, "tensor", split_axis=1, concat_axis=0, tiled=True)

    seg, codes, slot_right, slot_left = plan(lengths, prefill_owner, row_start, me, left, right)

    own = ssm_state.reshape(SLOTS, GC, STATE)
    conv = jnp.concatenate([conv_x_state, conv_bc_state], axis=2)
    width = conv.shape[2]
    lines = 3 * width // STATE

    def mover(slot):
        state = lax.dynamic_index_in_dim(own, slot, 0, keepdims=False)
        small = lax.dynamic_index_in_dim(conv, slot, 0, keepdims=False).reshape(lines, STATE)
        return jnp.concatenate([state, small, jnp.zeros((2, STATE), F32)], axis=0)

    from_left = shifted(mover(slot_right), 1)
    from_right = shifted(mover(slot_left), -1)

    def small_of(packed):
        return packed[GC : GC + lines].reshape(1, 3, width)

    candidates = jnp.concatenate([conv, small_of(from_left), small_of(from_right)], axis=0)
    match = codes[:, None] == jnp.arange(SLOTS + 2, dtype=jnp.int32)[None, :]
    conv_init = jnp.sum(jnp.where(match[:, :, None, None], candidates[None], 0.0), axis=1)
    conv_init = jnp.concatenate([conv_init.reshape(3 * SLOTS, width), jnp.zeros((4, width), F32)])

    b_t, c_rows, mix, col, row, dec, last_bc, init = prep(
        seg,
        bcdt,
        conv_init[:, GC:],
        own,
        from_left,
        from_right,
        conv_bc_param,
        decay_rate[:, None],
        dt_bias[:, None],
    )
    y, own_new, back_left, back_right, last_x = scan(
        seg,
        x_rows,
        conv_init[:, :GC],
        conv_x_param,
        jnp.repeat(skip_gain, HEADDIM)[None, :],
        (b_t, c_rows, mix, col, row, dec, init),
    )
    last = jnp.concatenate([last_x, last_bc], axis=1)[: 3 * SLOTS].reshape(SLOTS, 3, width)

    def last_of(code):
        return jnp.sum(jnp.where((codes == code)[:, None, None], last, 0.0), axis=0)

    def back(state, code):
        small = last_of(code).astype(BF16).reshape(lines, STATE)
        return jnp.concatenate([state, small, jnp.zeros((2, STATE), BF16)], axis=0)

    returned_right = shifted(back(back_left, SLOTS), -1)
    returned_left = shifted(back(back_right, SLOTS + 1), 1)

    new_ssm = own_new
    for packed, slot in ((returned_right, slot_right), (returned_left, slot_left)):
        new_ssm = lax.dynamic_update_index_in_dim(new_ssm, packed[:GC].astype(F32), slot, 0)
    slots = jnp.arange(SLOTS, dtype=jnp.int32)
    stay = slots[:, None] == codes[None, :]
    new_conv = jnp.sum(jnp.where(stay[:, :, None, None], last[None], 0.0), axis=1)
    for packed, slot in ((returned_right, slot_right), (returned_left, slot_left)):
        new_conv = jnp.where(
            (slots == slot)[:, None, None], small_of(packed).astype(F32), new_conv
        )
    y_out = gate(y, z_rows, norm_gain[None, :])
    return (
        y_out,
        new_ssm.reshape(ssm_state.shape),
        new_conv[:, :, :GC],
        new_conv[:, :, GC:],
    )


def solution(mesh):
    in_specs = (
        P(("dp", "tensor"), None),
        P(("dp", "tensor"), None),
        P(("dp", "tensor"), None),
        P(("dp", "tensor"), None),
        P(None, "tensor"),
        P(None, "tensor"),
        P("tensor"),
        P("tensor"),
        P("tensor"),
        P("tensor"),
        P("dp", "tensor", None, None),
        P("dp", None, "tensor"),
        P("dp", None, "tensor"),
        P(),
        P(),
        P(),
    )
    out_specs = (
        P("dp", "tensor"),
        P("dp", "tensor", None, None),
        P("dp", None, "tensor"),
        P("dp", None, "tensor"),
    )
    return jax.shard_map(shards, mesh=mesh, in_specs=in_specs, out_specs=out_specs, check_vma=False)
```

```python
import functools
import math

import jax
import jax.numpy as jnp
from jax import lax
from jax.experimental import pallas as pl
from jax.experimental.pallas import tpu as pltpu
from jax.sharding import PartitionSpec as P

HEADS = 128
HEADDIM = 64
STATE = 128
GROUPS = 8
SLOTS = 4
ROWS = 1024
GH = HEADS // GROUPS
GC = GH * HEADDIM
Q = 256
CHUNKS = ROWS // Q
TENSOR = 8
SRC_ROWS = ROWS // TENSOR
EPSILON = 1e-05
LOG2E = math.log2(math.e)
LANES = 2 * STATE
TILES = GC // LANES
BC_ROW = TILES * SRC_ROWS
DT_ROW = BC_ROW + SRC_ROWS
BLOCK_ROWS = DT_ROW + GH
MOVER_ROWS = GC + 32
GATE_ROWS = 128
ORDER = (4, 3, 5, 2, 6, 1, 7)
FIRST = (4, 3, 5)
SECOND = (2, 6)
THIRD = (1, 7)
MIB = 1 << 20

F32 = jnp.float32
BF16 = jnp.bfloat16


def mm(a, b):
    return jnp.dot(a, b, preferred_element_type=F32)


def iota(shape, dim):
    return lax.broadcasted_iota(jnp.int32, shape, dim)


def silu(v):
    half = v * 0.5
    return half + half * jnp.tanh(half)


def split2(v):
    hi = v.astype(BF16)
    return hi, (v - hi.astype(F32)).astype(BF16)


def split3(v):
    hi = v.astype(BF16)
    rest = v - hi.astype(F32)
    mid = rest.astype(BF16)
    return hi, mid, (rest - mid.astype(F32)).astype(BF16)


def segment_of(row_ids, seg):
    total = jnp.zeros(row_ids.shape, jnp.int32)
    for k in range(1, SLOTS):
        total = total + (row_ids >= seg[k]).astype(jnp.int32)
    return total


def boundary_targets(shape, dim, seg):
    idx = iota(shape, dim) % 16
    target = jnp.full(shape, -1, jnp.int32)
    for s in range(SLOTS):
        for q in range(3):
            target = jnp.where(idx == 3 * s + q, seg[s] + q, target)
    return jnp.where(iota(shape, dim) < 48, target, -1)


def last_rows(x_ref, lanes, seg):
    idx = iota((16, 1), 0)
    target = jnp.full((16, 1), -1, jnp.int32)
    for s in range(SLOTS):
        for q in range(3):
            target = jnp.where(idx == 3 * s + q, seg[4 + s] - 3 + q, target)
    picker = (iota((16, ROWS), 1) == target).astype(F32).astype(BF16)
    return mm(picker, x_ref[0:ROWS, lanes])


def boundary_terms(last, state, param, lanes):
    diff = state - pltpu.roll(last, 3, 0)
    q = iota((16, 1), 0) % 3
    term = param[0:1, lanes] * diff
    term = term + jnp.where(q <= 1, param[1:2, lanes] * pltpu.roll(diff, 15, 0), 0.0)
    term = term + jnp.where(q == 0, param[2:3, lanes] * pltpu.roll(diff, 14, 0), 0.0)
    return split3(term)


def conv_rows(x_ref, r0, count, lanes, param, terms_ref, targets):
    prev = pl.multiple_of(jnp.maximum(r0 - 16, 0), 16)
    halo = x_ref[pl.ds(prev, 16), lanes].astype(F32) * jnp.where(r0 > 0, 1.0, 0.0)
    value = jnp.concatenate([halo, x_ref[pl.ds(r0, count), lanes].astype(F32)], axis=0)
    onehot = (iota((count, 128), 0) + r0 == targets).astype(F32).astype(BF16)
    total = mm(onehot, terms_ref[:, lanes]) + param[4:5, lanes]
    total = total + param[3:4, lanes] * value[16:]
    for lag in (1, 2, 3):
        total = total + param[3 - lag : 4 - lag, lanes] * pltpu.roll(value, lag, 0)[16:]
    return silu(total)


def store_terms(terms_ref, lanes, parts):
    for i, part in enumerate(parts):
        terms_ref[16 * i : 16 * i + 16, lanes] = part


def copy_all(copies, sems):
    started = [
        pltpu.make_async_copy(source, target, sems.at[i])
        for i, (source, target) in enumerate(copies)
    ]
    for copy in started:
        copy.start()
    for copy in started:
        copy.wait()


def pack_kernel(offsets, here, x, bc, dt, *rest):
    count = len(offsets)
    outs, (stage, dt_all, dt_turned, sems, out_sems, dt_sem) = rest[:count], rest[count:]
    dt_load = pltpu.make_async_copy(dt, dt_all, dt_sem)
    dt_load.start()
    loads = []
    for n, d in enumerate(offsets):
        to = (here[0] + d) % TENSOR
        sources = []
        for i in range(TILES):
            lanes = pl.ds(pl.multiple_of(to * GC + LANES * i, LANES), LANES)
            sources.append(x.at[:, lanes])
        sources.append(bc.at[:, pl.ds(pl.multiple_of(to * LANES, LANES), LANES)])
        loads.append(
            [
                pltpu.make_async_copy(
                    source,
                    stage.at[n, SRC_ROWS * i : SRC_ROWS * (i + 1), :],
                    sems.at[n * (TILES + 1) + i],
                )
                for i, source in enumerate(sources)
            ]
        )
        for copy in loads[-1]:
            copy.start()
    dt_load.wait()
    dt_turned[...] = dt_all[...].astype(F32).T.astype(BF16)
    stores = []
    for n, d in enumerate(offsets):
        to = (here[0] + d) % TENSOR
        heads = pl.ds(pl.multiple_of(to * GH, GH), GH)
        stage[n, DT_ROW:BLOCK_ROWS, 0:SRC_ROWS] = dt_turned[heads, :]
        stage[n, DT_ROW:BLOCK_ROWS, SRC_ROWS:] = jnp.zeros((GH, LANES - SRC_ROWS), BF16)
        for copy in loads[n]:
            copy.wait()
        stores.append(pltpu.make_async_copy(stage.at[n], outs[n], out_sems.at[n]))
        stores[-1].start()
    for copy in stores:
        copy.wait()


def mover_kernel(slots, own, small, right_out, left_out, sems):
    outs = (right_out, left_out)
    for i in range(2):
        outs[i][GC:MOVER_ROWS, :] = small[i]
    copy_all([(own.at[slots[i]], outs[i].at[0:GC, :]) for i in range(2)], sems)


def init_kernel(seg, own, lft, rgt, init_out):
    def load_state(k, block_of):
        for b in range(GC // 128):
            init_out[k, :, 128 * b : 128 * (b + 1)] = block_of(b).T

    @pl.loop(0, SLOTS)
    def _(k):
        source = seg[8 + k]

        @pl.when(source < SLOTS)
        def _():
            load_state(k, lambda b: own[jnp.minimum(source, SLOTS - 1), 128 * b : 128 * (b + 1), :])

        @pl.when(source == SLOTS)
        def _():
            load_state(k, lambda b: lft[128 * b : 128 * (b + 1), :])

        @pl.when(source == SLOTS + 1)
        def _():
            load_state(k, lambda b: rgt[128 * b : 128 * (b + 1), :])


def source_of(here, d):
    return (here[0] + (TENSOR - d)) % TENSOR


def prep_kernel(
    seg,
    here,
    *rest,
):
    prep_body(seg, here, rest[:TENSOR], *rest[TENSOR:])


def prep_body(
    seg,
    here,
    blocks,
    conv_state,
    param,
    rate,
    bias,
    b_t_out,
    c_out,
    mix_out,
    col_out,
    row_out,
    dec_out,
    last_out,
    bc_rows,
    dt_rows,
    b_rows,
    terms,
    sems,
):
    copies = []
    for d in range(TENSOR):
        source = source_of(here, d)
        rows = pl.ds(pl.multiple_of(source * SRC_ROWS, SRC_ROWS), SRC_ROWS)
        copies.append((blocks[d].at[BC_ROW:DT_ROW, :], bc_rows.at[rows, :]))
        copies.append((blocks[d].at[DT_ROW:BLOCK_ROWS, :], dt_rows.at[source]))
    copy_all(copies, sems)
    every = slice(0, 2 * STATE)
    last = last_rows(bc_rows, every, seg)
    last_out[...] = last
    terms[...] = jnp.zeros_like(terms)
    store_terms(terms, every, boundary_terms(last, conv_state[...], param, every))
    targets = boundary_targets((1, 128), 1, seg)

    @pl.loop(0, ROWS // 64)
    def _(i):
        r0 = pl.multiple_of(i * 64, 64)
        value = conv_rows(bc_rows, r0, 64, every, param, terms, targets).astype(BF16)
        b_rows[pl.ds(r0, 64), :] = value[:, 0:STATE]
        c_out[pl.ds(r0, 64), :] = value[:, STATE:]

    dec_sum = jnp.zeros((GH, 128), F32)
    for c in range(CHUNKS):
        b_t = b_rows[Q * c : Q * (c + 1), :].astype(F32).T.astype(BF16)
        b_t_out[c] = b_t
        seg_col = segment_of(iota((Q, 1), 0) + Q * c, seg)
        seg_row = segment_of(iota((1, Q), 1) + Q * c, seg)
        same = seg_col == seg_row
        row_id, col_id = iota((Q, Q), 0), iota((Q, Q), 1)
        mix = mm(c_out[Q * c : Q * (c + 1), :], b_t)
        mix_out[c] = jnp.where(same & (col_id <= row_id), mix, 0.0)
        up_to = jnp.where(same & (row_id <= col_id), 1.0, 0.0).astype(BF16)
        after = jnp.where(same & (row_id > col_id), 1.0, 0.0).astype(BF16)
        raw = jnp.concatenate(
            [dt_rows[s, :, 0:SRC_ROWS] for s in (2 * c, 2 * c + 1)], axis=1
        ).astype(F32) + bias[...]
        step = jnp.maximum(raw, 0.0) + jnp.log1p(jnp.exp(-jnp.abs(raw)))
        log_decay = step * rate[...] * (-LOG2E)
        parts = jnp.concatenate(split3(log_decay), axis=0)

        def summed(mask):
            three = mm(parts, mask)
            return three[0:GH] + three[GH : 2 * GH] + three[2 * GH : 3 * GH]

        running = summed(up_to)
        rest = summed(after)
        row_out[c] = running - jnp.log2(step)
        stack = jnp.concatenate(
            [running, jnp.exp2(running), jnp.exp2(rest) * step, jnp.zeros((80, Q), F32)], axis=0
        )
        col_out[c] = stack.T
        pair = jnp.where(seg_col + SLOTS * c == iota((Q, 128), 1), 1.0, 0.0).astype(BF16)
        dec_sum = dec_sum + summed(pair)
    decay = jnp.concatenate([jnp.exp2(dec_sum), jnp.zeros((128 - GH, 128), F32)], axis=0).T[0:16]
    spread = jnp.where(iota((128, GC), 0) == iota((128, GC), 1) // HEADDIM, 1.0, 0.0).astype(BF16)
    dec_hi, dec_lo = split2(decay)
    dec_out[...] = mm(dec_hi, spread) + mm(dec_lo, spread)


def main_kernel(seg, here, *rest):
    main_body(seg, here, rest[:TENSOR], *rest[TENSOR:])


def main_body(
    seg,
    here,
    blocks,
    conv_state,
    param,
    skip,
    b_t_in,
    c_in,
    mix_in,
    col_in,
    row_in,
    dec_in,
    init_in,
    last_bc,
    y_out,
    own_out,
    lft_out,
    rgt_out,
    last_out,
    terms,
    x_conv,
    x_weighted,
    state,
    inter,
    spread_e,
    spread_w,
    x_in,
    tail,
    sems,
    y_stage,
    y_sems,
):
    def store(c):
        rows = pl.ds(pl.multiple_of(c * Q, Q), Q)
        return pltpu.make_async_copy(y_stage.at[rows, :], y_out.at[rows, :], y_sems.at[c])

    copies = []
    for d in range(TENSOR):
        rows = pl.ds(pl.multiple_of(source_of(here, d) * SRC_ROWS, SRC_ROWS), SRC_ROWS)
        for i in range(TILES):
            part = blocks[d].at[SRC_ROWS * i : SRC_ROWS * (i + 1), :]
            copies.append((part, x_in.at[rows, LANES * i : LANES * (i + 1)]))
    copy_all(copies, sems)
    terms[...] = jnp.zeros_like(terms)
    targets = boundary_targets((1, 128), 1, seg)
    for lt in range(GC // 256):
        lanes = slice(256 * lt, 256 * (lt + 1))
        last = last_rows(x_in, lanes, seg)
        last_out[:, lanes] = last
        store_terms(terms, lanes, boundary_terms(last, conv_state[:, lanes], param, lanes))
        row_id = iota((256, 256), 0) % 128
        head_id = (iota((256, 256), 1) + 256 * lt) // HEADDIM
        spread_e[:, lanes] = jnp.where(row_id - GH == head_id, 1.0, 0.0).astype(BF16)
        spread_w[:, lanes] = jnp.where(row_id - 2 * GH == head_id, 1.0, 0.0).astype(BF16)

    @pl.loop(0, ROWS // 64)
    def _(i):
        r0 = pl.multiple_of(i * 64, 64)
        for lt in range(GC // 256):
            lanes = slice(256 * lt, 256 * (lt + 1))
            value = conv_rows(x_in, r0, 64, lanes, param, terms, targets)
            x_conv[pl.ds(r0, 64), lanes] = value.astype(BF16)

    @pl.loop(0, SLOTS)
    def _(k):
        state[k] = init_in[k]

    @pl.loop(0, CHUNKS)
    def _(c):
        r0 = pl.multiple_of(c * Q, Q)
        rows = pl.ds(r0, Q)
        col = col_in[c]
        col_hi, col_lo = split2(col)
        col_two = jnp.concatenate([col_hi, col_lo], axis=1)
        for lt in range(GC // 256):
            lanes = slice(256 * lt, 256 * (lt + 1))
            weight = mm(col_two, spread_w[:, lanes])
            x_weighted[:, lanes] = (x_conv[rows, lanes].astype(F32) * weight).astype(BF16)
            inter[:, lanes] = jnp.zeros((Q, 256), F32)

        @pl.loop(0, SLOTS)
        def _(k):
            first, end = seg[k], seg[4 + k]

            @pl.when((first < r0 + Q) & (end > r0))
            def _():
                row_id = iota((Q, STATE), 0) + r0
                c_part = jnp.where(
                    (row_id >= first) & (row_id < end), c_in[rows, :].astype(F32), 0.0
                ).astype(BF16)
                c_two = jnp.concatenate([c_part, c_part], axis=1)
                col_id = iota((STATE, Q), 1) + r0
                b_part = jnp.where(
                    (col_id >= first) & (col_id < end), b_t_in[c].astype(F32), 0.0
                ).astype(BF16)
                decay = dec_in[pl.ds(c * SLOTS + k, 1), :]
                for lt in range(GC // 256):
                    lanes = slice(256 * lt, 256 * (lt + 1))
                    old = state[k, :, lanes]
                    both = jnp.concatenate(split2(old), axis=0)
                    inter[:, lanes] += mm(c_two, both)
                    state[k, :, lanes] = old * decay[:, lanes] + mm(b_part, x_weighted[:, lanes])

        low_half = iota((Q, 128), 1) < HEADDIM
        for lt in range(GC // 256):
            lanes = slice(256 * lt, 256 * (lt + 1))
            scale = mm(col_two, spread_e[:, lanes])
            inter[:, lanes] = inter[:, lanes] * scale + x_conv[rows, lanes].astype(F32) * skip[
                0:1, lanes
            ]
        for hp in range(GH // 2):
            lanes = slice(128 * hp, 128 * (hp + 1))
            x_pair = x_conv[rows, lanes].astype(F32)
            x_low = jnp.where(low_half, x_pair, 0.0).astype(BF16)
            x_high = jnp.where(low_half, 0.0, x_pair).astype(BF16)
            for half in range(2):
                depth = 128 * (half + 1)
                part = slice(128 * half, 128 * (half + 1))
                mix = mix_in[c, part, 0:depth]
                total = inter[part, lanes]
                for h, x_one in ((2 * hp, x_low), (2 * hp + 1, x_high)):
                    spread = col[part, h : h + 1] - row_in[c, h : h + 1, 0:depth]
                    scores = (jnp.exp2(jnp.minimum(spread, 126.0)) * mix).astype(BF16)
                    total = total + mm(scores, x_one[0:depth])
                y_stage[pl.ds(r0 + 128 * half, 128), lanes] = total
        store(c).start()

    def send_back(k, out):
        for b in range(GC // 128):
            part = slice(128 * b, 128 * (b + 1))
            out[part, :] = state[k, :, part].T.astype(BF16)
        lines = (GC + LANES) // 128
        tail[...] = jnp.zeros_like(tail)
        for j in range(3):
            row = pl.ds(3 * k + j, 1)
            line = jnp.concatenate([last_out[row, :], last_bc[row, :]], axis=1)
            for b in range(lines):
                place = slice(j * lines + b, j * lines + b + 1)
                tail[place, :] = line[:, 128 * b : 128 * (b + 1)]
        out[GC:MOVER_ROWS, :] = tail[...].astype(BF16)

    @pl.loop(0, SLOTS)
    def _(k):
        source = seg[8 + k]

        @pl.when(source < SLOTS)
        def _():
            for b in range(GC // 128):
                part = slice(128 * b, 128 * (b + 1))
                own_out[jnp.minimum(source, SLOTS - 1), part, :] = state[k, :, part].T

        @pl.when(source == SLOTS)
        def _():
            send_back(k, lft_out)

        @pl.when(source == SLOTS + 1)
        def _():
            send_back(k, rgt_out)

    @pl.loop(0, CHUNKS)
    def _(c):
        store(c).wait()


def gate_kernel(y_in, z_in, gain, out, y_stage, stage, load_sems, sems):
    def rows_of(i):
        return pl.ds(pl.multiple_of(i * GATE_ROWS, GATE_ROWS), GATE_ROWS)

    def load(i):
        return pltpu.make_async_copy(
            y_in.at[rows_of(i), :], y_stage.at[rows_of(i), :], load_sems.at[i]
        )

    def store(i):
        return pltpu.make_async_copy(stage.at[rows_of(i), :], out.at[rows_of(i), :], sems.at[i])

    for i in range(ROWS // GATE_ROWS):
        load(i).start()

    @pl.loop(0, ROWS // GATE_ROWS)
    def _(i):
        load(i).wait()
        for part in range(GATE_ROWS // 16):
            rows = pl.ds(pl.multiple_of(i * GATE_ROWS + 16 * part, 16), 16)
            gated = y_stage[rows, :] * silu(z_in[rows, :].astype(F32))
            mean = jnp.sum(gated * gated, axis=1, keepdims=True) * (1.0 / GC)
            stage[rows, :] = (gated * lax.rsqrt(mean + EPSILON) * gain[...]).astype(BF16)
        store(i).start()

    @pl.loop(0, ROWS // GATE_ROWS)
    def _(i):
        store(i).wait()


VMEM = pl.BlockSpec(memory_space=pltpu.VMEM)
SMEM = pl.BlockSpec(memory_space=pltpu.SMEM)
ANY = pl.BlockSpec(memory_space=pl.ANY)
HBM = pl.BlockSpec(memory_space=pltpu.HBM)


def in_hbm(value):
    return pltpu.with_memory_space_constraint(value, pltpu.HBM)


def params(mib):
    return pltpu.CompilerParams(vmem_limit_bytes=mib * MIB)


def pack(offsets, here, x_in, bc_in, dt_in):
    count = len(offsets)
    blocks = pl.pallas_call(
        functools.partial(pack_kernel, offsets),
        out_shape=(pltpu.HBM((BLOCK_ROWS, LANES), BF16),) * count,
        in_specs=[SMEM, HBM, HBM, HBM],
        out_specs=(HBM,) * count,
        scratch_shapes=[
            pltpu.VMEM((count, BLOCK_ROWS, LANES), BF16),
            pltpu.VMEM((SRC_ROWS, HEADS), BF16),
            pltpu.VMEM((HEADS, SRC_ROWS), BF16),
            pltpu.SemaphoreType.DMA((count * (TILES + 1),)),
            pltpu.SemaphoreType.DMA((count,)),
            pltpu.SemaphoreType.DMA,
        ],
        compiler_params=params(8),
        name="pack",
    )(here, in_hbm(x_in), in_hbm(bc_in), in_hbm(dt_in))
    return dict(zip(offsets, blocks))


def movers(slots, own, small):
    return pl.pallas_call(
        mover_kernel,
        out_shape=(jax.ShapeDtypeStruct((MOVER_ROWS, STATE), F32),) * 2,
        in_specs=[SMEM, HBM, VMEM],
        out_specs=(VMEM,) * 2,
        scratch_shapes=[pltpu.SemaphoreType.DMA((2,))],
        compiler_params=params(8),
        name="movers",
    )(slots, in_hbm(own), small)


def initial(seg, own, lft, rgt):
    return pl.pallas_call(
        init_kernel,
        out_shape=jax.ShapeDtypeStruct((SLOTS, STATE, GC), F32),
        in_specs=[SMEM] + [VMEM] * 3,
        out_specs=VMEM,
        compiler_params=params(8),
        cost_estimate=pl.CostEstimate(
            flops=2_000_000_000, bytes_accessed=4 * MIB, transcendentals=0
        ),
        name="initial",
    )(seg, own, lft, rgt)


def prep(seg, here, blocks, conv_state, param, rate, bias):
    return pl.pallas_call(
        prep_kernel,
        out_shape=(
            jax.ShapeDtypeStruct((CHUNKS, STATE, Q), BF16),
            jax.ShapeDtypeStruct((ROWS, STATE), BF16),
            jax.ShapeDtypeStruct((CHUNKS, Q, Q), F32),
            jax.ShapeDtypeStruct((CHUNKS, Q, 128), F32),
            jax.ShapeDtypeStruct((CHUNKS, GH, Q), F32),
            jax.ShapeDtypeStruct((16, GC), F32),
            jax.ShapeDtypeStruct((16, 2 * STATE), F32),
        ),
        in_specs=[SMEM, SMEM] + [ANY] * TENSOR + [VMEM] * 4,
        out_specs=(VMEM,) * 7,
        scratch_shapes=[
            pltpu.VMEM((ROWS, 2 * STATE), BF16),
            pltpu.VMEM((TENSOR, GH, LANES), BF16),
            pltpu.VMEM((ROWS, STATE), BF16),
            pltpu.VMEM((128, 2 * STATE), BF16),
            pltpu.SemaphoreType.DMA((2 * TENSOR,)),
        ],
        compiler_params=params(8),
        cost_estimate=pl.CostEstimate(
            flops=6_000_000_000, bytes_accessed=8 * MIB, transcendentals=500_000
        ),
        name="prep",
    )(seg, here, *blocks, conv_state, param, rate, bias)


def scan(seg, here, blocks, conv_state, param, skip, prepared, init):
    b_t, c_rows, mix, col, row, dec, last_bc = prepared
    return pl.pallas_call(
        main_kernel,
        out_shape=(
            pltpu.HBM((ROWS, GC), F32),
            jax.ShapeDtypeStruct((SLOTS, GC, STATE), F32),
            jax.ShapeDtypeStruct((MOVER_ROWS, STATE), BF16),
            jax.ShapeDtypeStruct((MOVER_ROWS, STATE), BF16),
            jax.ShapeDtypeStruct((16, GC), F32),
        ),
        in_specs=[SMEM, SMEM] + [ANY] * TENSOR + [VMEM] * 11,
        out_specs=(HBM,) + (VMEM,) * 4,
        scratch_shapes=[
            pltpu.VMEM((128, GC), BF16),
            pltpu.VMEM((ROWS, GC), BF16),
            pltpu.VMEM((Q, GC), BF16),
            pltpu.VMEM((SLOTS, STATE, GC), F32),
            pltpu.VMEM((Q, GC), F32),
            pltpu.VMEM((256, GC), BF16),
            pltpu.VMEM((256, GC), BF16),
            pltpu.VMEM((ROWS, GC), BF16),
            pltpu.VMEM((32, STATE), F32),
            pltpu.SemaphoreType.DMA((TENSOR * TILES,)),
            pltpu.VMEM((ROWS, GC), F32),
            pltpu.SemaphoreType.DMA((CHUNKS,)),
        ],
        compiler_params=params(20),
        cost_estimate=pl.CostEstimate(
            flops=20_000_000_000, bytes_accessed=16 * MIB, transcendentals=5_000_000
        ),
        name="scan",
    )(
        seg, here, *blocks, conv_state, param, skip, b_t, c_rows, mix, col, row, dec, init, last_bc
    )


def gate(y, z_rows, gain):
    return pl.pallas_call(
        gate_kernel,
        out_shape=jax.ShapeDtypeStruct((ROWS, GC), BF16),
        in_specs=[HBM, VMEM, VMEM],
        out_specs=ANY,
        scratch_shapes=[
            pltpu.VMEM((ROWS, GC), F32),
            pltpu.VMEM((ROWS, GC), BF16),
            pltpu.SemaphoreType.DMA((ROWS // GATE_ROWS,)),
            pltpu.SemaphoreType.DMA((ROWS // GATE_ROWS,)),
        ],
        compiler_params=params(12),
        cost_estimate=pl.CostEstimate(
            flops=20_000_000, bytes_accessed=8 * MIB, transcendentals=1_000_000
        ),
        name="gate",
    )(in_hbm(y), z_rows, gain)


def shifted(value, steps):
    count = lax.axis_size("dp")
    pairs = [(source, (source + steps) % count) for source in range(count)]
    return lax.ppermute(value, "dp", pairs)


def rotated(value, steps):
    count = lax.axis_size("tensor")
    pairs = [(source, (source + steps) % count) for source in range(count)]
    return lax.ppermute(value, "tensor", pairs)


def after(value, *earlier):
    if not earlier:
        return value
    return lax.optimization_barrier((value, *earlier))[0]


def plan(lengths, prefill_owner, row_start, me, left, right):
    ids = jnp.arange(prefill_owner.shape[0], dtype=jnp.int32)
    mine = prefill_owner == me
    home = ids // SLOTS
    code = jnp.where(home == me, ids % SLOTS, jnp.where(home == left, SLOTS, SLOTS + 1))
    before = mine[None, :] & (row_start[None, :] < row_start[:, None])
    rank = jnp.sum(before.astype(jnp.int32), axis=1)
    chosen = mine[None, :] & (rank[None, :] == jnp.arange(SLOTS, dtype=jnp.int32)[:, None])

    def pick(values):
        return jnp.sum(jnp.where(chosen, values[None, :], 0), axis=1)

    starts = pick(row_start)
    codes = pick(code)
    seg = jnp.concatenate([starts, starts + pick(lengths), codes, jnp.zeros((4,), jnp.int32)])
    slot_right = jnp.sum(jnp.where((home == me) & (prefill_owner == right), ids % SLOTS, 0))
    slot_left = jnp.sum(jnp.where((home == me) & (prefill_owner == left), ids % SLOTS, 0))
    return seg, codes, slot_right, slot_left


def shards(
    x_in,
    z_in,
    bc_in,
    dt_in,
    conv_x_param,
    conv_bc_param,
    decay_rate,
    dt_bias,
    skip_gain,
    norm_gain,
    ssm_state,
    conv_x_state,
    conv_bc_state,
    lengths,
    prefill_owner,
    row_start,
):
    dp_count = lax.axis_size("dp")
    me = lax.axis_index("dp")
    left = (me + dp_count - 1) % dp_count
    right = (me + 1) % dp_count
    here = lax.axis_index("tensor")
    here_ref = here.astype(jnp.int32)[None]
    packed = pack(FIRST, here_ref, x_in, bc_in, dt_in)
    packed |= pack(
        SECOND + THIRD + (0,), after(here_ref, packed[FIRST[0]]), x_in, bc_in, dt_in
    )
    blocks = {0: packed[0]}
    for d in FIRST:
        blocks[d] = rotated(packed[d], d)

    seg, codes, slot_right, slot_left = plan(lengths, prefill_owner, row_start, me, left, right)

    own = ssm_state.reshape(SLOTS, GC, STATE)
    conv = jnp.concatenate([conv_x_state, conv_bc_state], axis=2)
    width = conv.shape[2]
    lines = 3 * width // STATE

    def small_mover(slot):
        small = lax.dynamic_index_in_dim(conv, slot, 0, keepdims=False).reshape(lines, STATE)
        return jnp.concatenate([small, jnp.zeros((2, STATE), F32)], axis=0)

    move_right, move_left = movers(
        after(jnp.stack([slot_right, slot_left]).astype(jnp.int32), packed[0]),
        own,
        jnp.stack([small_mover(slot_right), small_mover(slot_left)]),
    )
    from_left = shifted(move_right, 1)
    from_right = shifted(move_left, -1)
    for d in SECOND:
        blocks[d] = rotated(after(packed[d], from_left, from_right), d)

    def small_of(packed):
        return packed[GC : GC + lines].reshape(1, 3, width)

    candidates = jnp.concatenate([conv, small_of(from_left), small_of(from_right)], axis=0)
    match = codes[:, None] == jnp.arange(SLOTS + 2, dtype=jnp.int32)[None, :]
    conv_init = jnp.sum(jnp.where(match[:, :, None, None], candidates[None], 0.0), axis=1)
    conv_init = jnp.concatenate([conv_init.reshape(3 * SLOTS, width), jnp.zeros((4, width), F32)])

    z_sent = z_in.reshape(SRC_ROWS, TENSOR, GC).transpose(1, 0, 2)
    init = initial(seg, own, from_left, from_right)
    conv_init, init, z_sent, seg, gain, skip, rate, bias = lax.optimization_barrier(
        (
            conv_init,
            init,
            z_sent,
            seg,
            norm_gain[None, :],
            jnp.repeat(skip_gain, HEADDIM)[None, :],
            decay_rate[:, None],
            dt_bias[:, None],
        )
    )
    for d in THIRD:
        blocks[d] = rotated(after(packed[d], conv_init, z_sent, *[blocks[e] for e in FIRST[1:]]), d)
    z_sent = after(z_sent, *[blocks[e] for e in FIRST])
    z_rows = lax.all_to_all(z_sent, "tensor", split_axis=0, concat_axis=0, tiled=True)
    z_rows = z_rows.reshape(ROWS, GC)

    in_order = [blocks[d] for d in range(TENSOR)]
    prepared = prep(
        seg,
        here_ref,
        in_order,
        conv_init[:, GC:],
        conv_bc_param,
        rate,
        bias,
    )
    y, own_new, back_left, back_right, last_x = scan(
        seg,
        here_ref,
        in_order,
        conv_init[:, :GC],
        conv_x_param,
        skip,
        prepared,
        init,
    )
    returned_right = shifted(back_left, -1)
    returned_left = shifted(back_right, 1)
    last = jnp.concatenate([last_x, prepared[6]], axis=1)[: 3 * SLOTS].reshape(SLOTS, 3, width)

    new_ssm = own_new
    for packed, slot in ((returned_right, slot_right), (returned_left, slot_left)):
        new_ssm = lax.dynamic_update_index_in_dim(new_ssm, packed[:GC].astype(F32), slot, 0)
    slots = jnp.arange(SLOTS, dtype=jnp.int32)
    stay = slots[:, None] == codes[None, :]
    new_conv = jnp.sum(jnp.where(stay[:, :, None, None], last[None], 0.0), axis=1)
    for packed, slot in ((returned_right, slot_right), (returned_left, slot_left)):
        new_conv = jnp.where(
            (slots == slot)[:, None, None], small_of(packed).astype(F32), new_conv
        )
    new_cx, new_cbc = new_conv[:, :, :GC], new_conv[:, :, GC:]

    y, new_ssm, new_cx, new_cbc = lax.optimization_barrier((y, new_ssm, new_cx, new_cbc))
    y_out = gate(y, z_rows, gain)
    return y_out, new_ssm.reshape(ssm_state.shape), new_cx, new_cbc


def solution(mesh):
    in_specs = (
        P(("dp", "tensor"), None),
        P(("dp", "tensor"), None),
        P(("dp", "tensor"), None),
        P(("dp", "tensor"), None),
        P(None, "tensor"),
        P(None, "tensor"),
        P("tensor"),
        P("tensor"),
        P("tensor"),
        P("tensor"),
        P("dp", "tensor", None, None),
        P("dp", None, "tensor"),
        P("dp", None, "tensor"),
        P(),
        P(),
        P(),
    )
    out_specs = (
        P("dp", "tensor"),
        P("dp", "tensor", None, None),
        P("dp", None, "tensor"),
        P("dp", None, "tensor"),
    )
    return jax.shard_map(shards, mesh=mesh, in_specs=in_specs, out_specs=out_specs, check_vma=False)
```

```python
import functools
import math

import jax
import jax.numpy as jnp
from jax import lax
from jax.experimental import pallas as pl
from jax.experimental.pallas import tpu as pltpu
from jax.sharding import PartitionSpec as P

HEADS = 128
HEADDIM = 64
STATE = 128
GROUPS = 8
SLOTS = 4
ROWS = 1024
GH = HEADS // GROUPS
GC = GH * HEADDIM
Q = 256
CHUNKS = ROWS // Q
TENSOR = 8
SRC_ROWS = ROWS // TENSOR
EPSILON = 1e-05
LOG2E = math.log2(math.e)
LANES = 128
TILES = GC // LANES
BC_TILES = 2 * STATE // LANES
BC_ROW = TILES * SRC_ROWS
DT_ROW = BC_ROW + BC_TILES * SRC_ROWS
BLOCK_ROWS = DT_ROW + GH
MOVER_ROWS = GC + 32
GATE_ROWS = 128
ORDER = (4, 3, 5, 2, 6, 1, 7)
FIRST = (4, 3, 5)
SECOND = (2, 6)
THIRD = (1, 7)
MIB = 1 << 20

F32 = jnp.float32
BF16 = jnp.bfloat16


def mm(a, b):
    return jnp.dot(a, b, preferred_element_type=F32)


def iota(shape, dim):
    return lax.broadcasted_iota(jnp.int32, shape, dim)


def silu(v):
    half = v * 0.5
    return half + half * jnp.tanh(half)


def split2(v):
    hi = v.astype(BF16)
    return hi, (v - hi.astype(F32)).astype(BF16)


def split3(v):
    hi = v.astype(BF16)
    rest = v - hi.astype(F32)
    mid = rest.astype(BF16)
    return hi, mid, (rest - mid.astype(F32)).astype(BF16)


def segment_of(row_ids, seg):
    total = jnp.zeros(row_ids.shape, jnp.int32)
    for k in range(1, SLOTS):
        total = total + (row_ids >= seg[k]).astype(jnp.int32)
    return total


def boundary_targets(shape, dim, seg):
    idx = iota(shape, dim) % 16
    target = jnp.full(shape, -1, jnp.int32)
    for s in range(SLOTS):
        for q in range(3):
            target = jnp.where(idx == 3 * s + q, seg[s] + q, target)
    return jnp.where(iota(shape, dim) < 48, target, -1)


def last_rows(x_ref, lanes, seg):
    idx = iota((16, 1), 0)
    target = jnp.full((16, 1), -1, jnp.int32)
    for s in range(SLOTS):
        for q in range(3):
            target = jnp.where(idx == 3 * s + q, seg[4 + s] - 3 + q, target)
    picker = (iota((16, ROWS), 1) == target).astype(F32).astype(BF16)
    return mm(picker, x_ref[0:ROWS, lanes])


def boundary_terms(last, state, param, lanes):
    diff = state - pltpu.roll(last, 3, 0)
    q = iota((16, 1), 0) % 3
    term = param[0:1, lanes] * diff
    term = term + jnp.where(q <= 1, param[1:2, lanes] * pltpu.roll(diff, 15, 0), 0.0)
    term = term + jnp.where(q == 0, param[2:3, lanes] * pltpu.roll(diff, 14, 0), 0.0)
    return split3(term)


def conv_rows(x_ref, r0, count, lanes, param, terms_ref, targets):
    prev = pl.multiple_of(jnp.maximum(r0 - 16, 0), 16)
    halo = x_ref[pl.ds(prev, 16), lanes].astype(F32) * jnp.where(r0 > 0, 1.0, 0.0)
    value = jnp.concatenate([halo, x_ref[pl.ds(r0, count), lanes].astype(F32)], axis=0)
    onehot = (iota((count, 128), 0) + r0 == targets).astype(F32).astype(BF16)
    total = mm(onehot, terms_ref[:, lanes]) + param[4:5, lanes]
    total = total + param[3:4, lanes] * value[16:]
    for lag in (1, 2, 3):
        total = total + param[3 - lag : 4 - lag, lanes] * pltpu.roll(value, lag, 0)[16:]
    return silu(total)


def store_terms(terms_ref, lanes, parts):
    for i, part in enumerate(parts):
        terms_ref[16 * i : 16 * i + 16, lanes] = part


def copy_all(copies, sems):
    started = [
        pltpu.make_async_copy(source, target, sems.at[i])
        for i, (source, target) in enumerate(copies)
    ]
    for copy in started:
        copy.start()
    for copy in started:
        copy.wait()


def pack_kernel(offsets, here, x, bc, dt, *rest):
    count = len(offsets)
    outs, (stage, dt_all, dt_turned, sems, out_sems, dt_sem) = rest[:count], rest[count:]
    dt_load = pltpu.make_async_copy(dt, dt_all, dt_sem)
    dt_load.start()
    loads = []
    for n, d in enumerate(offsets):
        to = (here[0] + d) % TENSOR
        sources = []
        for i in range(TILES):
            lanes = pl.ds(pl.multiple_of(to * GC + LANES * i, LANES), LANES)
            sources.append(x.at[:, lanes])
        for i in range(BC_TILES):
            lanes = pl.ds(pl.multiple_of(to * 2 * STATE + LANES * i, LANES), LANES)
            sources.append(bc.at[:, lanes])
        loads.append(
            [
                pltpu.make_async_copy(
                    source,
                    stage.at[n, SRC_ROWS * i : SRC_ROWS * (i + 1), :],
                    sems.at[n * (TILES + BC_TILES) + i],
                )
                for i, source in enumerate(sources)
            ]
        )
        for copy in loads[-1]:
            copy.start()
    dt_load.wait()
    dt_turned[...] = dt_all[...].astype(F32).T.astype(BF16)
    stores = []
    for n, d in enumerate(offsets):
        to = (here[0] + d) % TENSOR
        heads = pl.ds(pl.multiple_of(to * GH, GH), GH)
        stage[n, DT_ROW:BLOCK_ROWS, :] = dt_turned[heads, :]
        for copy in loads[n]:
            copy.wait()
        stores.append(pltpu.make_async_copy(stage.at[n], outs[n], out_sems.at[n]))
        stores[-1].start()
    for copy in stores:
        copy.wait()


def mover_kernel(slots, own, small, right_out, left_out, sems):
    outs = (right_out, left_out)
    for i in range(2):
        outs[i][GC:MOVER_ROWS, :] = small[i]
    copy_all([(own.at[slots[i]], outs[i].at[0:GC, :]) for i in range(2)], sems)


def init_kernel(seg, own, lft, rgt, init_out):
    def load_state(k, block_of):
        for b in range(GC // 128):
            init_out[k, :, 128 * b : 128 * (b + 1)] = block_of(b).T

    @pl.loop(0, SLOTS)
    def _(k):
        source = seg[8 + k]

        @pl.when(source < SLOTS)
        def _():
            load_state(k, lambda b: own[jnp.minimum(source, SLOTS - 1), 128 * b : 128 * (b + 1), :])

        @pl.when(source == SLOTS)
        def _():
            load_state(k, lambda b: lft[128 * b : 128 * (b + 1), :])

        @pl.when(source == SLOTS + 1)
        def _():
            load_state(k, lambda b: rgt[128 * b : 128 * (b + 1), :])


def source_of(here, d):
    return (here[0] + (TENSOR - d)) % TENSOR


def prep_kernel(
    seg,
    here,
    *rest,
):
    prep_body(seg, here, rest[:TENSOR], *rest[TENSOR:])


def prep_body(
    seg,
    here,
    blocks,
    conv_state,
    param,
    rate,
    bias,
    b_t_out,
    c_out,
    mix_out,
    col_out,
    row_out,
    dec_out,
    last_out,
    bc_rows,
    dt_rows,
    b_rows,
    terms,
    sems,
):
    copies = []
    for d in range(TENSOR):
        source = source_of(here, d)
        rows = pl.ds(pl.multiple_of(source * SRC_ROWS, SRC_ROWS), SRC_ROWS)
        for i in range(BC_TILES):
            part = blocks[d].at[BC_ROW + SRC_ROWS * i : BC_ROW + SRC_ROWS * (i + 1), :]
            copies.append((part, bc_rows.at[rows, LANES * i : LANES * (i + 1)]))
        copies.append((blocks[d].at[DT_ROW:BLOCK_ROWS, :], dt_rows.at[source]))
    copy_all(copies, sems)
    every = slice(0, 2 * STATE)
    last = last_rows(bc_rows, every, seg)
    last_out[...] = last
    terms[...] = jnp.zeros_like(terms)
    store_terms(terms, every, boundary_terms(last, conv_state[...], param, every))
    targets = boundary_targets((1, 128), 1, seg)

    @pl.loop(0, ROWS // 64)
    def _(i):
        r0 = pl.multiple_of(i * 64, 64)
        value = conv_rows(bc_rows, r0, 64, every, param, terms, targets).astype(BF16)
        b_rows[pl.ds(r0, 64), :] = value[:, 0:STATE]
        c_out[pl.ds(r0, 64), :] = value[:, STATE:]

    dec_sum = jnp.zeros((GH, 128), F32)
    for c in range(CHUNKS):
        b_t = b_rows[Q * c : Q * (c + 1), :].astype(F32).T.astype(BF16)
        b_t_out[c] = b_t
        seg_col = segment_of(iota((Q, 1), 0) + Q * c, seg)
        seg_row = segment_of(iota((1, Q), 1) + Q * c, seg)
        same = seg_col == seg_row
        row_id, col_id = iota((Q, Q), 0), iota((Q, Q), 1)
        mix = mm(c_out[Q * c : Q * (c + 1), :], b_t)
        mix_out[c] = jnp.where(same & (col_id <= row_id), mix, 0.0)
        up_to = jnp.where(same & (row_id <= col_id), 1.0, 0.0).astype(BF16)
        after = jnp.where(same & (row_id > col_id), 1.0, 0.0).astype(BF16)
        raw = jnp.concatenate(
            [dt_rows[s, :, 0:SRC_ROWS] for s in (2 * c, 2 * c + 1)], axis=1
        ).astype(F32) + bias[...]
        step = jnp.maximum(raw, 0.0) + jnp.log1p(jnp.exp(-jnp.abs(raw)))
        log_decay = step * rate[...] * (-LOG2E)
        parts = jnp.concatenate(split3(log_decay), axis=0)

        def summed(mask):
            three = mm(parts, mask)
            return three[0:GH] + three[GH : 2 * GH] + three[2 * GH : 3 * GH]

        running = summed(up_to)
        rest = summed(after)
        row_out[c] = running - jnp.log2(step)
        stack = jnp.concatenate(
            [running, jnp.exp2(running), jnp.exp2(rest) * step, jnp.zeros((80, Q), F32)], axis=0
        )
        col_out[c] = stack.T
        pair = jnp.where(seg_col + SLOTS * c == iota((Q, 128), 1), 1.0, 0.0).astype(BF16)
        dec_sum = dec_sum + summed(pair)
    decay = jnp.concatenate([jnp.exp2(dec_sum), jnp.zeros((128 - GH, 128), F32)], axis=0).T[0:16]
    spread = jnp.where(iota((128, GC), 0) == iota((128, GC), 1) // HEADDIM, 1.0, 0.0).astype(BF16)
    dec_hi, dec_lo = split2(decay)
    dec_out[...] = mm(dec_hi, spread) + mm(dec_lo, spread)


def main_kernel(seg, here, *rest):
    main_body(seg, here, rest[:TENSOR], *rest[TENSOR:])


def main_body(
    seg,
    here,
    blocks,
    conv_state,
    param,
    skip,
    b_t_in,
    c_in,
    mix_in,
    col_in,
    row_in,
    dec_in,
    init_in,
    last_bc,
    y_out,
    own_out,
    lft_out,
    rgt_out,
    last_out,
    terms,
    x_conv,
    x_weighted,
    state,
    inter,
    spread_e,
    spread_w,
    x_in,
    tail,
    sems,
    y_stage,
    y_sems,
):
    def store(c):
        rows = pl.ds(pl.multiple_of(c * Q, Q), Q)
        return pltpu.make_async_copy(y_stage.at[rows, :], y_out.at[rows, :], y_sems.at[c])

    copies = []
    for d in range(TENSOR):
        rows = pl.ds(pl.multiple_of(source_of(here, d) * SRC_ROWS, SRC_ROWS), SRC_ROWS)
        for i in range(TILES):
            part = blocks[d].at[SRC_ROWS * i : SRC_ROWS * (i + 1), :]
            copies.append((part, x_in.at[rows, LANES * i : LANES * (i + 1)]))
    copy_all(copies, sems)
    terms[...] = jnp.zeros_like(terms)
    targets = boundary_targets((1, 128), 1, seg)
    for lt in range(GC // 256):
        lanes = slice(256 * lt, 256 * (lt + 1))
        last = last_rows(x_in, lanes, seg)
        last_out[:, lanes] = last
        store_terms(terms, lanes, boundary_terms(last, conv_state[:, lanes], param, lanes))
        row_id = iota((256, 256), 0) % 128
        head_id = (iota((256, 256), 1) + 256 * lt) // HEADDIM
        spread_e[:, lanes] = jnp.where(row_id - GH == head_id, 1.0, 0.0).astype(BF16)
        spread_w[:, lanes] = jnp.where(row_id - 2 * GH == head_id, 1.0, 0.0).astype(BF16)

    @pl.loop(0, ROWS // 64)
    def _(i):
        r0 = pl.multiple_of(i * 64, 64)
        for lt in range(GC // 256):
            lanes = slice(256 * lt, 256 * (lt + 1))
            value = conv_rows(x_in, r0, 64, lanes, param, terms, targets)
            x_conv[pl.ds(r0, 64), lanes] = value.astype(BF16)

    @pl.loop(0, SLOTS)
    def _(k):
        state[k] = init_in[k]

    @pl.loop(0, CHUNKS)
    def _(c):
        r0 = pl.multiple_of(c * Q, Q)
        rows = pl.ds(r0, Q)
        col = col_in[c]
        col_hi, col_lo = split2(col)
        col_two = jnp.concatenate([col_hi, col_lo], axis=1)
        for lt in range(GC // 256):
            lanes = slice(256 * lt, 256 * (lt + 1))
            weight = mm(col_two, spread_w[:, lanes])
            x_weighted[:, lanes] = (x_conv[rows, lanes].astype(F32) * weight).astype(BF16)
            inter[:, lanes] = jnp.zeros((Q, 256), F32)

        @pl.loop(0, SLOTS)
        def _(k):
            first, end = seg[k], seg[4 + k]

            @pl.when((first < r0 + Q) & (end > r0))
            def _():
                row_id = iota((Q, STATE), 0) + r0
                c_part = jnp.where(
                    (row_id >= first) & (row_id < end), c_in[rows, :].astype(F32), 0.0
                ).astype(BF16)
                c_two = jnp.concatenate([c_part, c_part], axis=1)
                col_id = iota((STATE, Q), 1) + r0
                b_part = jnp.where(
                    (col_id >= first) & (col_id < end), b_t_in[c].astype(F32), 0.0
                ).astype(BF16)
                decay = dec_in[pl.ds(c * SLOTS + k, 1), :]
                for lt in range(GC // 256):
                    lanes = slice(256 * lt, 256 * (lt + 1))
                    old = state[k, :, lanes]
                    both = jnp.concatenate(split2(old), axis=0)
                    inter[:, lanes] += mm(c_two, both)
                    state[k, :, lanes] = old * decay[:, lanes] + mm(b_part, x_weighted[:, lanes])

        low_half = iota((Q, 128), 1) < HEADDIM
        for lt in range(GC // 256):
            lanes = slice(256 * lt, 256 * (lt + 1))
            scale = mm(col_two, spread_e[:, lanes])
            inter[:, lanes] = inter[:, lanes] * scale + x_conv[rows, lanes].astype(F32) * skip[
                0:1, lanes
            ]
        for hp in range(GH // 2):
            lanes = slice(128 * hp, 128 * (hp + 1))
            x_pair = x_conv[rows, lanes].astype(F32)
            x_low = jnp.where(low_half, x_pair, 0.0).astype(BF16)
            x_high = jnp.where(low_half, 0.0, x_pair).astype(BF16)
            for half in range(2):
                depth = 128 * (half + 1)
                part = slice(128 * half, 128 * (half + 1))
                mix = mix_in[c, part, 0:depth]
                total = inter[part, lanes]
                for h, x_one in ((2 * hp, x_low), (2 * hp + 1, x_high)):
                    spread = col[part, h : h + 1] - row_in[c, h : h + 1, 0:depth]
                    scores = (jnp.exp2(jnp.minimum(spread, 126.0)) * mix).astype(BF16)
                    total = total + mm(scores, x_one[0:depth])
                y_stage[pl.ds(r0 + 128 * half, 128), lanes] = total
        store(c).start()

    def send_back(k, out):
        for b in range(GC // 128):
            part = slice(128 * b, 128 * (b + 1))
            out[part, :] = state[k, :, part].T.astype(BF16)
        lines = (GC + 2 * STATE) // 128
        tail[...] = jnp.zeros_like(tail)
        for j in range(3):
            row = pl.ds(3 * k + j, 1)
            line = jnp.concatenate([last_out[row, :], last_bc[row, :]], axis=1)
            for b in range(lines):
                place = slice(j * lines + b, j * lines + b + 1)
                tail[place, :] = line[:, 128 * b : 128 * (b + 1)]
        out[GC:MOVER_ROWS, :] = tail[...].astype(BF16)

    @pl.loop(0, SLOTS)
    def _(k):
        source = seg[8 + k]

        @pl.when(source < SLOTS)
        def _():
            for b in range(GC // 128):
                part = slice(128 * b, 128 * (b + 1))
                own_out[jnp.minimum(source, SLOTS - 1), part, :] = state[k, :, part].T

        @pl.when(source == SLOTS)
        def _():
            send_back(k, lft_out)

        @pl.when(source == SLOTS + 1)
        def _():
            send_back(k, rgt_out)

    @pl.loop(0, CHUNKS)
    def _(c):
        store(c).wait()


def gate_kernel(y_in, z_in, gain, out, y_stage, stage, load_sems, sems):
    def rows_of(i):
        return pl.ds(pl.multiple_of(i * GATE_ROWS, GATE_ROWS), GATE_ROWS)

    def load(i):
        return pltpu.make_async_copy(
            y_in.at[rows_of(i), :], y_stage.at[rows_of(i), :], load_sems.at[i]
        )

    def store(i):
        return pltpu.make_async_copy(stage.at[rows_of(i), :], out.at[rows_of(i), :], sems.at[i])

    for i in range(ROWS // GATE_ROWS):
        load(i).start()

    @pl.loop(0, ROWS // GATE_ROWS)
    def _(i):
        load(i).wait()
        for part in range(GATE_ROWS // 16):
            rows = pl.ds(pl.multiple_of(i * GATE_ROWS + 16 * part, 16), 16)
            gated = y_stage[rows, :] * silu(z_in[rows, :].astype(F32))
            mean = jnp.sum(gated * gated, axis=1, keepdims=True) * (1.0 / GC)
            stage[rows, :] = (gated * lax.rsqrt(mean + EPSILON) * gain[...]).astype(BF16)
        store(i).start()

    @pl.loop(0, ROWS // GATE_ROWS)
    def _(i):
        store(i).wait()


VMEM = pl.BlockSpec(memory_space=pltpu.VMEM)
SMEM = pl.BlockSpec(memory_space=pltpu.SMEM)
ANY = pl.BlockSpec(memory_space=pl.ANY)
HBM = pl.BlockSpec(memory_space=pltpu.HBM)


def in_hbm(value):
    return pltpu.with_memory_space_constraint(value, pltpu.HBM)


def params(mib):
    return pltpu.CompilerParams(vmem_limit_bytes=mib * MIB)


def pack(offsets, here, x_in, bc_in, dt_in):
    count = len(offsets)
    blocks = pl.pallas_call(
        functools.partial(pack_kernel, offsets),
        out_shape=(pltpu.HBM((BLOCK_ROWS, LANES), BF16),) * count,
        in_specs=[SMEM, HBM, HBM, HBM],
        out_specs=(HBM,) * count,
        scratch_shapes=[
            pltpu.VMEM((count, BLOCK_ROWS, LANES), BF16),
            pltpu.VMEM((SRC_ROWS, HEADS), BF16),
            pltpu.VMEM((HEADS, SRC_ROWS), BF16),
            pltpu.SemaphoreType.DMA((count * (TILES + BC_TILES),)),
            pltpu.SemaphoreType.DMA((count,)),
            pltpu.SemaphoreType.DMA,
        ],
        compiler_params=params(8),
        name="pack",
    )(here, in_hbm(x_in), in_hbm(bc_in), in_hbm(dt_in))
    return dict(zip(offsets, blocks))


def movers(slots, own, small):
    return pl.pallas_call(
        mover_kernel,
        out_shape=(jax.ShapeDtypeStruct((MOVER_ROWS, STATE), F32),) * 2,
        in_specs=[SMEM, HBM, VMEM],
        out_specs=(VMEM,) * 2,
        scratch_shapes=[pltpu.SemaphoreType.DMA((2,))],
        compiler_params=params(8),
        name="movers",
    )(slots, in_hbm(own), small)


def initial(seg, own, lft, rgt):
    return pl.pallas_call(
        init_kernel,
        out_shape=jax.ShapeDtypeStruct((SLOTS, STATE, GC), F32),
        in_specs=[SMEM] + [VMEM] * 3,
        out_specs=VMEM,
        compiler_params=params(8),
        cost_estimate=pl.CostEstimate(
            flops=2_000_000_000, bytes_accessed=4 * MIB, transcendentals=0
        ),
        name="initial",
    )(seg, own, lft, rgt)


def prep(seg, here, blocks, conv_state, param, rate, bias):
    return pl.pallas_call(
        prep_kernel,
        out_shape=(
            jax.ShapeDtypeStruct((CHUNKS, STATE, Q), BF16),
            jax.ShapeDtypeStruct((ROWS, STATE), BF16),
            jax.ShapeDtypeStruct((CHUNKS, Q, Q), F32),
            jax.ShapeDtypeStruct((CHUNKS, Q, 128), F32),
            jax.ShapeDtypeStruct((CHUNKS, GH, Q), F32),
            jax.ShapeDtypeStruct((16, GC), F32),
            jax.ShapeDtypeStruct((16, 2 * STATE), F32),
        ),
        in_specs=[SMEM, SMEM] + [ANY] * TENSOR + [VMEM] * 4,
        out_specs=(VMEM,) * 7,
        scratch_shapes=[
            pltpu.VMEM((ROWS, 2 * STATE), BF16),
            pltpu.VMEM((TENSOR, GH, LANES), BF16),
            pltpu.VMEM((ROWS, STATE), BF16),
            pltpu.VMEM((128, 2 * STATE), BF16),
            pltpu.SemaphoreType.DMA(((BC_TILES + 1) * TENSOR,)),
        ],
        compiler_params=params(8),
        cost_estimate=pl.CostEstimate(
            flops=6_000_000_000, bytes_accessed=8 * MIB, transcendentals=500_000
        ),
        name="prep",
    )(seg, here, *blocks, conv_state, param, rate, bias)


def scan(seg, here, blocks, conv_state, param, skip, prepared, init):
    b_t, c_rows, mix, col, row, dec, last_bc = prepared
    return pl.pallas_call(
        main_kernel,
        out_shape=(
            pltpu.HBM((ROWS, GC), F32),
            jax.ShapeDtypeStruct((SLOTS, GC, STATE), F32),
            jax.ShapeDtypeStruct((MOVER_ROWS, STATE), BF16),
            jax.ShapeDtypeStruct((MOVER_ROWS, STATE), BF16),
            jax.ShapeDtypeStruct((16, GC), F32),
        ),
        in_specs=[SMEM, SMEM] + [ANY] * TENSOR + [VMEM] * 11,
        out_specs=(HBM,) + (VMEM,) * 4,
        scratch_shapes=[
            pltpu.VMEM((128, GC), BF16),
            pltpu.VMEM((ROWS, GC), BF16),
            pltpu.VMEM((Q, GC), BF16),
            pltpu.VMEM((SLOTS, STATE, GC), F32),
            pltpu.VMEM((Q, GC), F32),
            pltpu.VMEM((256, GC), BF16),
            pltpu.VMEM((256, GC), BF16),
            pltpu.VMEM((ROWS, GC), BF16),
            pltpu.VMEM((32, STATE), F32),
            pltpu.SemaphoreType.DMA((TENSOR * TILES,)),
            pltpu.VMEM((ROWS, GC), F32),
            pltpu.SemaphoreType.DMA((CHUNKS,)),
        ],
        compiler_params=params(20),
        cost_estimate=pl.CostEstimate(
            flops=20_000_000_000, bytes_accessed=16 * MIB, transcendentals=5_000_000
        ),
        name="scan",
    )(
        seg, here, *blocks, conv_state, param, skip, b_t, c_rows, mix, col, row, dec, init, last_bc
    )


def gate(y, z_rows, gain):
    return pl.pallas_call(
        gate_kernel,
        out_shape=jax.ShapeDtypeStruct((ROWS, GC), BF16),
        in_specs=[HBM, VMEM, VMEM],
        out_specs=ANY,
        scratch_shapes=[
            pltpu.VMEM((ROWS, GC), F32),
            pltpu.VMEM((ROWS, GC), BF16),
            pltpu.SemaphoreType.DMA((ROWS // GATE_ROWS,)),
            pltpu.SemaphoreType.DMA((ROWS // GATE_ROWS,)),
        ],
        compiler_params=params(12),
        cost_estimate=pl.CostEstimate(
            flops=20_000_000, bytes_accessed=8 * MIB, transcendentals=1_000_000
        ),
        name="gate",
    )(in_hbm(y), z_rows, gain)


def shifted(value, steps):
    count = lax.axis_size("dp")
    pairs = [(source, (source + steps) % count) for source in range(count)]
    return lax.ppermute(value, "dp", pairs)


def rotated(value, steps):
    count = lax.axis_size("tensor")
    pairs = [(source, (source + steps) % count) for source in range(count)]
    return lax.ppermute(value, "tensor", pairs)


def after(value, *earlier):
    if not earlier:
        return value
    return lax.optimization_barrier((value, *earlier))[0]


def plan(lengths, prefill_owner, row_start, me, left, right):
    ids = jnp.arange(prefill_owner.shape[0], dtype=jnp.int32)
    mine = prefill_owner == me
    home = ids // SLOTS
    code = jnp.where(home == me, ids % SLOTS, jnp.where(home == left, SLOTS, SLOTS + 1))
    before = mine[None, :] & (row_start[None, :] < row_start[:, None])
    rank = jnp.sum(before.astype(jnp.int32), axis=1)
    chosen = mine[None, :] & (rank[None, :] == jnp.arange(SLOTS, dtype=jnp.int32)[:, None])

    def pick(values):
        return jnp.sum(jnp.where(chosen, values[None, :], 0), axis=1)

    starts = pick(row_start)
    codes = pick(code)
    seg = jnp.concatenate([starts, starts + pick(lengths), codes, jnp.zeros((4,), jnp.int32)])
    slot_right = jnp.sum(jnp.where((home == me) & (prefill_owner == right), ids % SLOTS, 0))
    slot_left = jnp.sum(jnp.where((home == me) & (prefill_owner == left), ids % SLOTS, 0))
    return seg, codes, slot_right, slot_left


def shards(
    x_in,
    z_in,
    bc_in,
    dt_in,
    conv_x_param,
    conv_bc_param,
    decay_rate,
    dt_bias,
    skip_gain,
    norm_gain,
    ssm_state,
    conv_x_state,
    conv_bc_state,
    lengths,
    prefill_owner,
    row_start,
):
    dp_count = lax.axis_size("dp")
    me = lax.axis_index("dp")
    left = (me + dp_count - 1) % dp_count
    right = (me + 1) % dp_count
    here = lax.axis_index("tensor")
    here_ref = here.astype(jnp.int32)[None]
    packed = {}
    turn = here_ref
    for offsets in (FIRST[:1], FIRST[1:], SECOND + THIRD + (0,)):
        packed |= pack(offsets, turn, x_in, bc_in, dt_in)
        turn = after(here_ref, packed[offsets[0]])
    blocks = {0: packed[0]}
    for d in FIRST:
        blocks[d] = rotated(packed[d], d)

    seg, codes, slot_right, slot_left = plan(lengths, prefill_owner, row_start, me, left, right)

    own = ssm_state.reshape(SLOTS, GC, STATE)
    conv = jnp.concatenate([conv_x_state, conv_bc_state], axis=2)
    width = conv.shape[2]
    lines = 3 * width // STATE

    def small_mover(slot):
        small = lax.dynamic_index_in_dim(conv, slot, 0, keepdims=False).reshape(lines, STATE)
        return jnp.concatenate([small, jnp.zeros((2, STATE), F32)], axis=0)

    move_right, move_left = movers(
        after(jnp.stack([slot_right, slot_left]).astype(jnp.int32), packed[0]),
        own,
        jnp.stack([small_mover(slot_right), small_mover(slot_left)]),
    )
    from_left = shifted(move_right, 1)
    from_right = shifted(move_left, -1)
    for d in SECOND:
        blocks[d] = rotated(after(packed[d], from_left, from_right), d)

    def small_of(packed):
        return packed[GC : GC + lines].reshape(1, 3, width)

    candidates = jnp.concatenate([conv, small_of(from_left), small_of(from_right)], axis=0)
    match = codes[:, None] == jnp.arange(SLOTS + 2, dtype=jnp.int32)[None, :]
    conv_init = jnp.sum(jnp.where(match[:, :, None, None], candidates[None], 0.0), axis=1)
    conv_init = jnp.concatenate([conv_init.reshape(3 * SLOTS, width), jnp.zeros((4, width), F32)])

    z_sent = z_in.reshape(SRC_ROWS, TENSOR, GC).transpose(1, 0, 2)
    init = initial(seg, own, from_left, from_right)
    conv_init, init, z_sent, seg, gain, skip, rate, bias = lax.optimization_barrier(
        (
            conv_init,
            init,
            z_sent,
            seg,
            norm_gain[None, :],
            jnp.repeat(skip_gain, HEADDIM)[None, :],
            decay_rate[:, None],
            dt_bias[:, None],
        )
    )
    for d in THIRD:
        blocks[d] = rotated(after(packed[d], conv_init, z_sent, *[blocks[e] for e in FIRST[1:]]), d)
    z_sent = after(z_sent, *[blocks[e] for e in FIRST])
    z_rows = lax.all_to_all(z_sent, "tensor", split_axis=0, concat_axis=0, tiled=True)
    z_rows = z_rows.reshape(ROWS, GC)

    in_order = [blocks[d] for d in range(TENSOR)]
    prepared = prep(
        seg,
        here_ref,
        in_order,
        conv_init[:, GC:],
        conv_bc_param,
        rate,
        bias,
    )
    y, own_new, back_left, back_right, last_x = scan(
        seg,
        here_ref,
        in_order,
        conv_init[:, :GC],
        conv_x_param,
        skip,
        prepared,
        init,
    )
    returned_right = shifted(back_left, -1)
    returned_left = shifted(back_right, 1)
    last = jnp.concatenate([last_x, prepared[6]], axis=1)[: 3 * SLOTS].reshape(SLOTS, 3, width)

    new_ssm = own_new
    for packed, slot in ((returned_right, slot_right), (returned_left, slot_left)):
        new_ssm = lax.dynamic_update_index_in_dim(new_ssm, packed[:GC].astype(F32), slot, 0)
    slots = jnp.arange(SLOTS, dtype=jnp.int32)
    stay = slots[:, None] == codes[None, :]
    new_conv = jnp.sum(jnp.where(stay[:, :, None, None], last[None], 0.0), axis=1)
    for packed, slot in ((returned_right, slot_right), (returned_left, slot_left)):
        new_conv = jnp.where(
            (slots == slot)[:, None, None], small_of(packed).astype(F32), new_conv
        )
    new_cx, new_cbc = new_conv[:, :, :GC], new_conv[:, :, GC:]

    y, new_ssm, new_cx, new_cbc = lax.optimization_barrier((y, new_ssm, new_cx, new_cbc))
    y_out = gate(y, z_rows, gain)
    return y_out, new_ssm.reshape(ssm_state.shape), new_cx, new_cbc


def solution(mesh):
    in_specs = (
        P(("dp", "tensor"), None),
        P(("dp", "tensor"), None),
        P(("dp", "tensor"), None),
        P(("dp", "tensor"), None),
        P(None, "tensor"),
        P(None, "tensor"),
        P("tensor"),
        P("tensor"),
        P("tensor"),
        P("tensor"),
        P("dp", "tensor", None, None),
        P("dp", None, "tensor"),
        P("dp", None, "tensor"),
        P(),
        P(),
        P(),
    )
    out_specs = (
        P("dp", "tensor"),
        P("dp", "tensor", None, None),
        P("dp", None, "tensor"),
        P("dp", None, "tensor"),
    )
    return jax.shard_map(shards, mesh=mesh, in_specs=in_specs, out_specs=out_specs, check_vma=False)
```

```python
import functools
import math

import jax
import jax.numpy as jnp
from jax import lax
from jax.experimental import pallas as pl
from jax.experimental.pallas import tpu as pltpu
from jax.sharding import PartitionSpec as P

HEADS = 128
HEADDIM = 64
STATE = 128
GROUPS = 8
SLOTS = 4
ROWS = 1024
GH = HEADS // GROUPS
GC = GH * HEADDIM
Q = 256
CHUNKS = ROWS // Q
TENSOR = 8
SRC_ROWS = ROWS // TENSOR
EPSILON = 1e-05
LOG2E = math.log2(math.e)
LANES = 128
TILES = GC // LANES
BC_TILES = 2 * STATE // LANES
BC_ROW = TILES * SRC_ROWS
DT_ROW = BC_ROW + BC_TILES * SRC_ROWS
BLOCK_ROWS = DT_ROW + GH
MOVER_ROWS = GC + 32
GATE_ROWS = 128
ORDER = (4, 3, 5, 2, 6, 1, 7)
FIRST = (4, 3, 5)
SECOND = (2, 6)
THIRD = (1, 7)
MIB = 1 << 20

F32 = jnp.float32
BF16 = jnp.bfloat16


def mm(a, b):
    return jnp.dot(a, b, preferred_element_type=F32)


def iota(shape, dim):
    return lax.broadcasted_iota(jnp.int32, shape, dim)


def silu(v):
    half = v * 0.5
    return half + half * jnp.tanh(half)


def split2(v):
    hi = v.astype(BF16)
    return hi, (v - hi.astype(F32)).astype(BF16)


def split3(v):
    hi = v.astype(BF16)
    rest = v - hi.astype(F32)
    mid = rest.astype(BF16)
    return hi, mid, (rest - mid.astype(F32)).astype(BF16)


def segment_of(row_ids, seg):
    total = jnp.zeros(row_ids.shape, jnp.int32)
    for k in range(1, SLOTS):
        total = total + (row_ids >= seg[k]).astype(jnp.int32)
    return total


def boundary_targets(shape, dim, seg):
    idx = iota(shape, dim) % 16
    target = jnp.full(shape, -1, jnp.int32)
    for s in range(SLOTS):
        for q in range(3):
            target = jnp.where(idx == 3 * s + q, seg[s] + q, target)
    return jnp.where(iota(shape, dim) < 48, target, -1)


def last_rows(x_ref, lanes, seg):
    idx = iota((16, 1), 0)
    target = jnp.full((16, 1), -1, jnp.int32)
    for s in range(SLOTS):
        for q in range(3):
            target = jnp.where(idx == 3 * s + q, seg[4 + s] - 3 + q, target)
    picker = (iota((16, ROWS), 1) == target).astype(F32).astype(BF16)
    return mm(picker, x_ref[0:ROWS, lanes])


def boundary_terms(last, state, param, lanes):
    diff = state - pltpu.roll(last, 3, 0)
    q = iota((16, 1), 0) % 3
    term = param[0:1, lanes] * diff
    term = term + jnp.where(q <= 1, param[1:2, lanes] * pltpu.roll(diff, 15, 0), 0.0)
    term = term + jnp.where(q == 0, param[2:3, lanes] * pltpu.roll(diff, 14, 0), 0.0)
    return split3(term)


def conv_rows(x_ref, r0, count, lanes, param, terms_ref, targets):
    prev = pl.multiple_of(jnp.maximum(r0 - 16, 0), 16)
    halo = x_ref[pl.ds(prev, 16), lanes].astype(F32) * jnp.where(r0 > 0, 1.0, 0.0)
    value = jnp.concatenate([halo, x_ref[pl.ds(r0, count), lanes].astype(F32)], axis=0)
    onehot = (iota((count, 128), 0) + r0 == targets).astype(F32).astype(BF16)
    total = mm(onehot, terms_ref[:, lanes]) + param[4:5, lanes]
    total = total + param[3:4, lanes] * value[16:]
    for lag in (1, 2, 3):
        total = total + param[3 - lag : 4 - lag, lanes] * pltpu.roll(value, lag, 0)[16:]
    return silu(total)


def store_terms(terms_ref, lanes, parts):
    for i, part in enumerate(parts):
        terms_ref[16 * i : 16 * i + 16, lanes] = part


def copy_all(copies, sems):
    started = [
        pltpu.make_async_copy(source, target, sems.at[i])
        for i, (source, target) in enumerate(copies)
    ]
    for copy in started:
        copy.start()
    for copy in started:
        copy.wait()


def pack_kernel(offsets, here, x, bc, dt, *rest):
    count = len(offsets)
    outs, (stage, dt_all, dt_turned, sems, out_sems, dt_sem) = rest[:count], rest[count:]
    direct = count == 1
    parts = list(outs) if direct else [stage.at[n] for n in range(count)]
    dt_load = pltpu.make_async_copy(dt, dt_all, dt_sem)
    dt_load.start()
    loads = []
    for n, d in enumerate(offsets):
        to = (here[0] + d) % TENSOR
        sources = []
        for i in range(TILES):
            lanes = pl.ds(pl.multiple_of(to * GC + LANES * i, LANES), LANES)
            sources.append(x.at[:, lanes])
        for i in range(BC_TILES):
            lanes = pl.ds(pl.multiple_of(to * 2 * STATE + LANES * i, LANES), LANES)
            sources.append(bc.at[:, lanes])
        loads.append(
            [
                pltpu.make_async_copy(
                    source,
                    parts[n].at[SRC_ROWS * i : SRC_ROWS * (i + 1), :],
                    sems.at[n * (TILES + BC_TILES) + i],
                )
                for i, source in enumerate(sources)
            ]
        )
        for copy in loads[-1]:
            copy.start()
    dt_load.wait()
    dt_turned[...] = dt_all[...].astype(F32).T.astype(BF16)
    stores = []
    for n, d in enumerate(offsets):
        to = (here[0] + d) % TENSOR
        heads = pl.ds(pl.multiple_of(to * GH, GH), GH)
        parts[n][DT_ROW:BLOCK_ROWS, :] = dt_turned[heads, :]
        for copy in loads[n]:
            copy.wait()
        if not direct:
            stores.append(pltpu.make_async_copy(parts[n], outs[n], out_sems.at[n]))
            stores[-1].start()
    for copy in stores:
        copy.wait()


def mover_kernel(slots, own, small, right_out, left_out, sems):
    outs = (right_out, left_out)
    for i in range(2):
        outs[i][GC:MOVER_ROWS, :] = small[i]
    copy_all([(own.at[slots[i]], outs[i].at[0:GC, :]) for i in range(2)], sems)


def init_kernel(seg, own, lft, rgt, init_out):
    def load_state(k, block_of):
        for b in range(GC // 128):
            init_out[k, :, 128 * b : 128 * (b + 1)] = block_of(b).T

    @pl.loop(0, SLOTS)
    def _(k):
        source = seg[8 + k]

        @pl.when(source < SLOTS)
        def _():
            load_state(k, lambda b: own[jnp.minimum(source, SLOTS - 1), 128 * b : 128 * (b + 1), :])

        @pl.when(source == SLOTS)
        def _():
            load_state(k, lambda b: lft[128 * b : 128 * (b + 1), :])

        @pl.when(source == SLOTS + 1)
        def _():
            load_state(k, lambda b: rgt[128 * b : 128 * (b + 1), :])


def source_of(here, d):
    return (here[0] + (TENSOR - d)) % TENSOR


def prep_kernel(
    seg,
    here,
    *rest,
):
    prep_body(seg, here, rest[:TENSOR], *rest[TENSOR:])


def prep_body(
    seg,
    here,
    blocks,
    conv_state,
    param,
    rate,
    bias,
    b_t_out,
    c_out,
    mix_out,
    col_out,
    row_out,
    dec_out,
    last_out,
    bc_rows,
    dt_rows,
    b_rows,
    terms,
    sems,
):
    copies = []
    for d in range(TENSOR):
        source = source_of(here, d)
        rows = pl.ds(pl.multiple_of(source * SRC_ROWS, SRC_ROWS), SRC_ROWS)
        for i in range(BC_TILES):
            part = blocks[d].at[BC_ROW + SRC_ROWS * i : BC_ROW + SRC_ROWS * (i + 1), :]
            copies.append((part, bc_rows.at[rows, LANES * i : LANES * (i + 1)]))
        copies.append((blocks[d].at[DT_ROW:BLOCK_ROWS, :], dt_rows.at[source]))
    copy_all(copies, sems)
    every = slice(0, 2 * STATE)
    last = last_rows(bc_rows, every, seg)
    last_out[...] = last
    terms[...] = jnp.zeros_like(terms)
    store_terms(terms, every, boundary_terms(last, conv_state[...], param, every))
    targets = boundary_targets((1, 128), 1, seg)

    @pl.loop(0, ROWS // 64)
    def _(i):
        r0 = pl.multiple_of(i * 64, 64)
        value = conv_rows(bc_rows, r0, 64, every, param, terms, targets).astype(BF16)
        b_rows[pl.ds(r0, 64), :] = value[:, 0:STATE]
        c_out[pl.ds(r0, 64), :] = value[:, STATE:]

    dec_sum = jnp.zeros((GH, 128), F32)
    for c in range(CHUNKS):
        b_t = b_rows[Q * c : Q * (c + 1), :].astype(F32).T.astype(BF16)
        b_t_out[c] = b_t
        seg_col = segment_of(iota((Q, 1), 0) + Q * c, seg)
        seg_row = segment_of(iota((1, Q), 1) + Q * c, seg)
        same = seg_col == seg_row
        row_id, col_id = iota((Q, Q), 0), iota((Q, Q), 1)
        mix = mm(c_out[Q * c : Q * (c + 1), :], b_t)
        mix_out[c] = jnp.where(same & (col_id <= row_id), mix, 0.0)
        up_to = jnp.where(same & (row_id <= col_id), 1.0, 0.0).astype(BF16)
        after = jnp.where(same & (row_id > col_id), 1.0, 0.0).astype(BF16)
        raw = jnp.concatenate(
            [dt_rows[s, :, 0:SRC_ROWS] for s in (2 * c, 2 * c + 1)], axis=1
        ).astype(F32) + bias[...]
        step = jnp.maximum(raw, 0.0) + jnp.log1p(jnp.exp(-jnp.abs(raw)))
        log_decay = step * rate[...] * (-LOG2E)
        parts = jnp.concatenate(split3(log_decay), axis=0)

        def summed(mask):
            three = mm(parts, mask)
            return three[0:GH] + three[GH : 2 * GH] + three[2 * GH : 3 * GH]

        running = summed(up_to)
        rest = summed(after)
        row_out[c] = running - jnp.log2(step)
        stack = jnp.concatenate(
            [running, jnp.exp2(running), jnp.exp2(rest) * step, jnp.zeros((80, Q), F32)], axis=0
        )
        col_out[c] = stack.T
        pair = jnp.where(seg_col + SLOTS * c == iota((Q, 128), 1), 1.0, 0.0).astype(BF16)
        dec_sum = dec_sum + summed(pair)
    decay = jnp.concatenate([jnp.exp2(dec_sum), jnp.zeros((128 - GH, 128), F32)], axis=0).T[0:16]
    spread = jnp.where(iota((128, GC), 0) == iota((128, GC), 1) // HEADDIM, 1.0, 0.0).astype(BF16)
    dec_hi, dec_lo = split2(decay)
    dec_out[...] = mm(dec_hi, spread) + mm(dec_lo, spread)


def main_kernel(seg, here, *rest):
    main_body(seg, here, rest[:TENSOR], *rest[TENSOR:])


def main_body(
    seg,
    here,
    blocks,
    conv_state,
    param,
    skip,
    b_t_in,
    c_in,
    mix_in,
    col_in,
    row_in,
    dec_in,
    init_in,
    last_bc,
    y_out,
    own_out,
    lft_out,
    rgt_out,
    last_out,
    terms,
    x_conv,
    x_weighted,
    state,
    inter,
    spread_e,
    spread_w,
    x_in,
    tail,
    sems,
    y_stage,
    y_sems,
):
    def store(c):
        rows = pl.ds(pl.multiple_of(c * Q, Q), Q)
        return pltpu.make_async_copy(y_stage.at[rows, :], y_out.at[rows, :], y_sems.at[c])

    copies = []
    for d in range(TENSOR):
        rows = pl.ds(pl.multiple_of(source_of(here, d) * SRC_ROWS, SRC_ROWS), SRC_ROWS)
        for i in range(TILES):
            part = blocks[d].at[SRC_ROWS * i : SRC_ROWS * (i + 1), :]
            copies.append((part, x_in.at[rows, LANES * i : LANES * (i + 1)]))
    copy_all(copies, sems)
    terms[...] = jnp.zeros_like(terms)
    targets = boundary_targets((1, 128), 1, seg)
    for lt in range(GC // 256):
        lanes = slice(256 * lt, 256 * (lt + 1))
        last = last_rows(x_in, lanes, seg)
        last_out[:, lanes] = last
        store_terms(terms, lanes, boundary_terms(last, conv_state[:, lanes], param, lanes))
        row_id = iota((256, 256), 0) % 128
        head_id = (iota((256, 256), 1) + 256 * lt) // HEADDIM
        spread_e[:, lanes] = jnp.where(row_id - GH == head_id, 1.0, 0.0).astype(BF16)
        spread_w[:, lanes] = jnp.where(row_id - 2 * GH == head_id, 1.0, 0.0).astype(BF16)

    @pl.loop(0, ROWS // 64)
    def _(i):
        r0 = pl.multiple_of(i * 64, 64)
        for lt in range(GC // 256):
            lanes = slice(256 * lt, 256 * (lt + 1))
            value = conv_rows(x_in, r0, 64, lanes, param, terms, targets)
            x_conv[pl.ds(r0, 64), lanes] = value.astype(BF16)

    @pl.loop(0, SLOTS)
    def _(k):
        state[k] = init_in[k]

    @pl.loop(0, CHUNKS)
    def _(c):
        r0 = pl.multiple_of(c * Q, Q)
        rows = pl.ds(r0, Q)
        col = col_in[c]
        col_hi, col_lo = split2(col)
        col_two = jnp.concatenate([col_hi, col_lo], axis=1)
        for lt in range(GC // 256):
            lanes = slice(256 * lt, 256 * (lt + 1))
            weight = mm(col_two, spread_w[:, lanes])
            x_weighted[:, lanes] = (x_conv[rows, lanes].astype(F32) * weight).astype(BF16)
            inter[:, lanes] = jnp.zeros((Q, 256), F32)

        @pl.loop(0, SLOTS)
        def _(k):
            first, end = seg[k], seg[4 + k]

            @pl.when((first < r0 + Q) & (end > r0))
            def _():
                row_id = iota((Q, STATE), 0) + r0
                c_part = jnp.where(
                    (row_id >= first) & (row_id < end), c_in[rows, :].astype(F32), 0.0
                ).astype(BF16)
                c_two = jnp.concatenate([c_part, c_part], axis=1)
                col_id = iota((STATE, Q), 1) + r0
                b_part = jnp.where(
                    (col_id >= first) & (col_id < end), b_t_in[c].astype(F32), 0.0
                ).astype(BF16)
                decay = dec_in[pl.ds(c * SLOTS + k, 1), :]
                for lt in range(GC // 256):
                    lanes = slice(256 * lt, 256 * (lt + 1))
                    old = state[k, :, lanes]
                    both = jnp.concatenate(split2(old), axis=0)
                    inter[:, lanes] += mm(c_two, both)
                    state[k, :, lanes] = old * decay[:, lanes] + mm(b_part, x_weighted[:, lanes])

        low_half = iota((Q, 128), 1) < HEADDIM
        for lt in range(GC // 256):
            lanes = slice(256 * lt, 256 * (lt + 1))
            scale = mm(col_two, spread_e[:, lanes])
            inter[:, lanes] = inter[:, lanes] * scale + x_conv[rows, lanes].astype(F32) * skip[
                0:1, lanes
            ]
        for hp in range(GH // 2):
            lanes = slice(128 * hp, 128 * (hp + 1))
            x_pair = x_conv[rows, lanes].astype(F32)
            x_low = jnp.where(low_half, x_pair, 0.0).astype(BF16)
            x_high = jnp.where(low_half, 0.0, x_pair).astype(BF16)
            for half in range(2):
                depth = 128 * (half + 1)
                part = slice(128 * half, 128 * (half + 1))
                mix = mix_in[c, part, 0:depth]
                total = inter[part, lanes]
                for h, x_one in ((2 * hp, x_low), (2 * hp + 1, x_high)):
                    spread = col[part, h : h + 1] - row_in[c, h : h + 1, 0:depth]
                    scores = (jnp.exp2(jnp.minimum(spread, 126.0)) * mix).astype(BF16)
                    total = total + mm(scores, x_one[0:depth])
                y_stage[pl.ds(r0 + 128 * half, 128), lanes] = total
        store(c).start()

    def send_back(k, out):
        for b in range(GC // 128):
            part = slice(128 * b, 128 * (b + 1))
            out[part, :] = state[k, :, part].T.astype(BF16)
        lines = (GC + 2 * STATE) // 128
        tail[...] = jnp.zeros_like(tail)
        for j in range(3):
            row = pl.ds(3 * k + j, 1)
            line = jnp.concatenate([last_out[row, :], last_bc[row, :]], axis=1)
            for b in range(lines):
                place = slice(j * lines + b, j * lines + b + 1)
                tail[place, :] = line[:, 128 * b : 128 * (b + 1)]
        out[GC:MOVER_ROWS, :] = tail[...].astype(BF16)

    @pl.loop(0, SLOTS)
    def _(k):
        source = seg[8 + k]

        @pl.when(source < SLOTS)
        def _():
            for b in range(GC // 128):
                part = slice(128 * b, 128 * (b + 1))
                own_out[jnp.minimum(source, SLOTS - 1), part, :] = state[k, :, part].T

        @pl.when(source == SLOTS)
        def _():
            send_back(k, lft_out)

        @pl.when(source == SLOTS + 1)
        def _():
            send_back(k, rgt_out)

    @pl.loop(0, CHUNKS)
    def _(c):
        store(c).wait()


def gate_kernel(y_in, z_in, gain, out, y_stage, stage, load_sems, sems):
    def rows_of(i):
        return pl.ds(pl.multiple_of(i * GATE_ROWS, GATE_ROWS), GATE_ROWS)

    def load(i):
        return pltpu.make_async_copy(
            y_in.at[rows_of(i), :], y_stage.at[rows_of(i), :], load_sems.at[i]
        )

    def store(i):
        return pltpu.make_async_copy(stage.at[rows_of(i), :], out.at[rows_of(i), :], sems.at[i])

    for i in range(ROWS // GATE_ROWS):
        load(i).start()

    @pl.loop(0, ROWS // GATE_ROWS)
    def _(i):
        load(i).wait()
        for part in range(GATE_ROWS // 16):
            rows = pl.ds(pl.multiple_of(i * GATE_ROWS + 16 * part, 16), 16)
            gated = y_stage[rows, :] * silu(z_in[rows, :].astype(F32))
            mean = jnp.sum(gated * gated, axis=1, keepdims=True) * (1.0 / GC)
            stage[rows, :] = (gated * lax.rsqrt(mean + EPSILON) * gain[...]).astype(BF16)
        store(i).start()

    @pl.loop(0, ROWS // GATE_ROWS)
    def _(i):
        store(i).wait()


VMEM = pl.BlockSpec(memory_space=pltpu.VMEM)
SMEM = pl.BlockSpec(memory_space=pltpu.SMEM)
ANY = pl.BlockSpec(memory_space=pl.ANY)
HBM = pl.BlockSpec(memory_space=pltpu.HBM)


def in_hbm(value):
    return pltpu.with_memory_space_constraint(value, pltpu.HBM)


def params(mib):
    return pltpu.CompilerParams(vmem_limit_bytes=mib * MIB)


def pack(offsets, here, x_in, bc_in, dt_in):
    count = len(offsets)
    blocks = pl.pallas_call(
        functools.partial(pack_kernel, offsets),
        out_shape=(
            jax.ShapeDtypeStruct((BLOCK_ROWS, LANES), BF16)
            if count == 1
            else pltpu.HBM((BLOCK_ROWS, LANES), BF16),
        )
        * count,
        in_specs=[SMEM, HBM, HBM, HBM],
        out_specs=(VMEM if count == 1 else HBM,) * count,
        scratch_shapes=[
            pltpu.VMEM((count, BLOCK_ROWS, LANES), BF16),
            pltpu.VMEM((SRC_ROWS, HEADS), BF16),
            pltpu.VMEM((HEADS, SRC_ROWS), BF16),
            pltpu.SemaphoreType.DMA((count * (TILES + BC_TILES),)),
            pltpu.SemaphoreType.DMA((count,)),
            pltpu.SemaphoreType.DMA,
        ],
        compiler_params=params(8),
        name="pack",
    )(here, in_hbm(x_in), in_hbm(bc_in), in_hbm(dt_in))
    return dict(zip(offsets, blocks))


def movers(slots, own, small):
    return pl.pallas_call(
        mover_kernel,
        out_shape=(jax.ShapeDtypeStruct((MOVER_ROWS, STATE), F32),) * 2,
        in_specs=[SMEM, HBM, VMEM],
        out_specs=(VMEM,) * 2,
        scratch_shapes=[pltpu.SemaphoreType.DMA((2,))],
        compiler_params=params(8),
        name="movers",
    )(slots, in_hbm(own), small)


def initial(seg, own, lft, rgt):
    return pl.pallas_call(
        init_kernel,
        out_shape=jax.ShapeDtypeStruct((SLOTS, STATE, GC), F32),
        in_specs=[SMEM] + [VMEM] * 3,
        out_specs=VMEM,
        compiler_params=params(8),
        cost_estimate=pl.CostEstimate(
            flops=2_000_000_000, bytes_accessed=4 * MIB, transcendentals=0
        ),
        name="initial",
    )(seg, own, lft, rgt)


def prep(seg, here, blocks, conv_state, param, rate, bias):
    return pl.pallas_call(
        prep_kernel,
        out_shape=(
            jax.ShapeDtypeStruct((CHUNKS, STATE, Q), BF16),
            jax.ShapeDtypeStruct((ROWS, STATE), BF16),
            jax.ShapeDtypeStruct((CHUNKS, Q, Q), F32),
            jax.ShapeDtypeStruct((CHUNKS, Q, 128), F32),
            jax.ShapeDtypeStruct((CHUNKS, GH, Q), F32),
            jax.ShapeDtypeStruct((16, GC), F32),
            jax.ShapeDtypeStruct((16, 2 * STATE), F32),
        ),
        in_specs=[SMEM, SMEM] + [ANY] * TENSOR + [VMEM] * 4,
        out_specs=(VMEM,) * 7,
        scratch_shapes=[
            pltpu.VMEM((ROWS, 2 * STATE), BF16),
            pltpu.VMEM((TENSOR, GH, LANES), BF16),
            pltpu.VMEM((ROWS, STATE), BF16),
            pltpu.VMEM((128, 2 * STATE), BF16),
            pltpu.SemaphoreType.DMA(((BC_TILES + 1) * TENSOR,)),
        ],
        compiler_params=params(8),
        cost_estimate=pl.CostEstimate(
            flops=6_000_000_000, bytes_accessed=8 * MIB, transcendentals=500_000
        ),
        name="prep",
    )(seg, here, *blocks, conv_state, param, rate, bias)


def scan(seg, here, blocks, conv_state, param, skip, prepared, init):
    b_t, c_rows, mix, col, row, dec, last_bc = prepared
    return pl.pallas_call(
        main_kernel,
        out_shape=(
            pltpu.HBM((ROWS, GC), F32),
            jax.ShapeDtypeStruct((SLOTS, GC, STATE), F32),
            jax.ShapeDtypeStruct((MOVER_ROWS, STATE), BF16),
            jax.ShapeDtypeStruct((MOVER_ROWS, STATE), BF16),
            jax.ShapeDtypeStruct((16, GC), F32),
        ),
        in_specs=[SMEM, SMEM] + [ANY] * TENSOR + [VMEM] * 11,
        out_specs=(HBM,) + (VMEM,) * 4,
        scratch_shapes=[
            pltpu.VMEM((128, GC), BF16),
            pltpu.VMEM((ROWS, GC), BF16),
            pltpu.VMEM((Q, GC), BF16),
            pltpu.VMEM((SLOTS, STATE, GC), F32),
            pltpu.VMEM((Q, GC), F32),
            pltpu.VMEM((256, GC), BF16),
            pltpu.VMEM((256, GC), BF16),
            pltpu.VMEM((ROWS, GC), BF16),
            pltpu.VMEM((32, STATE), F32),
            pltpu.SemaphoreType.DMA((TENSOR * TILES,)),
            pltpu.VMEM((ROWS, GC), F32),
            pltpu.SemaphoreType.DMA((CHUNKS,)),
        ],
        compiler_params=params(20),
        cost_estimate=pl.CostEstimate(
            flops=20_000_000_000, bytes_accessed=16 * MIB, transcendentals=5_000_000
        ),
        name="scan",
    )(
        seg, here, *blocks, conv_state, param, skip, b_t, c_rows, mix, col, row, dec, init, last_bc
    )


def gate(y, z_rows, gain):
    return pl.pallas_call(
        gate_kernel,
        out_shape=jax.ShapeDtypeStruct((ROWS, GC), BF16),
        in_specs=[HBM, VMEM, VMEM],
        out_specs=ANY,
        scratch_shapes=[
            pltpu.VMEM((ROWS, GC), F32),
            pltpu.VMEM((ROWS, GC), BF16),
            pltpu.SemaphoreType.DMA((ROWS // GATE_ROWS,)),
            pltpu.SemaphoreType.DMA((ROWS // GATE_ROWS,)),
        ],
        compiler_params=params(12),
        cost_estimate=pl.CostEstimate(
            flops=20_000_000, bytes_accessed=8 * MIB, transcendentals=1_000_000
        ),
        name="gate",
    )(in_hbm(y), z_rows, gain)


def shifted(value, steps):
    count = lax.axis_size("dp")
    pairs = [(source, (source + steps) % count) for source in range(count)]
    return lax.ppermute(value, "dp", pairs)


def rotated(value, steps):
    count = lax.axis_size("tensor")
    pairs = [(source, (source + steps) % count) for source in range(count)]
    return lax.ppermute(value, "tensor", pairs)


def after(value, *earlier):
    if not earlier:
        return value
    return lax.optimization_barrier((value, *earlier))[0]


def plan(lengths, prefill_owner, row_start, me, left, right):
    ids = jnp.arange(prefill_owner.shape[0], dtype=jnp.int32)
    mine = prefill_owner == me
    home = ids // SLOTS
    code = jnp.where(home == me, ids % SLOTS, jnp.where(home == left, SLOTS, SLOTS + 1))
    before = mine[None, :] & (row_start[None, :] < row_start[:, None])
    rank = jnp.sum(before.astype(jnp.int32), axis=1)
    chosen = mine[None, :] & (rank[None, :] == jnp.arange(SLOTS, dtype=jnp.int32)[:, None])

    def pick(values):
        return jnp.sum(jnp.where(chosen, values[None, :], 0), axis=1)

    starts = pick(row_start)
    codes = pick(code)
    seg = jnp.concatenate([starts, starts + pick(lengths), codes, jnp.zeros((4,), jnp.int32)])
    slot_right = jnp.sum(jnp.where((home == me) & (prefill_owner == right), ids % SLOTS, 0))
    slot_left = jnp.sum(jnp.where((home == me) & (prefill_owner == left), ids % SLOTS, 0))
    return seg, codes, slot_right, slot_left


def shards(
    x_in,
    z_in,
    bc_in,
    dt_in,
    conv_x_param,
    conv_bc_param,
    decay_rate,
    dt_bias,
    skip_gain,
    norm_gain,
    ssm_state,
    conv_x_state,
    conv_bc_state,
    lengths,
    prefill_owner,
    row_start,
):
    dp_count = lax.axis_size("dp")
    me = lax.axis_index("dp")
    left = (me + dp_count - 1) % dp_count
    right = (me + 1) % dp_count
    here = lax.axis_index("tensor")
    here_ref = here.astype(jnp.int32)[None]
    packed = {}
    turn = here_ref
    for offsets in (FIRST[:1], FIRST[1:], SECOND + THIRD + (0,)):
        packed |= pack(offsets, turn, x_in, bc_in, dt_in)
        turn = after(here_ref, packed[offsets[0]])
    blocks = {0: packed[0]}
    for d in FIRST:
        blocks[d] = rotated(packed[d], d)

    seg, codes, slot_right, slot_left = plan(lengths, prefill_owner, row_start, me, left, right)

    own = ssm_state.reshape(SLOTS, GC, STATE)
    conv = jnp.concatenate([conv_x_state, conv_bc_state], axis=2)
    width = conv.shape[2]
    lines = 3 * width // STATE

    def small_mover(slot):
        small = lax.dynamic_index_in_dim(conv, slot, 0, keepdims=False).reshape(lines, STATE)
        return jnp.concatenate([small, jnp.zeros((2, STATE), F32)], axis=0)

    move_right, move_left = movers(
        after(jnp.stack([slot_right, slot_left]).astype(jnp.int32), packed[0]),
        own,
        jnp.stack([small_mover(slot_right), small_mover(slot_left)]),
    )
    from_left = shifted(move_right, 1)
    from_right = shifted(move_left, -1)
    for d in SECOND:
        blocks[d] = rotated(after(packed[d], from_left, from_right), d)

    def small_of(packed):
        return packed[GC : GC + lines].reshape(1, 3, width)

    candidates = jnp.concatenate([conv, small_of(from_left), small_of(from_right)], axis=0)
    match = codes[:, None] == jnp.arange(SLOTS + 2, dtype=jnp.int32)[None, :]
    conv_init = jnp.sum(jnp.where(match[:, :, None, None], candidates[None], 0.0), axis=1)
    conv_init = jnp.concatenate([conv_init.reshape(3 * SLOTS, width), jnp.zeros((4, width), F32)])

    z_sent = z_in.reshape(SRC_ROWS, TENSOR, GC).transpose(1, 0, 2)
    init = initial(seg, own, from_left, from_right)
    conv_init, init, z_sent, seg, gain, skip, rate, bias = lax.optimization_barrier(
        (
            conv_init,
            init,
            z_sent,
            seg,
            norm_gain[None, :],
            jnp.repeat(skip_gain, HEADDIM)[None, :],
            decay_rate[:, None],
            dt_bias[:, None],
        )
    )
    for d in THIRD:
        blocks[d] = rotated(after(packed[d], conv_init, z_sent, *[blocks[e] for e in FIRST[1:]]), d)
    z_sent = after(z_sent, *[blocks[e] for e in FIRST])
    z_rows = lax.all_to_all(z_sent, "tensor", split_axis=0, concat_axis=0, tiled=True)
    z_rows = z_rows.reshape(ROWS, GC)

    in_order = [blocks[d] for d in range(TENSOR)]
    prepared = prep(
        seg,
        here_ref,
        in_order,
        conv_init[:, GC:],
        conv_bc_param,
        rate,
        bias,
    )
    y, own_new, back_left, back_right, last_x = scan(
        seg,
        here_ref,
        in_order,
        conv_init[:, :GC],
        conv_x_param,
        skip,
        prepared,
        init,
    )
    returned_right = shifted(back_left, -1)
    returned_left = shifted(back_right, 1)
    last = jnp.concatenate([last_x, prepared[6]], axis=1)[: 3 * SLOTS].reshape(SLOTS, 3, width)

    new_ssm = own_new
    for packed, slot in ((returned_right, slot_right), (returned_left, slot_left)):
        new_ssm = lax.dynamic_update_index_in_dim(new_ssm, packed[:GC].astype(F32), slot, 0)
    slots = jnp.arange(SLOTS, dtype=jnp.int32)
    stay = slots[:, None] == codes[None, :]
    new_conv = jnp.sum(jnp.where(stay[:, :, None, None], last[None], 0.0), axis=1)
    for packed, slot in ((returned_right, slot_right), (returned_left, slot_left)):
        new_conv = jnp.where(
            (slots == slot)[:, None, None], small_of(packed).astype(F32), new_conv
        )
    new_cx, new_cbc = new_conv[:, :, :GC], new_conv[:, :, GC:]

    y, new_ssm, new_cx, new_cbc = lax.optimization_barrier((y, new_ssm, new_cx, new_cbc))
    y_out = gate(y, z_rows, gain)
    return y_out, new_ssm.reshape(ssm_state.shape), new_cx, new_cbc


def solution(mesh):
    in_specs = (
        P(("dp", "tensor"), None),
        P(("dp", "tensor"), None),
        P(("dp", "tensor"), None),
        P(("dp", "tensor"), None),
        P(None, "tensor"),
        P(None, "tensor"),
        P("tensor"),
        P("tensor"),
        P("tensor"),
        P("tensor"),
        P("dp", "tensor", None, None),
        P("dp", None, "tensor"),
        P("dp", None, "tensor"),
        P(),
        P(),
        P(),
    )
    out_specs = (
        P("dp", "tensor"),
        P("dp", "tensor", None, None),
        P("dp", None, "tensor"),
        P("dp", None, "tensor"),
    )
    return jax.shard_map(shards, mesh=mesh, in_specs=in_specs, out_specs=out_specs, check_vma=False)
```

```python
import functools
import math

import jax
import jax.numpy as jnp
from jax import lax
from jax.experimental import pallas as pl
from jax.experimental.pallas import tpu as pltpu
from jax.sharding import PartitionSpec as P

HEADS = 128
HEADDIM = 64
STATE = 128
GROUPS = 8
SLOTS = 4
ROWS = 1024
GH = HEADS // GROUPS
GC = GH * HEADDIM
Q = 256
CHUNKS = ROWS // Q
TENSOR = 8
SRC_ROWS = ROWS // TENSOR
EPSILON = 1e-05
LOG2E = math.log2(math.e)
LANES = 128
TILES = GC // LANES
BC_TILES = 2 * STATE // LANES
BC_ROW = TILES * SRC_ROWS
DT_ROW = BC_ROW + BC_TILES * SRC_ROWS
BLOCK_ROWS = DT_ROW + GH
MOVER_ROWS = GC + 32
GATE_ROWS = 256
ORDER = (4, 3, 5, 2, 6, 1, 7)
FIRST = (4, 3, 5)
SECOND = (2, 6)
THIRD = (1, 7)
MIB = 1 << 20

F32 = jnp.float32
BF16 = jnp.bfloat16


def mm(a, b):
    return jnp.dot(a, b, preferred_element_type=F32)


def iota(shape, dim):
    return lax.broadcasted_iota(jnp.int32, shape, dim)


def silu(v):
    half = v * 0.5
    return half + half * jnp.tanh(half)


def split2(v):
    hi = v.astype(BF16)
    return hi, (v - hi.astype(F32)).astype(BF16)


def split3(v):
    hi = v.astype(BF16)
    rest = v - hi.astype(F32)
    mid = rest.astype(BF16)
    return hi, mid, (rest - mid.astype(F32)).astype(BF16)


def segment_of(row_ids, seg):
    total = jnp.zeros(row_ids.shape, jnp.int32)
    for k in range(1, SLOTS):
        total = total + (row_ids >= seg[k]).astype(jnp.int32)
    return total


def boundary_targets(shape, dim, seg):
    idx = iota(shape, dim) % 16
    target = jnp.full(shape, -1, jnp.int32)
    for s in range(SLOTS):
        for q in range(3):
            target = jnp.where(idx == 3 * s + q, seg[s] + q, target)
    return jnp.where(iota(shape, dim) < 48, target, -1)


def last_rows(x_ref, lanes, seg):
    idx = iota((16, 1), 0)
    target = jnp.full((16, 1), -1, jnp.int32)
    for s in range(SLOTS):
        for q in range(3):
            target = jnp.where(idx == 3 * s + q, seg[4 + s] - 3 + q, target)
    picker = (iota((16, ROWS), 1) == target).astype(F32).astype(BF16)
    return mm(picker, x_ref[0:ROWS, lanes])


def boundary_terms(last, state, param, lanes):
    diff = state - pltpu.roll(last, 3, 0)
    q = iota((16, 1), 0) % 3
    term = param[0:1, lanes] * diff
    term = term + jnp.where(q <= 1, param[1:2, lanes] * pltpu.roll(diff, 15, 0), 0.0)
    term = term + jnp.where(q == 0, param[2:3, lanes] * pltpu.roll(diff, 14, 0), 0.0)
    return split3(term)


def conv_rows(x_ref, r0, count, lanes, param, terms_ref, targets):
    prev = pl.multiple_of(jnp.maximum(r0 - 16, 0), 16)
    halo = x_ref[pl.ds(prev, 16), lanes].astype(F32) * jnp.where(r0 > 0, 1.0, 0.0)
    value = jnp.concatenate([halo, x_ref[pl.ds(r0, count), lanes].astype(F32)], axis=0)
    onehot = (iota((count, 128), 0) + r0 == targets).astype(F32).astype(BF16)
    total = mm(onehot, terms_ref[:, lanes]) + param[4:5, lanes]
    total = total + param[3:4, lanes] * value[16:]
    for lag in (1, 2, 3):
        total = total + param[3 - lag : 4 - lag, lanes] * pltpu.roll(value, lag, 0)[16:]
    return silu(total)


def store_terms(terms_ref, lanes, parts):
    for i, part in enumerate(parts):
        terms_ref[16 * i : 16 * i + 16, lanes] = part


def copy_all(copies, sems, later=()):
    started = [
        pltpu.make_async_copy(source, target, sems.at[i])
        for i, (source, target) in enumerate(copies)
    ]
    for copy in [*started, *later]:
        copy.start()
    for copy in started:
        copy.wait()


def pack_kernel(offsets, here, x, bc, dt, *rest):
    count = len(offsets)
    outs, (stage, dt_all, dt_turned, sems, out_sems, dt_sem) = rest[:count], rest[count:]
    direct = count == 1
    parts = list(outs) if direct else [stage.at[n] for n in range(count)]
    dt_load = pltpu.make_async_copy(dt, dt_all, dt_sem)
    dt_load.start()
    loads = []
    for n, d in enumerate(offsets):
        to = (here[0] + d) % TENSOR
        sources = []
        for i in range(TILES):
            lanes = pl.ds(pl.multiple_of(to * GC + LANES * i, LANES), LANES)
            sources.append(x.at[:, lanes])
        for i in range(BC_TILES):
            lanes = pl.ds(pl.multiple_of(to * 2 * STATE + LANES * i, LANES), LANES)
            sources.append(bc.at[:, lanes])
        loads.append(
            [
                pltpu.make_async_copy(
                    source,
                    parts[n].at[SRC_ROWS * i : SRC_ROWS * (i + 1), :],
                    sems.at[n * (TILES + BC_TILES) + i],
                )
                for i, source in enumerate(sources)
            ]
        )
        for copy in loads[-1]:
            copy.start()
    dt_load.wait()
    dt_turned[...] = dt_all[...].astype(F32).T.astype(BF16)
    stores = []
    for n, d in enumerate(offsets):
        to = (here[0] + d) % TENSOR
        heads = pl.ds(pl.multiple_of(to * GH, GH), GH)
        parts[n][DT_ROW:BLOCK_ROWS, :] = dt_turned[heads, :]
        for copy in loads[n]:
            copy.wait()
        if not direct:
            stores.append(pltpu.make_async_copy(parts[n], outs[n], out_sems.at[n]))
            stores[-1].start()
    for copy in stores:
        copy.wait()


def mover_kernel(slots, own, small, right_out, left_out, sems):
    outs = (right_out, left_out)
    for i in range(2):
        outs[i][GC:MOVER_ROWS, :] = small[i]
    copy_all([(own.at[slots[i]], outs[i].at[0:GC, :]) for i in range(2)], sems)


def init_kernel(seg, own, lft, rgt, init_out):
    def load_state(k, block_of):
        for b in range(GC // 128):
            init_out[k, :, 128 * b : 128 * (b + 1)] = block_of(b).T

    @pl.loop(0, SLOTS)
    def _(k):
        source = seg[8 + k]

        @pl.when(source < SLOTS)
        def _():
            load_state(k, lambda b: own[jnp.minimum(source, SLOTS - 1), 128 * b : 128 * (b + 1), :])

        @pl.when(source == SLOTS)
        def _():
            load_state(k, lambda b: lft[128 * b : 128 * (b + 1), :])

        @pl.when(source == SLOTS + 1)
        def _():
            load_state(k, lambda b: rgt[128 * b : 128 * (b + 1), :])


def source_of(here, d):
    return (here[0] + (TENSOR - d)) % TENSOR


def prep_body(
    seg,
    here,
    blocks,
    conv_state,
    param,
    rate,
    bias,
    b_t_out,
    c_out,
    mix_out,
    col_out,
    row_out,
    dec_out,
    last_out,
    bc_rows,
    dt_rows,
    b_rows,
    terms,
    sems,
    loads,
):
    copies = []
    for d in range(TENSOR):
        source = source_of(here, d)
        rows = pl.ds(pl.multiple_of(source * SRC_ROWS, SRC_ROWS), SRC_ROWS)
        for i in range(BC_TILES):
            part = blocks[d].at[BC_ROW + SRC_ROWS * i : BC_ROW + SRC_ROWS * (i + 1), :]
            copies.append((part, bc_rows.at[rows, LANES * i : LANES * (i + 1)]))
        copies.append((blocks[d].at[DT_ROW:BLOCK_ROWS, :], dt_rows.at[source]))
    copy_all(copies, sems, loads)
    every = slice(0, 2 * STATE)
    last = last_rows(bc_rows, every, seg)
    last_out[...] = last
    terms[...] = jnp.zeros_like(terms)
    store_terms(terms, every, boundary_terms(last, conv_state[...], param, every))
    targets = boundary_targets((1, 128), 1, seg)

    @pl.loop(0, ROWS // 64)
    def _(i):
        r0 = pl.multiple_of(i * 64, 64)
        value = conv_rows(bc_rows, r0, 64, every, param, terms, targets).astype(BF16)
        b_rows[pl.ds(r0, 64), :] = value[:, 0:STATE]
        c_out[pl.ds(r0, 64), :] = value[:, STATE:]

    dec_sum = jnp.zeros((GH, 128), F32)
    for c in range(CHUNKS):
        b_t = b_rows[Q * c : Q * (c + 1), :].astype(F32).T.astype(BF16)
        b_t_out[c] = b_t
        seg_col = segment_of(iota((Q, 1), 0) + Q * c, seg)
        seg_row = segment_of(iota((1, Q), 1) + Q * c, seg)
        same = seg_col == seg_row
        row_id, col_id = iota((Q, Q), 0), iota((Q, Q), 1)
        mix = mm(c_out[Q * c : Q * (c + 1), :], b_t)
        mix_out[c] = jnp.where(same & (col_id <= row_id), mix, 0.0)
        up_to = jnp.where(same & (row_id <= col_id), 1.0, 0.0).astype(BF16)
        after = jnp.where(same & (row_id > col_id), 1.0, 0.0).astype(BF16)
        raw = jnp.concatenate(
            [dt_rows[s, :, 0:SRC_ROWS] for s in (2 * c, 2 * c + 1)], axis=1
        ).astype(F32) + bias[...]
        step = jnp.maximum(raw, 0.0) + jnp.log1p(jnp.exp(-jnp.abs(raw)))
        log_decay = step * rate[...] * (-LOG2E)
        parts = jnp.concatenate(split3(log_decay), axis=0)

        def summed(mask):
            three = mm(parts, mask)
            return three[0:GH] + three[GH : 2 * GH] + three[2 * GH : 3 * GH]

        running = summed(up_to)
        rest = summed(after)
        row_out[c] = running - jnp.log2(step)
        stack = jnp.concatenate(
            [running, jnp.exp2(running), jnp.exp2(rest) * step, jnp.zeros((80, Q), F32)], axis=0
        )
        col_out[c] = stack.T
        pair = jnp.where(seg_col + SLOTS * c == iota((Q, 128), 1), 1.0, 0.0).astype(BF16)
        dec_sum = dec_sum + summed(pair)
    decay = jnp.concatenate([jnp.exp2(dec_sum), jnp.zeros((128 - GH, 128), F32)], axis=0).T[0:16]
    spread = jnp.where(iota((128, GC), 0) == iota((128, GC), 1) // HEADDIM, 1.0, 0.0).astype(BF16)
    dec_hi, dec_lo = split2(decay)
    dec_out[...] = mm(dec_hi, spread) + mm(dec_lo, spread)


def scan_kernel(seg, here, *rest):
    blocks, rest = rest[:TENSOR], rest[TENSOR:]
    conv_x, conv_bc, x_param, skip, bc_param, rate, bias, init = rest[:8]
    y_out, own_out, lft_out, rgt_out, last_x, last_bc = rest[8:14]
    prep_out, prep_scratch, scratch = rest[14:20], rest[20:25], rest[25:]
    x_rows, x_sems = scratch[7], scratch[9]
    loads = [pltpu.make_async_copy(init, scratch[3], x_sems.at[TENSOR * TILES])]
    for d in range(TENSOR):
        rows = pl.ds(pl.multiple_of(source_of(here, d) * SRC_ROWS, SRC_ROWS), SRC_ROWS)
        for i in range(TILES):
            part = blocks[d].at[SRC_ROWS * i : SRC_ROWS * (i + 1), :]
            place = x_rows.at[rows, LANES * i : LANES * (i + 1)]
            loads.append(pltpu.make_async_copy(part, place, x_sems.at[d * TILES + i]))
    prep_body(
        seg, here, blocks, conv_bc, bc_param, rate, bias, *prep_out, last_bc, *prep_scratch, loads
    )
    for copy in loads:
        copy.wait()

    main_body(
        seg, conv_x, x_param, skip, *prep_out, last_bc, y_out, own_out, lft_out, rgt_out,
        last_x, *scratch
    )


def main_body(
    seg,
    conv_state,
    param,
    skip,
    b_t_in,
    c_in,
    mix_in,
    col_in,
    row_in,
    dec_in,
    last_bc,
    y_out,
    own_out,
    lft_out,
    rgt_out,
    last_out,
    terms,
    x_conv,
    x_weighted,
    state,
    inter,
    spread_e,
    spread_w,
    x_in,
    tail,
    sems,
    y_stage,
    y_sems,
):
    def store(c):
        rows = pl.ds(pl.multiple_of(c * Q, Q), Q)
        return pltpu.make_async_copy(y_stage.at[rows, :], y_out.at[rows, :], y_sems.at[c])

    terms[...] = jnp.zeros_like(terms)
    targets = boundary_targets((1, 128), 1, seg)
    for lt in range(GC // 256):
        lanes = slice(256 * lt, 256 * (lt + 1))
        last = last_rows(x_in, lanes, seg)
        last_out[:, lanes] = last
        store_terms(terms, lanes, boundary_terms(last, conv_state[:, lanes], param, lanes))
        row_id = iota((256, 256), 0) % 128
        head_id = (iota((256, 256), 1) + 256 * lt) // HEADDIM
        spread_e[:, lanes] = jnp.where(row_id - GH == head_id, 1.0, 0.0).astype(BF16)
        spread_w[:, lanes] = jnp.where(row_id - 2 * GH == head_id, 1.0, 0.0).astype(BF16)

    @pl.loop(0, ROWS // 64)
    def _(i):
        r0 = pl.multiple_of(i * 64, 64)
        for lt in range(GC // 256):
            lanes = slice(256 * lt, 256 * (lt + 1))
            value = conv_rows(x_in, r0, 64, lanes, param, terms, targets)
            x_conv[pl.ds(r0, 64), lanes] = value.astype(BF16)

    @pl.loop(0, CHUNKS)
    def _(c):
        r0 = pl.multiple_of(c * Q, Q)
        rows = pl.ds(r0, Q)
        col = col_in[c]
        col_hi, col_lo = split2(col)
        col_two = jnp.concatenate([col_hi, col_lo], axis=1)
        for lt in range(GC // 256):
            lanes = slice(256 * lt, 256 * (lt + 1))
            weight = mm(col_two, spread_w[:, lanes])
            x_weighted[:, lanes] = (x_conv[rows, lanes].astype(F32) * weight).astype(BF16)
            inter[:, lanes] = jnp.zeros((Q, 256), F32)

        @pl.loop(0, SLOTS)
        def _(k):
            first, end = seg[k], seg[4 + k]

            @pl.when((first < r0 + Q) & (end > r0))
            def _():
                row_id = iota((Q, STATE), 0) + r0
                c_part = jnp.where(
                    (row_id >= first) & (row_id < end), c_in[rows, :].astype(F32), 0.0
                ).astype(BF16)
                c_two = jnp.concatenate([c_part, c_part], axis=1)
                col_id = iota((STATE, Q), 1) + r0
                b_part = jnp.where(
                    (col_id >= first) & (col_id < end), b_t_in[c].astype(F32), 0.0
                ).astype(BF16)
                decay = dec_in[pl.ds(c * SLOTS + k, 1), :]
                for lt in range(GC // 256):
                    lanes = slice(256 * lt, 256 * (lt + 1))
                    old = state[k, :, lanes]
                    both = jnp.concatenate(split2(old), axis=0)
                    inter[:, lanes] += mm(c_two, both)
                    state[k, :, lanes] = old * decay[:, lanes] + mm(b_part, x_weighted[:, lanes])

        low_half = iota((Q, 128), 1) < HEADDIM
        for lt in range(GC // 256):
            lanes = slice(256 * lt, 256 * (lt + 1))
            scale = mm(col_two, spread_e[:, lanes])
            inter[:, lanes] = inter[:, lanes] * scale + x_conv[rows, lanes].astype(F32) * skip[
                0:1, lanes
            ]
        for hp in range(GH // 2):
            lanes = slice(128 * hp, 128 * (hp + 1))
            x_pair = x_conv[rows, lanes].astype(F32)
            x_low = jnp.where(low_half, x_pair, 0.0).astype(BF16)
            x_high = jnp.where(low_half, 0.0, x_pair).astype(BF16)
            for half in range(2):
                depth = 128 * (half + 1)
                part = slice(128 * half, 128 * (half + 1))
                mix = mix_in[c, part, 0:depth]
                total = inter[part, lanes]
                for h, x_one in ((2 * hp, x_low), (2 * hp + 1, x_high)):
                    spread = col[part, h : h + 1] - row_in[c, h : h + 1, 0:depth]
                    scores = (jnp.exp2(jnp.minimum(spread, 126.0)) * mix).astype(BF16)
                    total = total + mm(scores, x_one[0:depth])
                y_stage[pl.ds(r0 + 128 * half, 128), lanes] = total
        store(c).start()

    def send_back(k, out):
        for b in range(GC // 128):
            part = slice(128 * b, 128 * (b + 1))
            out[part, :] = state[k, :, part].T.astype(BF16)
        lines = (GC + 2 * STATE) // 128
        tail[...] = jnp.zeros_like(tail)
        for j in range(3):
            row = pl.ds(3 * k + j, 1)
            line = jnp.concatenate([last_out[row, :], last_bc[row, :]], axis=1)
            for b in range(lines):
                place = slice(j * lines + b, j * lines + b + 1)
                tail[place, :] = line[:, 128 * b : 128 * (b + 1)]
        out[GC:MOVER_ROWS, :] = tail[...].astype(BF16)

    @pl.loop(0, SLOTS)
    def _(k):
        source = seg[8 + k]

        @pl.when(source < SLOTS)
        def _():
            for b in range(GC // 128):
                part = slice(128 * b, 128 * (b + 1))
                own_out[jnp.minimum(source, SLOTS - 1), part, :] = state[k, :, part].T

        @pl.when(source == SLOTS)
        def _():
            send_back(k, lft_out)

        @pl.when(source == SLOTS + 1)
        def _():
            send_back(k, rgt_out)

    @pl.loop(0, CHUNKS)
    def _(c):
        store(c).wait()


def gate_kernel(y_in, z_in, gain, out, y_stage, stage, load_sems, sems):
    def rows_of(i):
        return pl.ds(pl.multiple_of(i * GATE_ROWS, GATE_ROWS), GATE_ROWS)

    def load(i):
        return pltpu.make_async_copy(
            y_in.at[rows_of(i), :], y_stage.at[rows_of(i), :], load_sems.at[i]
        )

    def store(i):
        return pltpu.make_async_copy(stage.at[rows_of(i), :], out.at[rows_of(i), :], sems.at[i])

    for i in range(ROWS // GATE_ROWS):
        load(i).start()

    @pl.loop(0, ROWS // GATE_ROWS)
    def _(i):
        load(i).wait()
        for part in range(GATE_ROWS // 16):
            rows = pl.ds(pl.multiple_of(i * GATE_ROWS + 16 * part, 16), 16)
            gated = y_stage[rows, :] * silu(z_in[rows, :].astype(F32))
            mean = jnp.sum(gated * gated, axis=1, keepdims=True) * (1.0 / GC)
            stage[rows, :] = (gated * lax.rsqrt(mean + EPSILON) * gain[...]).astype(BF16)
        store(i).start()

    @pl.loop(0, ROWS // GATE_ROWS)
    def _(i):
        store(i).wait()


VMEM = pl.BlockSpec(memory_space=pltpu.VMEM)
SMEM = pl.BlockSpec(memory_space=pltpu.SMEM)
ANY = pl.BlockSpec(memory_space=pl.ANY)
HBM = pl.BlockSpec(memory_space=pltpu.HBM)


def in_hbm(value):
    return pltpu.with_memory_space_constraint(value, pltpu.HBM)


def params(mib):
    return pltpu.CompilerParams(vmem_limit_bytes=mib * MIB)


def pack(offsets, here, x_in, bc_in, dt_in):
    count = len(offsets)
    blocks = pl.pallas_call(
        functools.partial(pack_kernel, offsets),
        out_shape=(
            jax.ShapeDtypeStruct((BLOCK_ROWS, LANES), BF16)
            if count == 1
            else pltpu.HBM((BLOCK_ROWS, LANES), BF16),
        )
        * count,
        in_specs=[SMEM, HBM, HBM, HBM],
        out_specs=(VMEM if count == 1 else HBM,) * count,
        scratch_shapes=[
            pltpu.VMEM((count, BLOCK_ROWS, LANES), BF16),
            pltpu.VMEM((SRC_ROWS, HEADS), BF16),
            pltpu.VMEM((HEADS, SRC_ROWS), BF16),
            pltpu.SemaphoreType.DMA((count * (TILES + BC_TILES),)),
            pltpu.SemaphoreType.DMA((count,)),
            pltpu.SemaphoreType.DMA,
        ],
        compiler_params=params(8),
        name="pack",
    )(here, in_hbm(x_in), in_hbm(bc_in), in_hbm(dt_in))
    return dict(zip(offsets, blocks))


def movers(slots, own, small):
    return pl.pallas_call(
        mover_kernel,
        out_shape=(jax.ShapeDtypeStruct((MOVER_ROWS, STATE), F32),) * 2,
        in_specs=[SMEM, HBM, VMEM],
        out_specs=(VMEM,) * 2,
        scratch_shapes=[pltpu.SemaphoreType.DMA((2,))],
        compiler_params=params(8),
        name="movers",
    )(slots, in_hbm(own), small)


def initial(seg, own, lft, rgt):
    return pl.pallas_call(
        init_kernel,
        out_shape=pltpu.HBM((SLOTS, STATE, GC), F32),
        in_specs=[SMEM] + [VMEM] * 3,
        out_specs=VMEM,
        compiler_params=params(8),
        cost_estimate=pl.CostEstimate(
            flops=2_000_000_000, bytes_accessed=4 * MIB, transcendentals=0
        ),
        name="initial",
    )(seg, own, lft, rgt)


def scan(seg, here, blocks, *operands):
    return pl.pallas_call(
        scan_kernel,
        out_shape=(
            pltpu.HBM((ROWS, GC), F32),
            jax.ShapeDtypeStruct((SLOTS, GC, STATE), F32),
            jax.ShapeDtypeStruct((MOVER_ROWS, STATE), BF16),
            jax.ShapeDtypeStruct((MOVER_ROWS, STATE), BF16),
            jax.ShapeDtypeStruct((16, GC), F32),
            jax.ShapeDtypeStruct((16, 2 * STATE), F32),
        ),
        in_specs=[SMEM, SMEM] + [ANY] * TENSOR + [VMEM] * (len(operands) - 1) + [HBM],
        out_specs=(HBM,) + (VMEM,) * 5,
        scratch_shapes=[
            pltpu.VMEM((CHUNKS, STATE, Q), BF16),
            pltpu.VMEM((ROWS, STATE), BF16),
            pltpu.VMEM((CHUNKS, Q, Q), F32),
            pltpu.VMEM((CHUNKS, Q, 128), F32),
            pltpu.VMEM((CHUNKS, GH, Q), F32),
            pltpu.VMEM((16, GC), F32),
            pltpu.VMEM((ROWS, 2 * STATE), BF16),
            pltpu.VMEM((TENSOR, GH, LANES), BF16),
            pltpu.VMEM((ROWS, STATE), BF16),
            pltpu.VMEM((128, 2 * STATE), BF16),
            pltpu.SemaphoreType.DMA(((BC_TILES + 1) * TENSOR,)),
            pltpu.VMEM((128, GC), BF16),
            pltpu.VMEM((ROWS, GC), BF16),
            pltpu.VMEM((Q, GC), BF16),
            pltpu.VMEM((SLOTS, STATE, GC), F32),
            pltpu.VMEM((Q, GC), F32),
            pltpu.VMEM((256, GC), BF16),
            pltpu.VMEM((256, GC), BF16),
            pltpu.VMEM((ROWS, GC), BF16),
            pltpu.VMEM((32, STATE), F32),
            pltpu.SemaphoreType.DMA((TENSOR * TILES + 1,)),
            pltpu.VMEM((ROWS, GC), F32),
            pltpu.SemaphoreType.DMA((CHUNKS,)),
        ],
        compiler_params=params(28),
        cost_estimate=pl.CostEstimate(
            flops=26_000_000_000, bytes_accessed=16 * MIB, transcendentals=5_500_000
        ),
        name="scan",
    )(seg, here, *blocks, *operands)


def gate(y, z_rows, gain):
    return pl.pallas_call(
        gate_kernel,
        out_shape=jax.ShapeDtypeStruct((ROWS, GC), BF16),
        in_specs=[HBM, VMEM, VMEM],
        out_specs=ANY,
        scratch_shapes=[
            pltpu.VMEM((ROWS, GC), F32),
            pltpu.VMEM((ROWS, GC), BF16),
            pltpu.SemaphoreType.DMA((ROWS // GATE_ROWS,)),
            pltpu.SemaphoreType.DMA((ROWS // GATE_ROWS,)),
        ],
        compiler_params=params(12),
        cost_estimate=pl.CostEstimate(
            flops=20_000_000, bytes_accessed=8 * MIB, transcendentals=1_000_000
        ),
        name="gate",
    )(in_hbm(y), z_rows, gain)


def shifted(value, steps):
    count = lax.axis_size("dp")
    pairs = [(source, (source + steps) % count) for source in range(count)]
    return lax.ppermute(value, "dp", pairs)


def rotated(value, steps):
    count = lax.axis_size("tensor")
    pairs = [(source, (source + steps) % count) for source in range(count)]
    return lax.ppermute(value, "tensor", pairs)


def after(value, *earlier):
    if not earlier:
        return value
    return lax.optimization_barrier((value, *earlier))[0]


def plan(lengths, prefill_owner, row_start, me, left, right):
    ids = jnp.arange(prefill_owner.shape[0], dtype=jnp.int32)
    mine = prefill_owner == me
    home = ids // SLOTS
    code = jnp.where(home == me, ids % SLOTS, jnp.where(home == left, SLOTS, SLOTS + 1))
    before = mine[None, :] & (row_start[None, :] < row_start[:, None])
    rank = jnp.sum(before.astype(jnp.int32), axis=1)
    chosen = mine[None, :] & (rank[None, :] == jnp.arange(SLOTS, dtype=jnp.int32)[:, None])

    def pick(values):
        return jnp.sum(jnp.where(chosen, values[None, :], 0), axis=1)

    starts = pick(row_start)
    codes = pick(code)
    seg = jnp.concatenate([starts, starts + pick(lengths), codes, jnp.zeros((4,), jnp.int32)])
    slot_right = jnp.sum(jnp.where((home == me) & (prefill_owner == right), ids % SLOTS, 0))
    slot_left = jnp.sum(jnp.where((home == me) & (prefill_owner == left), ids % SLOTS, 0))
    return seg, codes, slot_right, slot_left


def shards(
    x_in,
    z_in,
    bc_in,
    dt_in,
    conv_x_param,
    conv_bc_param,
    decay_rate,
    dt_bias,
    skip_gain,
    norm_gain,
    ssm_state,
    conv_x_state,
    conv_bc_state,
    lengths,
    prefill_owner,
    row_start,
):
    dp_count = lax.axis_size("dp")
    me = lax.axis_index("dp")
    left = (me + dp_count - 1) % dp_count
    right = (me + 1) % dp_count
    here = lax.axis_index("tensor")
    here_ref = here.astype(jnp.int32)[None]
    packed = {}
    turn = here_ref
    for offsets in (FIRST[:1], FIRST[1:], SECOND + THIRD + (0,)):
        packed |= pack(offsets, turn, x_in, bc_in, dt_in)
        turn = after(here_ref, packed[offsets[0]])
    blocks = {0: packed[0]}
    for d in FIRST:
        blocks[d] = rotated(packed[d], d)

    seg, codes, slot_right, slot_left = plan(lengths, prefill_owner, row_start, me, left, right)

    own = ssm_state.reshape(SLOTS, GC, STATE)
    conv = jnp.concatenate([conv_x_state, conv_bc_state], axis=2)
    width = conv.shape[2]
    lines = 3 * width // STATE

    def small_mover(slot):
        small = lax.dynamic_index_in_dim(conv, slot, 0, keepdims=False).reshape(lines, STATE)
        return jnp.concatenate([small, jnp.zeros((2, STATE), F32)], axis=0)

    move_right, move_left = movers(
        after(jnp.stack([slot_right, slot_left]).astype(jnp.int32), packed[0]),
        own,
        jnp.stack([small_mover(slot_right), small_mover(slot_left)]),
    )
    from_left = shifted(move_right, 1)
    from_right = shifted(move_left, -1)
    for d in SECOND:
        blocks[d] = rotated(after(packed[d], from_left, from_right), d)

    def small_of(packed):
        return packed[GC : GC + lines].reshape(1, 3, width)

    candidates = jnp.concatenate([conv, small_of(from_left), small_of(from_right)], axis=0)
    match = codes[:, None] == jnp.arange(SLOTS + 2, dtype=jnp.int32)[None, :]
    conv_init = jnp.sum(jnp.where(match[:, :, None, None], candidates[None], 0.0), axis=1)
    conv_init = jnp.concatenate([conv_init.reshape(3 * SLOTS, width), jnp.zeros((4, width), F32)])

    z_sent = z_in.reshape(SRC_ROWS, TENSOR, GC).transpose(1, 0, 2)
    init = initial(seg, own, from_left, from_right)
    conv_init, init, z_sent, seg, gain, skip, rate, bias = lax.optimization_barrier(
        (
            conv_init,
            init,
            z_sent,
            seg,
            norm_gain[None, :],
            jnp.repeat(skip_gain, HEADDIM)[None, :],
            decay_rate[:, None],
            dt_bias[:, None],
        )
    )
    for d in THIRD:
        blocks[d] = rotated(after(packed[d], conv_init, z_sent, *[blocks[e] for e in FIRST[1:]]), d)
    z_sent = after(z_sent, *[blocks[e] for e in FIRST])
    z_rows = lax.all_to_all(z_sent, "tensor", split_axis=0, concat_axis=0, tiled=True)
    z_rows = z_rows.reshape(ROWS, GC)

    in_order = [blocks[d] for d in range(TENSOR)]
    y, own_new, back_left, back_right, last_x, last_bc = scan(
        seg,
        here_ref,
        in_order,
        conv_init[:, :GC],
        conv_init[:, GC:],
        conv_x_param,
        skip,
        conv_bc_param,
        rate,
        bias,
        in_hbm(init),
    )
    returned_right = shifted(back_left, -1)
    returned_left = shifted(back_right, 1)
    last = jnp.concatenate([last_x, last_bc], axis=1)[: 3 * SLOTS].reshape(SLOTS, 3, width)

    new_ssm = own_new
    for packed, slot in ((returned_right, slot_right), (returned_left, slot_left)):
        new_ssm = lax.dynamic_update_index_in_dim(new_ssm, packed[:GC].astype(F32), slot, 0)
    slots = jnp.arange(SLOTS, dtype=jnp.int32)
    stay = slots[:, None] == codes[None, :]
    new_conv = jnp.sum(jnp.where(stay[:, :, None, None], last[None], 0.0), axis=1)
    for packed, slot in ((returned_right, slot_right), (returned_left, slot_left)):
        new_conv = jnp.where(
            (slots == slot)[:, None, None], small_of(packed).astype(F32), new_conv
        )
    new_cx, new_cbc = new_conv[:, :, :GC], new_conv[:, :, GC:]

    y, new_ssm, new_cx, new_cbc = lax.optimization_barrier((y, new_ssm, new_cx, new_cbc))
    y_out = gate(y, z_rows, gain)
    return y_out, new_ssm.reshape(ssm_state.shape), new_cx, new_cbc


def solution(mesh):
    in_specs = (
        P(("dp", "tensor"), None),
        P(("dp", "tensor"), None),
        P(("dp", "tensor"), None),
        P(("dp", "tensor"), None),
        P(None, "tensor"),
        P(None, "tensor"),
        P("tensor"),
        P("tensor"),
        P("tensor"),
        P("tensor"),
        P("dp", "tensor", None, None),
        P("dp", None, "tensor"),
        P("dp", None, "tensor"),
        P(),
        P(),
        P(),
    )
    out_specs = (
        P("dp", "tensor"),
        P("dp", "tensor", None, None),
        P("dp", None, "tensor"),
        P("dp", None, "tensor"),
    )
    return jax.shard_map(shards, mesh=mesh, in_specs=in_specs, out_specs=out_specs, check_vma=False)
```

```python
import functools
import math

import jax
import jax.numpy as jnp
from jax import lax
from jax.experimental import pallas as pl
from jax.experimental.pallas import tpu as pltpu
from jax.sharding import PartitionSpec as P

HEADS = 128
HEADDIM = 64
STATE = 128
GROUPS = 8
SLOTS = 4
ROWS = 1024
GH = HEADS // GROUPS
GC = GH * HEADDIM
Q = 256
CHUNKS = ROWS // Q
TENSOR = 8
SRC_ROWS = ROWS // TENSOR
EPSILON = 1e-05
LOG2E = math.log2(math.e)
LANES = 128
TILES = GC // LANES
BC_TILES = 2 * STATE // LANES
BC_ROW = TILES * SRC_ROWS
DT_ROW = BC_ROW + BC_TILES * SRC_ROWS
BLOCK_ROWS = DT_ROW + GH
MOVER_ROWS = GC + 32
GATE_ROWS = 128
HEAD_ROWS = 128
ORDER = (4, 3, 5, 2, 6, 1, 7)
FIRST = (4, 3, 5)
SECOND = (2, 6)
THIRD = (1, 7)
MIB = 1 << 20

F32 = jnp.float32
BF16 = jnp.bfloat16


def mm(a, b):
    return jnp.dot(a, b, preferred_element_type=F32)


def iota(shape, dim):
    return lax.broadcasted_iota(jnp.int32, shape, dim)


def silu(v):
    half = v * 0.5
    return half + half * jnp.tanh(half)


def split2(v):
    hi = v.astype(BF16)
    return hi, (v - hi.astype(F32)).astype(BF16)


def split3(v):
    hi = v.astype(BF16)
    rest = v - hi.astype(F32)
    mid = rest.astype(BF16)
    return hi, mid, (rest - mid.astype(F32)).astype(BF16)


def segment_of(row_ids, seg):
    total = jnp.zeros(row_ids.shape, jnp.int32)
    for k in range(1, SLOTS):
        total = total + (row_ids >= seg[k]).astype(jnp.int32)
    return total


def boundary_targets(shape, dim, seg):
    idx = iota(shape, dim) % 16
    target = jnp.full(shape, -1, jnp.int32)
    for s in range(SLOTS):
        for q in range(3):
            target = jnp.where(idx == 3 * s + q, seg[s] + q, target)
    return jnp.where(iota(shape, dim) < 48, target, -1)


def last_rows(x_ref, lanes, seg):
    idx = iota((16, 1), 0)
    target = jnp.full((16, 1), -1, jnp.int32)
    for s in range(SLOTS):
        for q in range(3):
            target = jnp.where(idx == 3 * s + q, seg[4 + s] - 3 + q, target)
    picker = (iota((16, ROWS), 1) == target).astype(F32).astype(BF16)
    return mm(picker, x_ref[0:ROWS, lanes])


def boundary_terms(last, state, param, lanes):
    diff = state - pltpu.roll(last, 3, 0)
    q = iota((16, 1), 0) % 3
    term = param[0:1, lanes] * diff
    term = term + jnp.where(q <= 1, param[1:2, lanes] * pltpu.roll(diff, 15, 0), 0.0)
    term = term + jnp.where(q == 0, param[2:3, lanes] * pltpu.roll(diff, 14, 0), 0.0)
    return split3(term)


def conv_rows(x_ref, r0, count, lanes, param, terms_ref, targets):
    prev = pl.multiple_of(jnp.maximum(r0 - 16, 0), 16)
    halo = x_ref[pl.ds(prev, 16), lanes].astype(F32) * jnp.where(r0 > 0, 1.0, 0.0)
    value = jnp.concatenate([halo, x_ref[pl.ds(r0, count), lanes].astype(F32)], axis=0)
    onehot = (iota((count, 128), 0) + r0 == targets).astype(F32).astype(BF16)
    total = mm(onehot, terms_ref[:, lanes]) + param[4:5, lanes]
    total = total + param[3:4, lanes] * value[16:]
    for lag in (1, 2, 3):
        total = total + param[3 - lag : 4 - lag, lanes] * pltpu.roll(value, lag, 0)[16:]
    return silu(total)


def store_terms(terms_ref, lanes, parts):
    for i, part in enumerate(parts):
        terms_ref[16 * i : 16 * i + 16, lanes] = part


def copy_all(copies, sems, later=()):
    started = [
        pltpu.make_async_copy(source, target, sems.at[i])
        for i, (source, target) in enumerate(copies)
    ]
    for copy in [*started, *later]:
        copy.start()
    for copy in started:
        copy.wait()


def pack_kernel(offsets, here, x, bc, dt, *rest):
    count = len(offsets)
    outs, (stage, dt_all, dt_turned, sems, out_sems, dt_sem) = rest[:count], rest[count:]
    direct = count == 1
    parts = list(outs) if direct else [stage.at[n] for n in range(count)]
    dt_load = pltpu.make_async_copy(dt, dt_all, dt_sem)
    dt_load.start()
    loads = []
    for n, d in enumerate(offsets):
        to = (here[0] + d) % TENSOR
        sources = []
        for i in range(TILES):
            lanes = pl.ds(pl.multiple_of(to * GC + LANES * i, LANES), LANES)
            sources.append(x.at[:, lanes])
        for i in range(BC_TILES):
            lanes = pl.ds(pl.multiple_of(to * 2 * STATE + LANES * i, LANES), LANES)
            sources.append(bc.at[:, lanes])
        loads.append(
            [
                pltpu.make_async_copy(
                    source,
                    parts[n].at[SRC_ROWS * i : SRC_ROWS * (i + 1), :],
                    sems.at[n * (TILES + BC_TILES) + i],
                )
                for i, source in enumerate(sources)
            ]
        )
        for copy in loads[-1]:
            copy.start()
    dt_load.wait()
    dt_turned[...] = dt_all[...].astype(F32).T.astype(BF16)
    stores = []
    for n, d in enumerate(offsets):
        to = (here[0] + d) % TENSOR
        heads = pl.ds(pl.multiple_of(to * GH, GH), GH)
        parts[n][DT_ROW:BLOCK_ROWS, :] = dt_turned[heads, :]
        for copy in loads[n]:
            copy.wait()
        if not direct:
            stores.append(pltpu.make_async_copy(parts[n], outs[n], out_sems.at[n]))
            stores[-1].start()
    for copy in stores:
        copy.wait()


def mover_kernel(slots, own, small, right_out, left_out, sems):
    outs = (right_out, left_out)
    for i in range(2):
        outs[i][GC:MOVER_ROWS, :] = small[i]
    copy_all([(own.at[slots[i]], outs[i].at[0:GC, :]) for i in range(2)], sems)


def init_kernel(seg, own, lft, rgt, init_out):
    def load_state(k, block_of):
        for b in range(GC // 128):
            init_out[k, :, 128 * b : 128 * (b + 1)] = block_of(b).T

    @pl.loop(0, SLOTS)
    def _(k):
        source = seg[8 + k]

        @pl.when(source < SLOTS)
        def _():
            load_state(k, lambda b: own[jnp.minimum(source, SLOTS - 1), 128 * b : 128 * (b + 1), :])

        @pl.when(source == SLOTS)
        def _():
            load_state(k, lambda b: lft[128 * b : 128 * (b + 1), :])

        @pl.when(source == SLOTS + 1)
        def _():
            load_state(k, lambda b: rgt[128 * b : 128 * (b + 1), :])


def source_of(here, d):
    return (here[0] + (TENSOR - d)) % TENSOR


def prep_body(
    seg,
    here,
    blocks,
    conv_state,
    param,
    rate,
    bias,
    b_t_out,
    c_out,
    mix_out,
    col_out,
    row_out,
    dec_out,
    last_out,
    bc_rows,
    dt_rows,
    b_rows,
    terms,
    sems,
    loads,
):
    copies = []
    for d in range(TENSOR):
        source = source_of(here, d)
        rows = pl.ds(pl.multiple_of(source * SRC_ROWS, SRC_ROWS), SRC_ROWS)
        for i in range(BC_TILES):
            part = blocks[d].at[BC_ROW + SRC_ROWS * i : BC_ROW + SRC_ROWS * (i + 1), :]
            copies.append((part, bc_rows.at[rows, LANES * i : LANES * (i + 1)]))
        copies.append((blocks[d].at[DT_ROW:BLOCK_ROWS, :], dt_rows.at[source]))
    copy_all(copies, sems, loads)
    every = slice(0, 2 * STATE)
    last = last_rows(bc_rows, every, seg)
    last_out[...] = last
    terms[...] = jnp.zeros_like(terms)
    store_terms(terms, every, boundary_terms(last, conv_state[...], param, every))
    targets = boundary_targets((1, 128), 1, seg)

    @pl.loop(0, ROWS // 64)
    def _(i):
        r0 = pl.multiple_of(i * 64, 64)
        value = conv_rows(bc_rows, r0, 64, every, param, terms, targets).astype(BF16)
        b_rows[pl.ds(r0, 64), :] = value[:, 0:STATE]
        c_out[pl.ds(r0, 64), :] = value[:, STATE:]

    dec_sum = jnp.zeros((GH, 128), F32)
    for c in range(CHUNKS):
        b_t = b_rows[Q * c : Q * (c + 1), :].astype(F32).T.astype(BF16)
        b_t_out[c] = b_t
        seg_col = segment_of(iota((Q, 1), 0) + Q * c, seg)
        seg_row = segment_of(iota((1, Q), 1) + Q * c, seg)
        same = seg_col == seg_row
        row_id, col_id = iota((Q, Q), 0), iota((Q, Q), 1)
        mix = mm(c_out[Q * c : Q * (c + 1), :], b_t)
        mix_out[c] = jnp.where(same & (col_id <= row_id), mix, 0.0)
        up_to = jnp.where(same & (row_id <= col_id), 1.0, 0.0).astype(BF16)
        after = jnp.where(same & (row_id > col_id), 1.0, 0.0).astype(BF16)
        raw = jnp.concatenate(
            [dt_rows[s, :, 0:SRC_ROWS] for s in (2 * c, 2 * c + 1)], axis=1
        ).astype(F32) + bias[...]
        step = jnp.maximum(raw, 0.0) + jnp.log1p(jnp.exp(-jnp.abs(raw)))
        log_decay = step * rate[...] * (-LOG2E)
        parts = jnp.concatenate(split3(log_decay), axis=0)

        def summed(mask):
            three = mm(parts, mask)
            return three[0:GH] + three[GH : 2 * GH] + three[2 * GH : 3 * GH]

        running = summed(up_to)
        rest = summed(after)
        row_out[c] = running - jnp.log2(step)
        stack = jnp.concatenate(
            [running, jnp.exp2(running), jnp.exp2(rest) * step, jnp.zeros((80, Q), F32)], axis=0
        )
        col_out[c] = stack.T
        pair = jnp.where(seg_col + SLOTS * c == iota((Q, 128), 1), 1.0, 0.0).astype(BF16)
        dec_sum = dec_sum + summed(pair)
    decay = jnp.concatenate([jnp.exp2(dec_sum), jnp.zeros((128 - GH, 128), F32)], axis=0).T[0:16]
    spread = jnp.where(iota((128, GC), 0) == iota((128, GC), 1) // HEADDIM, 1.0, 0.0).astype(BF16)
    dec_hi, dec_lo = split2(decay)
    dec_out[...] = mm(dec_hi, spread) + mm(dec_lo, spread)


def scan_kernel(seg, here, *rest):
    blocks, rest = rest[:TENSOR], rest[TENSOR:]
    conv_x, conv_bc, x_param, skip, bc_param, rate, bias, init = rest[:8]
    y_head, y_out, own_out, lft_out, rgt_out, last_x, last_bc = rest[8:15]
    prep_out, prep_scratch, scratch = rest[15:21], rest[21:26], rest[26:]
    x_rows, x_sems = scratch[7], scratch[9]
    loads = [pltpu.make_async_copy(init, scratch[3], x_sems.at[TENSOR * TILES])]
    for d in range(TENSOR):
        rows = pl.ds(pl.multiple_of(source_of(here, d) * SRC_ROWS, SRC_ROWS), SRC_ROWS)
        for i in range(TILES):
            part = blocks[d].at[SRC_ROWS * i : SRC_ROWS * (i + 1), :]
            place = x_rows.at[rows, LANES * i : LANES * (i + 1)]
            loads.append(pltpu.make_async_copy(part, place, x_sems.at[d * TILES + i]))
    prep_body(
        seg, here, blocks, conv_bc, bc_param, rate, bias, *prep_out, last_bc, *prep_scratch, loads
    )
    for copy in loads:
        copy.wait()

    main_body(
        seg, conv_x, x_param, skip, *prep_out, last_bc, y_head, y_out, own_out, lft_out, rgt_out,
        last_x, *scratch
    )


def main_body(
    seg,
    conv_state,
    param,
    skip,
    b_t_in,
    c_in,
    mix_in,
    col_in,
    row_in,
    dec_in,
    last_bc,
    y_head,
    y_out,
    own_out,
    lft_out,
    rgt_out,
    last_out,
    terms,
    x_conv,
    x_weighted,
    state,
    inter,
    spread_e,
    spread_w,
    x_in,
    tail,
    sems,
    y_stage,
    y_sems,
):
    def store(c):
        rows = pl.ds(pl.multiple_of(c * Q, Q), Q)
        return pltpu.make_async_copy(y_stage.at[rows, :], y_out.at[rows, :], y_sems.at[c])

    terms[...] = jnp.zeros_like(terms)
    targets = boundary_targets((1, 128), 1, seg)
    for lt in range(GC // 256):
        lanes = slice(256 * lt, 256 * (lt + 1))
        last = last_rows(x_in, lanes, seg)
        last_out[:, lanes] = last
        store_terms(terms, lanes, boundary_terms(last, conv_state[:, lanes], param, lanes))
        row_id = iota((256, 256), 0) % 128
        head_id = (iota((256, 256), 1) + 256 * lt) // HEADDIM
        spread_e[:, lanes] = jnp.where(row_id - GH == head_id, 1.0, 0.0).astype(BF16)
        spread_w[:, lanes] = jnp.where(row_id - 2 * GH == head_id, 1.0, 0.0).astype(BF16)

    @pl.loop(0, ROWS // 64)
    def _(i):
        r0 = pl.multiple_of(i * 64, 64)
        for lt in range(GC // 256):
            lanes = slice(256 * lt, 256 * (lt + 1))
            value = conv_rows(x_in, r0, 64, lanes, param, terms, targets)
            x_conv[pl.ds(r0, 64), lanes] = value.astype(BF16)

    @pl.loop(0, CHUNKS)
    def _(c):
        r0 = pl.multiple_of(c * Q, Q)
        rows = pl.ds(r0, Q)
        col = col_in[c]
        col_hi, col_lo = split2(col)
        col_two = jnp.concatenate([col_hi, col_lo], axis=1)
        for lt in range(GC // 256):
            lanes = slice(256 * lt, 256 * (lt + 1))
            weight = mm(col_two, spread_w[:, lanes])
            x_weighted[:, lanes] = (x_conv[rows, lanes].astype(F32) * weight).astype(BF16)
            inter[:, lanes] = jnp.zeros((Q, 256), F32)

        @pl.loop(0, SLOTS)
        def _(k):
            first, end = seg[k], seg[4 + k]

            @pl.when((first < r0 + Q) & (end > r0))
            def _():
                row_id = iota((Q, STATE), 0) + r0
                c_part = jnp.where(
                    (row_id >= first) & (row_id < end), c_in[rows, :].astype(F32), 0.0
                ).astype(BF16)
                c_two = jnp.concatenate([c_part, c_part], axis=1)
                col_id = iota((STATE, Q), 1) + r0
                b_part = jnp.where(
                    (col_id >= first) & (col_id < end), b_t_in[c].astype(F32), 0.0
                ).astype(BF16)
                decay = dec_in[pl.ds(c * SLOTS + k, 1), :]
                for lt in range(GC // 256):
                    lanes = slice(256 * lt, 256 * (lt + 1))
                    old = state[k, :, lanes]
                    both = jnp.concatenate(split2(old), axis=0)
                    inter[:, lanes] += mm(c_two, both)
                    state[k, :, lanes] = old * decay[:, lanes] + mm(b_part, x_weighted[:, lanes])

        low_half = iota((Q, 128), 1) < HEADDIM
        for lt in range(GC // 256):
            lanes = slice(256 * lt, 256 * (lt + 1))
            scale = mm(col_two, spread_e[:, lanes])
            inter[:, lanes] = inter[:, lanes] * scale + x_conv[rows, lanes].astype(F32) * skip[
                0:1, lanes
            ]
        for hp in range(GH // 2):
            lanes = slice(128 * hp, 128 * (hp + 1))
            x_pair = x_conv[rows, lanes].astype(F32)
            x_low = jnp.where(low_half, x_pair, 0.0).astype(BF16)
            x_high = jnp.where(low_half, 0.0, x_pair).astype(BF16)
            for half in range(2):
                depth = 128 * (half + 1)
                part = slice(128 * half, 128 * (half + 1))
                mix = mix_in[c, part, 0:depth]
                total = inter[part, lanes]
                for h, x_one in ((2 * hp, x_low), (2 * hp + 1, x_high)):
                    spread = col[part, h : h + 1] - row_in[c, h : h + 1, 0:depth]
                    scores = (jnp.exp2(jnp.minimum(spread, 126.0)) * mix).astype(BF16)
                    total = total + mm(scores, x_one[0:depth])
                y_stage[pl.ds(r0 + 128 * half, 128), lanes] = total
        store(c).start()

        @pl.when(c == 0)
        def _():
            y_head[...] = y_stage[0:HEAD_ROWS, :]

    def send_back(k, out):
        for b in range(GC // 128):
            part = slice(128 * b, 128 * (b + 1))
            out[part, :] = state[k, :, part].T.astype(BF16)
        lines = (GC + 2 * STATE) // 128
        tail[...] = jnp.zeros_like(tail)
        for j in range(3):
            row = pl.ds(3 * k + j, 1)
            line = jnp.concatenate([last_out[row, :], last_bc[row, :]], axis=1)
            for b in range(lines):
                place = slice(j * lines + b, j * lines + b + 1)
                tail[place, :] = line[:, 128 * b : 128 * (b + 1)]
        out[GC:MOVER_ROWS, :] = tail[...].astype(BF16)

    @pl.loop(0, SLOTS)
    def _(k):
        source = seg[8 + k]

        @pl.when(source < SLOTS)
        def _():
            for b in range(GC // 128):
                part = slice(128 * b, 128 * (b + 1))
                own_out[jnp.minimum(source, SLOTS - 1), part, :] = state[k, :, part].T

        @pl.when(source == SLOTS)
        def _():
            send_back(k, lft_out)

        @pl.when(source == SLOTS + 1)
        def _():
            send_back(k, rgt_out)

    @pl.loop(0, CHUNKS)
    def _(c):
        store(c).wait()


def gate_kernel(y_head, y_in, z_in, gain, out, y_stage, stage, load_sems, sems):
    head, count = HEAD_ROWS // GATE_ROWS, ROWS // GATE_ROWS

    def rows_of(i):
        return pl.ds(pl.multiple_of(i * GATE_ROWS, GATE_ROWS), GATE_ROWS)

    def load(i):
        return pltpu.make_async_copy(
            y_in.at[rows_of(i), :], y_stage.at[rows_of(i), :], load_sems.at[i]
        )

    def store(i):
        return pltpu.make_async_copy(stage.at[rows_of(i), :], out.at[rows_of(i), :], sems.at[i])

    def gate_rows(i, y_ref):
        for part in range(GATE_ROWS // 16):
            rows = pl.ds(pl.multiple_of(i * GATE_ROWS + 16 * part, 16), 16)
            gated = y_ref[rows, :] * silu(z_in[rows, :].astype(F32))
            mean = jnp.sum(gated * gated, axis=1, keepdims=True) * (1.0 / GC)
            stage[rows, :] = (gated * lax.rsqrt(mean + EPSILON) * gain[...]).astype(BF16)
        store(i).start()

    for i in range(head, count):
        load(i).start()

    @pl.loop(0, head)
    def _(i):
        gate_rows(i, y_head)

    @pl.loop(head, count)
    def _(i):
        load(i).wait()
        gate_rows(i, y_stage)

    @pl.loop(0, count)
    def _(i):
        store(i).wait()


VMEM = pl.BlockSpec(memory_space=pltpu.VMEM)
SMEM = pl.BlockSpec(memory_space=pltpu.SMEM)
ANY = pl.BlockSpec(memory_space=pl.ANY)
HBM = pl.BlockSpec(memory_space=pltpu.HBM)


def in_hbm(value):
    return pltpu.with_memory_space_constraint(value, pltpu.HBM)


def params(mib):
    return pltpu.CompilerParams(vmem_limit_bytes=mib * MIB)


def pack(offsets, here, x_in, bc_in, dt_in):
    count = len(offsets)
    blocks = pl.pallas_call(
        functools.partial(pack_kernel, offsets),
        out_shape=(
            jax.ShapeDtypeStruct((BLOCK_ROWS, LANES), BF16)
            if count == 1
            else pltpu.HBM((BLOCK_ROWS, LANES), BF16),
        )
        * count,
        in_specs=[SMEM, HBM, HBM, HBM],
        out_specs=(VMEM if count == 1 else HBM,) * count,
        scratch_shapes=[
            pltpu.VMEM((count, BLOCK_ROWS, LANES), BF16),
            pltpu.VMEM((SRC_ROWS, HEADS), BF16),
            pltpu.VMEM((HEADS, SRC_ROWS), BF16),
            pltpu.SemaphoreType.DMA((count * (TILES + BC_TILES),)),
            pltpu.SemaphoreType.DMA((count,)),
            pltpu.SemaphoreType.DMA,
        ],
        compiler_params=params(8),
        name="pack",
    )(here, in_hbm(x_in), in_hbm(bc_in), in_hbm(dt_in))
    return dict(zip(offsets, blocks))


def movers(slots, own, small):
    return pl.pallas_call(
        mover_kernel,
        out_shape=(jax.ShapeDtypeStruct((MOVER_ROWS, STATE), F32),) * 2,
        in_specs=[SMEM, HBM, VMEM],
        out_specs=(VMEM,) * 2,
        scratch_shapes=[pltpu.SemaphoreType.DMA((2,))],
        compiler_params=params(8),
        name="movers",
    )(slots, in_hbm(own), small)


def initial(seg, own, lft, rgt):
    return pl.pallas_call(
        init_kernel,
        out_shape=pltpu.HBM((SLOTS, STATE, GC), F32),
        in_specs=[SMEM] + [VMEM] * 3,
        out_specs=VMEM,
        compiler_params=params(8),
        cost_estimate=pl.CostEstimate(
            flops=2_000_000_000, bytes_accessed=4 * MIB, transcendentals=0
        ),
        name="initial",
    )(seg, own, lft, rgt)


def scan(seg, here, blocks, *operands):
    return pl.pallas_call(
        scan_kernel,
        out_shape=(
            jax.ShapeDtypeStruct((HEAD_ROWS, GC), F32),
            pltpu.HBM((ROWS, GC), F32),
            jax.ShapeDtypeStruct((SLOTS, GC, STATE), F32),
            jax.ShapeDtypeStruct((MOVER_ROWS, STATE), BF16),
            jax.ShapeDtypeStruct((MOVER_ROWS, STATE), BF16),
            jax.ShapeDtypeStruct((16, GC), F32),
            jax.ShapeDtypeStruct((16, 2 * STATE), F32),
        ),
        in_specs=[SMEM, SMEM] + [ANY] * TENSOR + [VMEM] * (len(operands) - 1) + [HBM],
        out_specs=(VMEM, HBM) + (VMEM,) * 5,
        scratch_shapes=[
            pltpu.VMEM((CHUNKS, STATE, Q), BF16),
            pltpu.VMEM((ROWS, STATE), BF16),
            pltpu.VMEM((CHUNKS, Q, Q), F32),
            pltpu.VMEM((CHUNKS, Q, 128), F32),
            pltpu.VMEM((CHUNKS, GH, Q), F32),
            pltpu.VMEM((16, GC), F32),
            pltpu.VMEM((ROWS, 2 * STATE), BF16),
            pltpu.VMEM((TENSOR, GH, LANES), BF16),
            pltpu.VMEM((ROWS, STATE), BF16),
            pltpu.VMEM((128, 2 * STATE), BF16),
            pltpu.SemaphoreType.DMA(((BC_TILES + 1) * TENSOR,)),
            pltpu.VMEM((128, GC), BF16),
            pltpu.VMEM((ROWS, GC), BF16),
            pltpu.VMEM((Q, GC), BF16),
            pltpu.VMEM((SLOTS, STATE, GC), F32),
            pltpu.VMEM((Q, GC), F32),
            pltpu.VMEM((256, GC), BF16),
            pltpu.VMEM((256, GC), BF16),
            pltpu.VMEM((ROWS, GC), BF16),
            pltpu.VMEM((32, STATE), F32),
            pltpu.SemaphoreType.DMA((TENSOR * TILES + 1,)),
            pltpu.VMEM((ROWS, GC), F32),
            pltpu.SemaphoreType.DMA((CHUNKS,)),
        ],
        compiler_params=params(28),
        cost_estimate=pl.CostEstimate(
            flops=26_000_000_000, bytes_accessed=16 * MIB, transcendentals=5_500_000
        ),
        name="scan",
    )(seg, here, *blocks, *operands)


def gate(y_head, y, z_rows, gain):
    return pl.pallas_call(
        gate_kernel,
        out_shape=jax.ShapeDtypeStruct((ROWS, GC), BF16),
        in_specs=[VMEM, HBM, VMEM, VMEM],
        out_specs=ANY,
        scratch_shapes=[
            pltpu.VMEM((ROWS, GC), F32),
            pltpu.VMEM((ROWS, GC), BF16),
            pltpu.SemaphoreType.DMA((ROWS // GATE_ROWS,)),
            pltpu.SemaphoreType.DMA((ROWS // GATE_ROWS,)),
        ],
        compiler_params=params(12),
        cost_estimate=pl.CostEstimate(
            flops=20_000_000, bytes_accessed=8 * MIB, transcendentals=1_000_000
        ),
        name="gate",
    )(y_head, in_hbm(y), z_rows, gain)


def shifted(value, steps):
    count = lax.axis_size("dp")
    pairs = [(source, (source + steps) % count) for source in range(count)]
    return lax.ppermute(value, "dp", pairs)


def rotated(value, steps):
    count = lax.axis_size("tensor")
    pairs = [(source, (source + steps) % count) for source in range(count)]
    return lax.ppermute(value, "tensor", pairs)


def after(value, *earlier):
    if not earlier:
        return value
    return lax.optimization_barrier((value, *earlier))[0]


def plan(lengths, prefill_owner, row_start, me, left, right):
    ids = jnp.arange(prefill_owner.shape[0], dtype=jnp.int32)
    mine = prefill_owner == me
    home = ids // SLOTS
    code = jnp.where(home == me, ids % SLOTS, jnp.where(home == left, SLOTS, SLOTS + 1))
    before = mine[None, :] & (row_start[None, :] < row_start[:, None])
    rank = jnp.sum(before.astype(jnp.int32), axis=1)
    chosen = mine[None, :] & (rank[None, :] == jnp.arange(SLOTS, dtype=jnp.int32)[:, None])

    def pick(values):
        return jnp.sum(jnp.where(chosen, values[None, :], 0), axis=1)

    starts = pick(row_start)
    codes = pick(code)
    seg = jnp.concatenate([starts, starts + pick(lengths), codes, jnp.zeros((4,), jnp.int32)])
    slot_right = jnp.sum(jnp.where((home == me) & (prefill_owner == right), ids % SLOTS, 0))
    slot_left = jnp.sum(jnp.where((home == me) & (prefill_owner == left), ids % SLOTS, 0))
    return seg, codes, slot_right, slot_left


def shards(
    x_in,
    z_in,
    bc_in,
    dt_in,
    conv_x_param,
    conv_bc_param,
    decay_rate,
    dt_bias,
    skip_gain,
    norm_gain,
    ssm_state,
    conv_x_state,
    conv_bc_state,
    lengths,
    prefill_owner,
    row_start,
):
    dp_count = lax.axis_size("dp")
    me = lax.axis_index("dp")
    left = (me + dp_count - 1) % dp_count
    right = (me + 1) % dp_count
    here = lax.axis_index("tensor")
    here_ref = here.astype(jnp.int32)[None]
    packed = {}
    turn = here_ref
    for offsets in (FIRST[:1], FIRST[1:], SECOND + THIRD + (0,)):
        packed |= pack(offsets, turn, x_in, bc_in, dt_in)
        turn = after(here_ref, packed[offsets[0]])
    blocks = {0: packed[0]}
    for d in FIRST:
        blocks[d] = rotated(packed[d], d)

    seg, codes, slot_right, slot_left = plan(lengths, prefill_owner, row_start, me, left, right)

    own = ssm_state.reshape(SLOTS, GC, STATE)
    conv = jnp.concatenate([conv_x_state, conv_bc_state], axis=2)
    width = conv.shape[2]
    lines = 3 * width // STATE

    def small_mover(slot):
        small = lax.dynamic_index_in_dim(conv, slot, 0, keepdims=False).reshape(lines, STATE)
        return jnp.concatenate([small, jnp.zeros((2, STATE), F32)], axis=0)

    move_right, move_left = movers(
        after(jnp.stack([slot_right, slot_left]).astype(jnp.int32), packed[0]),
        own,
        jnp.stack([small_mover(slot_right), small_mover(slot_left)]),
    )
    from_left = shifted(move_right, 1)
    from_right = shifted(move_left, -1)
    for d in SECOND:
        blocks[d] = rotated(packed[d], d)

    def small_of(packed):
        return packed[GC : GC + lines].reshape(1, 3, width)

    candidates = jnp.concatenate([conv, small_of(from_left), small_of(from_right)], axis=0)
    match = codes[:, None] == jnp.arange(SLOTS + 2, dtype=jnp.int32)[None, :]
    conv_init = jnp.sum(jnp.where(match[:, :, None, None], candidates[None], 0.0), axis=1)
    conv_init = jnp.concatenate([conv_init.reshape(3 * SLOTS, width), jnp.zeros((4, width), F32)])

    z_sent = z_in.reshape(SRC_ROWS, TENSOR, GC).transpose(1, 0, 2)
    init = initial(seg, own, from_left, from_right)
    conv_init, init, z_sent, seg, gain, skip, rate, bias = lax.optimization_barrier(
        (
            conv_init,
            init,
            z_sent,
            seg,
            norm_gain[None, :],
            jnp.repeat(skip_gain, HEADDIM)[None, :],
            decay_rate[:, None],
            dt_bias[:, None],
        )
    )
    for d in THIRD:
        blocks[d] = rotated(after(packed[d], conv_init, z_sent, *[blocks[e] for e in FIRST[1:]]), d)
    z_sent = after(z_sent, *[blocks[e] for e in FIRST])
    z_rows = lax.all_to_all(z_sent, "tensor", split_axis=0, concat_axis=0, tiled=True)
    z_rows = z_rows.reshape(ROWS, GC)

    in_order = [blocks[d] for d in range(TENSOR)]
    y_head, y, own_new, back_left, back_right, last_x, last_bc = scan(
        seg,
        here_ref,
        in_order,
        conv_init[:, :GC],
        conv_init[:, GC:],
        conv_x_param,
        skip,
        conv_bc_param,
        rate,
        bias,
        in_hbm(init),
    )
    returned_right = shifted(back_left, -1)
    returned_left = shifted(back_right, 1)
    last = jnp.concatenate([last_x, last_bc], axis=1)[: 3 * SLOTS].reshape(SLOTS, 3, width)

    new_ssm = own_new
    for packed, slot in ((returned_right, slot_right), (returned_left, slot_left)):
        new_ssm = lax.dynamic_update_index_in_dim(new_ssm, packed[:GC].astype(F32), slot, 0)
    slots = jnp.arange(SLOTS, dtype=jnp.int32)
    stay = slots[:, None] == codes[None, :]
    new_conv = jnp.sum(jnp.where(stay[:, :, None, None], last[None], 0.0), axis=1)
    for packed, slot in ((returned_right, slot_right), (returned_left, slot_left)):
        new_conv = jnp.where(
            (slots == slot)[:, None, None], small_of(packed).astype(F32), new_conv
        )
    new_cx, new_cbc = new_conv[:, :, :GC], new_conv[:, :, GC:]

    y, new_ssm, new_cx, new_cbc = lax.optimization_barrier((y, new_ssm, new_cx, new_cbc))
    y_out = gate(y_head, y, z_rows, gain)
    return y_out, new_ssm.reshape(ssm_state.shape), new_cx, new_cbc


def solution(mesh):
    in_specs = (
        P(("dp", "tensor"), None),
        P(("dp", "tensor"), None),
        P(("dp", "tensor"), None),
        P(("dp", "tensor"), None),
        P(None, "tensor"),
        P(None, "tensor"),
        P("tensor"),
        P("tensor"),
        P("tensor"),
        P("tensor"),
        P("dp", "tensor", None, None),
        P("dp", None, "tensor"),
        P("dp", None, "tensor"),
        P(),
        P(),
        P(),
    )
    out_specs = (
        P("dp", "tensor"),
        P("dp", "tensor", None, None),
        P("dp", None, "tensor"),
        P("dp", None, "tensor"),
    )
    return jax.shard_map(shards, mesh=mesh, in_specs=in_specs, out_specs=out_specs, check_vma=False)
```
